128 devices in a mesh: cluster: 16 (over x, z), helper: 8 (over y, core).
Axes of the slice: x: 4, y: 4, z: 4, core: 2. Of those that a mesh axis runs over, the one named last changes fastest.
Arguments:
- embeddings: bfloat16 [65536, 1024], P(('cluster', 'helper')), may hold values from -40 to 40
- clusters: int32 [65536], P(('cluster', 'helper')), may hold values from 0 to 511, as said below
- order: int32 [65536], P(('cluster', 'helper')), may hold values from 0 to 65535, each once
Outputs:
- best_similarity: float32 [65536], P(('cluster', 'helper'))
The draws below stay inside these ranges and needn't reach their ends.
Inputs may be any that keep to these rules, and one draw needn't show every extreme that they name: Cluster c belongs to owner c // 32. Among the 512 rows of one device, the clusters of one owner hold at most 80 rows; one owner, the same on every device, holds exactly 80 rows on every device, and on half of the devices all 80 of them lie in one cluster. `order`: each position occurs once.
All inputs are finite; a program needn't handle non-finite values.
Results may differ from the reference program's by a relative error of at most 0.0003.
Values may be sent and summed in bfloat16 or wider, within the bound.
No kernel may reach another device: no remote copies, remote signals or barrier semaphores. Data moves between devices by JAX's collectives and lax.ppermute only.
A program may use at most 128 MiB of HBM per device.

```python
import math
import jax
import jax.numpy as jnp
from jax import lax

D = 1024
ROW_DEV = 512
CL_OWN = 32
CAP = 80
CLUSTERS = 512
ROWS = 65536
N_CLUSTER = 16
N_HELPER = 8


def draw_embeddings(key, part):
    key = jax.random.fold_in(key, 5)
    rough_key, scale_key = jax.random.split(key, 2)
    scales = jnp.exp(jax.random.uniform(scale_key, (ROWS, 1), jnp.float32, 0.0, math.log(10.0)))
    values = jnp.clip(jax.random.normal(rough_key, (ROWS, D), jnp.float32), -4.0, 4.0) * scales
    return jnp.clip(values, -40.0, 40.0).astype(jnp.bfloat16)


def draw_clusters(key, part):
    key = jax.random.fold_in(key, 11)
    owners = CLUSTERS // CL_OWN
    devices = ROWS // ROW_DEV
    busy_key, jitter_key, shuffle_key, first_key, second_key, flag_key, pick_key = jax.random.split(key, 7)
    busy_owner = jax.random.randint(busy_key, (), 0, owners)
    others = owners - 1
    base_count = (ROW_DEV - CAP) // others
    extra_rows = ROW_DEV - CAP - base_count * others
    spread = base_count // 2 + 1
    jitter = jax.random.randint(jitter_key, (devices, others), 0, spread)
    other_counts = base_count + jitter - jnp.roll(jitter, 1, axis=1) + (jnp.arange(others) < extra_rows).astype(jnp.int32)
    owner_ids = jnp.arange(owners, dtype=jnp.int32)
    other_index = jnp.clip(owner_ids - (owner_ids > busy_owner).astype(jnp.int32), 0, others - 1)
    counts = jnp.where(owner_ids[None, :] == busy_owner, CAP, other_counts[:, other_index])
    bounds = jnp.cumsum(counts, axis=1)
    positions = jnp.arange(ROW_DEV, dtype=jnp.int32)
    owner_of_pos = jnp.sum((bounds[:, None, :] <= positions[None, :, None]).astype(jnp.int32), axis=2)
    shuffle = jax.vmap(lambda k: jax.random.permutation(k, ROW_DEV))(jax.random.split(shuffle_key, devices))
    owner_rows = jnp.take_along_axis(owner_of_pos, shuffle, axis=1)
    within = jnp.minimum(jax.random.randint(first_key, (devices, ROW_DEV), 0, CL_OWN), jax.random.randint(second_key, (devices, ROW_DEV), 0, CL_OWN))
    device_rank = jax.random.permutation(flag_key, devices)
    gathered_dev = (device_rank < devices // 2)[:, None]
    single_cluster = jax.random.randint(pick_key, (), 0, CL_OWN)
    within = jnp.where(gathered_dev & (owner_rows == busy_owner), single_cluster, within)
    return (owner_rows * CL_OWN + within).reshape(ROWS).astype(jnp.int32)


def setup_inputs(seed: int = 0) -> dict:
    streams_of = jax.random.split(jax.random.key(seed), 4)
    return {
        "embeddings": draw_embeddings(jax.random.fold_in(streams_of[3], 71), 0),
        "clusters": draw_clusters(jax.random.fold_in(streams_of[3], 71), 0),
        "order": jax.random.permutation(streams_of[2], ROWS).astype(jnp.int32),
    }


def inverse_norms(row_values):
    wide_rows = row_values.astype(jnp.float32)
    return lax.rsqrt(lax.optimization_barrier(jnp.sum(wide_rows * wide_rows, axis=1)) + 1e-06)

def reference(embeddings, clusters, order):
    row_count = embeddings.shape[0]
    window = N_CLUSTER * N_HELPER * CAP
    block_rows = min(512, row_count)
    sort_key = (clusters * row_count + order).astype(jnp.int32)
    sorted_idx = jnp.argsort(sort_key).astype(jnp.int32)
    sorted_emb = embeddings[sorted_idx].astype(jnp.float32)
    sorted_inv = inverse_norms(embeddings)[sorted_idx]
    sorted_cl = clusters[sorted_idx]
    sorted_ord = order[sorted_idx]
    padded_emb = jnp.concatenate([jnp.zeros((window, D), jnp.float32), sorted_emb], axis=0)
    padded_inv = jnp.concatenate([jnp.zeros((window,), jnp.float32), sorted_inv])
    padded_cl = jnp.concatenate([jnp.full((window,), -1, jnp.int32), sorted_cl.astype(jnp.int32)])
    padded_ord = jnp.concatenate([jnp.zeros((window,), jnp.int32), sorted_ord.astype(jnp.int32)])

    def one_block(index):
        begin = (index * block_rows).astype(jnp.int32)
        query_emb = lax.dynamic_slice_in_dim(sorted_emb, begin, block_rows, 0)
        query_inv = lax.dynamic_slice_in_dim(sorted_inv, begin, block_rows, 0)
        query_cl = lax.dynamic_slice_in_dim(sorted_cl, begin, block_rows, 0)
        query_ord = lax.dynamic_slice_in_dim(sorted_ord, begin, block_rows, 0)
        key_emb = lax.dynamic_slice_in_dim(padded_emb, begin, window + block_rows, 0)
        key_inv = lax.dynamic_slice_in_dim(padded_inv, begin, window + block_rows, 0)
        key_cl = lax.dynamic_slice_in_dim(padded_cl, begin, window + block_rows, 0)
        key_ord = lax.dynamic_slice_in_dim(padded_ord, begin, window + block_rows, 0)
        gram = jnp.dot(query_emb, key_emb.T, precision=lax.Precision.HIGHEST, preferred_element_type=jnp.float32)
        cosine = gram * query_inv[:, None] * key_inv[None, :]
        live = (key_cl[None, :] == query_cl[:, None]) & (key_ord[None, :] < query_ord[:, None])
        return lax.optimization_barrier(jnp.max(jnp.where(live, cosine, -1.0), axis=1))
    block_count = row_count // block_rows
    sorted_best = lax.map(one_block, jnp.arange(block_count, dtype=jnp.int32)).reshape(row_count)
    return jnp.zeros((row_count,), jnp.float32).at[sorted_idx].set(sorted_best.astype(jnp.float32))
```

```python
import jax
import jax.numpy as jnp
from jax import lax
from jax.experimental import pallas as pl
from jax.experimental.pallas import tpu as pltpu
from jax.sharding import Mesh, PartitionSpec as P

CL_OWN = 32
ROW_DEV = 512
FEAT = 1024
OWNERS = 16
CAP = 80
CHIPS = 64
BINS = 4
PLACES = 12
FIX = 16
META = 128
WIDE = FEAT + FEAT // 2 + META
NARROW = FEAT + META
SLOTS = CHIPS * 8
EXTRA = CHIPS * 4
TAIL = 64
OWN = SLOTS + EXTRA + TAIL
LOW = -1e30
BAD = 4.0
FIELDS = 16

CHIP_AXES = ("x", "z", "y")
ALL_AXES = ("x", "z", "y", "core")
CLUSTER_AXES = ("x", "z")
HELPER_AXES = ("y", "core")

f32 = jnp.float32
bf16 = jnp.bfloat16
i32 = jnp.int32


def iota(shape, axis):
    return lax.broadcasted_iota(i32, shape, axis)


def hot(condition):
    return jnp.where(condition, 1.0, 0.0).astype(bf16)


def mm(a, b):
    return lax.dot_general(a, b, (((1,), (0,)), ((), ())), preferred_element_type=f32)


def mm_t(a, b):
    return lax.dot_general(a, b, (((1,), (1,)), ((), ())), preferred_element_type=f32)


def pieces(value):
    high = value.astype(bf16)
    rest = value - high.astype(f32)
    middle = rest.astype(bf16)
    low = (rest - middle.astype(f32)).astype(bf16)
    return high, middle, low


def bin_of(local_cluster):
    folded = local_cluster & 7
    return jnp.minimum(folded, 7 - folded)


def pack_kernel(chip_ref, emb_ref, cl_ref, ord_ref, out_ref, box_ref, rank_ref, flag_ref):
    emb = emb_ref[...]
    cl = cl_ref[...]
    order = ord_ref[...]
    rows = emb.shape[0]
    wide = emb.astype(f32)
    square = wide * wide
    square_high = square.astype(bf16)
    square_low = (square - square_high.astype(f32)).astype(bf16)
    ones = jnp.ones((8, emb.shape[1]), bf16)
    total = (mm_t(ones, square_high) + mm_t(ones, square_low))[0:1, :] + 1e-06
    inv = lax.rsqrt(total)
    inv = inv * (1.5 - 0.5 * total * inv * inv)
    owner = cl >> 5
    local_cluster = cl & (CL_OWN - 1)
    bins = bin_of(local_cluster)
    earlier = hot(iota((rows, rows), 0) < iota((rows, rows), 1))
    is_owner = iota((OWNERS, rows), 0) == owner
    owner_hot = jnp.where(is_owner, 1.0, 0.0)
    owner_count = jnp.sum(owner_hot, axis=1, keepdims=True)
    full = jnp.where(owner_count == CAP, 1.0, 0.0)
    busy = jnp.sum(owner_hot * full, axis=0, keepdims=True) > 0.5
    is_group = iota((OWNERS * BINS, rows), 0) == owner * BINS + bins
    group_hot = jnp.where(is_group, 1.0, 0.0)
    group_count = jnp.sum(group_hot, axis=1, keepdims=True)
    ranks = mm(jnp.concatenate([group_hot, owner_hot], axis=0).astype(bf16), earlier)
    place = jnp.sum(group_hot * ranks[: OWNERS * BINS], axis=0, keepdims=True).astype(i32)
    owner_place = jnp.sum(owner_hot * ranks[OWNERS * BINS :], axis=0, keepdims=True).astype(i32)
    over = place >= PLACES
    over_ranks = mm((owner_hot * jnp.where(over, 1.0, 0.0)).astype(bf16), earlier)
    spill = jnp.sum(owner_hot * over_ranks, axis=0, keepdims=True).astype(i32)
    taken = jnp.minimum(group_count, float(PLACES))
    new_bin = bins
    new_place = place
    passed = jnp.zeros_like(place)
    for b in range(BINS):
        here = iota((OWNERS * BINS, rows), 0) == owner * BINS + b
        used = jnp.sum(jnp.where(here, taken, 0.0), axis=0, keepdims=True).astype(i32)
        fits = over & (spill >= passed) & (spill < passed + (PLACES - used))
        new_bin = jnp.where(fits, b, new_bin)
        new_place = jnp.where(fits, used + spill - passed, new_place)
        passed = passed + (PLACES - used)
    base = (owner * BINS + new_bin) * 8
    main_target = jnp.where(busy | (new_place >= 8), -1, base + new_place)
    extra_target = jnp.where(busy | (new_place < 8), -8, base + new_place - 8)
    rank = jnp.where(busy, owner_place, -1)
    rank_ref[...] = rank
    most = jnp.max(jnp.where(full > 0.5, 0.0, owner_count), axis=0, keepdims=True)
    flag = (jnp.sum(full, axis=0, keepdims=True) != 1.0) | (most > BINS * PLACES)
    flag_ref[...] = jnp.broadcast_to(jnp.where(flag, 1.0, 0.0), flag_ref.shape)
    high, middle, low = pieces(inv)
    at = iota((1, rows), 1)
    fields = [
        local_cluster.astype(f32),
        (order >> 8).astype(f32),
        (order & 255).astype(f32),
        high.astype(f32),
        middle.astype(f32),
        low.astype(f32),
        jnp.ones((1, rows), f32),
        jnp.full((1, rows), chip_ref[0], i32).astype(f32),
        (at >> 8).astype(f32),
        (at & 255).astype(f32),
    ]
    field_at = iota((META, rows), 0)
    meta = jnp.zeros((META, rows), f32)
    meta_extra = jnp.zeros((META, rows), f32)
    for k, value in enumerate(fields):
        meta = jnp.where(field_at == k, value, meta)
        meta_extra = jnp.where(field_at == FIELDS + k, value, meta_extra)
    meta = meta.astype(bf16)
    meta_extra = meta_extra.astype(bf16)
    pick = hot(iota((CAP, rows), 0) == rank)
    box_ref[:, :FEAT] = mm(pick, emb).astype(bf16)
    box_ref[:, FEAT:] = mm_t(pick, meta).astype(bf16)
    slot = iota((SLOTS, rows), 0)
    pick = hot(slot == main_target)
    pick_first = hot(slot == extra_target)
    pick_second = hot(slot - 4 == extra_target)
    half = FEAT // 2
    shape = (CHIPS, 8, -1)
    out_ref[:, :, :FEAT] = mm(pick, emb).astype(bf16).reshape(CHIPS, 8, FEAT)
    halves = mm(pick_first, emb[:, :half]) + mm(pick_second, emb[:, half:])
    out_ref[:, :, FEAT : FEAT + half] = halves.astype(bf16).reshape(CHIPS, 8, half)
    beside = mm_t(pick, meta) + mm_t(pick_first, meta_extra)
    out_ref[:, :, FEAT + half :] = beside.astype(bf16).reshape(CHIPS, 8, META)


def fix_kernel(y_ref, flag_in_ref, in_ref, fix_ref, flag_ref):
    half = FEAT // 2
    meta = in_ref[:, :, FEAT + half :].reshape(SLOTS, META)
    turn = hot(iota((2 * FIELDS, META), 0) == iota((2 * FIELDS, META), 1))
    rows = mm_t(turn, meta)
    earlier = hot(iota((SLOTS, SLOTS), 0) < iota((SLOTS, SLOTS), 1))
    y = y_ref[0]

    def away(first):
        steps = (bin_of(rows[first : first + 1].astype(i32)) - y) & 3
        return jnp.where(rows[first + 6 : first + 7] > 0.5, steps, 0)

    main = away(0)
    extra = away(FIELDS)
    step_at = iota((8, SLOTS), 0)
    main_hot = jnp.where(step_at == main, 1.0, 0.0)
    extra_hot = jnp.where(step_at == extra, 1.0, 0.0)
    ranks = mm(jnp.concatenate([main_hot, extra_hot], axis=0).astype(bf16), earlier)
    main_count = jnp.sum(main_hot, axis=1, keepdims=True)
    count = main_count + jnp.sum(extra_hot, axis=1, keepdims=True)
    main_place = jnp.sum(main_hot * ranks[:8], axis=0, keepdims=True).astype(i32)
    extra_place = jnp.sum(extra_hot * (ranks[8:] + main_count), axis=0, keepdims=True).astype(i32)
    main_target = jnp.where((main > 0) & (main_place < FIX), (main - 1) * FIX + main_place, -1)
    extra_target = jnp.where((extra > 0) & (extra_place < FIX), (extra - 1) * FIX + extra_place, -1)
    slot = iota((3 * FIX, SLOTS), 0)
    pick = hot(slot == main_target)
    pick_first = hot(slot == extra_target)
    later = hot(iota((SLOTS, SLOTS), 1) == iota((SLOTS, SLOTS), 0) + 4)
    pick_second = mm(pick_first, later).astype(bf16)
    whole = in_ref[:, :, :FEAT].reshape(SLOTS, FEAT)
    halves = in_ref[:, :, FEAT : FEAT + half].reshape(SLOTS, half)
    taken = mm(pick, whole)
    fix_ref[:, :half] = (taken[:, :half] + mm(pick_first, halves)).astype(bf16)
    fix_ref[:, half:FEAT] = (taken[:, half:] + mm(pick_second, halves)).astype(bf16)
    back = hot((iota((META, META), 0) == iota((META, META), 1) + FIELDS) & (iota((META, META), 1) < FIELDS))
    keep = hot((iota((META, META), 0) == iota((META, META), 1)) & (iota((META, META), 1) < FIELDS))
    beside = mm(mm(pick, meta).astype(bf16), keep) + mm(mm(pick_first, meta).astype(bf16), back)
    fix_ref[:, FEAT:] = beside.astype(bf16)
    step_row = iota((8, 1), 0)
    too_many = jnp.max(jnp.where((step_row > 0) & (count > FIX), 1.0, 0.0), axis=0, keepdims=True)
    flag = jnp.maximum(flag_in_ref[0:1, 0:1], too_many)
    spot = (iota((FIX, NARROW), 0) == 0) & (iota((FIX, NARROW), 1) == FEAT + 10)
    flag_ref[...] = jnp.where(spot, flag, 0.0).astype(bf16)


def key_columns(meta):
    wide = meta.astype(f32)
    position = wide[:, 1:2] * 256.0 + wide[:, 2:3]
    position = jnp.where(wide[:, 6:7] > 0.5, position, 1e9)
    return wide[:, 0:1], position, wide[:, 3:4] + wide[:, 4:5] + wide[:, 5:6]


def query_rows(meta):
    turn = hot(iota((FIELDS, META), 0) == iota((FIELDS, META), 1))
    return mm_t(turn, meta)


def best_over_keys(keys, metas, queries, query_fields, blocks):
    query_cl = query_fields[0:1]
    query_ord = query_fields[1:2] * 256.0 + query_fields[2:3]
    query_inv = query_fields[3:4] + query_fields[4:5] + query_fields[5:6]
    best = jnp.full(query_cl.shape, LOW, f32)
    size = keys.shape[0] // blocks
    for k in range(blocks):
        at = slice(k * size, (k + 1) * size)
        cl, position, inv = key_columns(metas[at, :])
        scaled = mm_t(keys[at, :], queries) * inv
        live = (cl == query_cl) & (position < query_ord)
        best = jnp.maximum(best, jnp.max(jnp.where(live, scaled, LOW), axis=0, keepdims=True))
    return jnp.maximum(best * query_inv, -1.0)


def owned_kernel(own_ref, other_ref, own_tail_ref, other_tail_ref, out_ref, keys, metas):
    half = FEAT // 2
    source = iota((EXTRA, SLOTS), 1)
    wanted = iota((EXTRA, SLOTS), 0)
    first = hot(source == (wanted >> 2) * 8 + (wanted & 3))
    second = hot(source == (wanted >> 2) * 8 + (wanted & 3) + 4)
    back = hot((iota((META, META), 0) == iota((META, META), 1) + FIELDS) & (iota((META, META), 1) < FIELDS))
    for ref, tail, base in ((own_ref, own_tail_ref, 0), (other_ref, other_tail_ref, OWN)):
        at = slice(base, base + SLOTS)
        keys[at, :] = ref[:, :, :FEAT].reshape(SLOTS, FEAT)
        meta = ref[:, :, FEAT + half :].reshape(SLOTS, META)
        metas[at, :] = meta
        at = slice(base + SLOTS, base + SLOTS + EXTRA)
        halves = ref[:, :, FEAT : FEAT + half].reshape(SLOTS, half)
        keys[at, :half] = mm(first, halves).astype(bf16)
        keys[at, half:] = mm(second, halves).astype(bf16)
        metas[at, :] = mm(mm(first, meta).astype(bf16), back).astype(bf16)
        at = slice(base + SLOTS + EXTRA, base + OWN)
        keys[at, :] = tail[:, :FEAT]
        metas[at, :] = tail[:, FEAT:]
    fields = query_rows(metas[:OWN, :])
    best = best_over_keys(keys, metas, keys[:OWN, :], fields, 8)
    from_chip = jnp.where((iota((CHIPS, OWN), 0).astype(f32) == fields[7:8]) & (fields[6:7] > 0.5), 1.0, 0.0)
    high, middle, low = pieces(best)
    left = jnp.concatenate(
        [from_chip, from_chip * high.astype(f32), from_chip * middle.astype(f32), from_chip * low.astype(f32)], axis=0
    ).astype(bf16)
    wide = metas[:OWN, :].astype(f32)
    place = wide[:, 8:9] * 256.0 + wide[:, 9:10]
    right = hot(iota((OWN, ROW_DEV), 1).astype(f32) == place)
    spread = mm(left, right)
    value = spread[CHIPS : 2 * CHIPS] + spread[2 * CHIPS : 3 * CHIPS] + spread[3 * CHIPS :]
    out = jnp.where(spread[:CHIPS] > 0.5, value, -1.0)
    flag = jnp.maximum(own_tail_ref[3 * FIX : 3 * FIX + 1, FEAT + 10 : FEAT + 11].astype(f32), other_tail_ref[3 * FIX : 3 * FIX + 1, FEAT + 10 : FEAT + 11].astype(f32))
    out_ref[...] = jnp.where(flag > 0.5, BAD, out)


def busy_kernel(y_ref, core_ref, keys_ref, queries_ref, out_ref):
    fields = query_rows(queries_ref[:, FEAT:])
    best = best_over_keys(keys_ref.at[:, :FEAT], keys_ref.at[:, FEAT:], queries_ref[:, :FEAT], fields, 8)
    out_ref[...] = jnp.full(out_ref.shape, -1.0, f32)
    for k in range(8):
        core = core_ref[0] if k < 4 else 1 - core_ref[0]
        helper = ((y_ref[0] + k) & 3) * 2 + core
        out_ref[pl.ds(helper, 1), :CAP] = best[:, k * CAP : (k + 1) * CAP]


def last_kernel(spread_ref, busy_ref, rank_ref, out_ref, flag_ref):
    spread = spread_ref[...]
    flag_ref[...] = jnp.broadcast_to(jnp.max(jnp.max(spread, axis=0, keepdims=True), axis=1, keepdims=True), flag_ref.shape)
    owned = jnp.max(spread, axis=0, keepdims=True)
    busy = jnp.max(busy_ref[...], axis=0, keepdims=True)
    high, middle, low = pieces(busy)
    parts = jnp.concatenate([high.astype(f32), middle.astype(f32), low.astype(f32), jnp.zeros((5, META), f32)], axis=0)
    rank = rank_ref[...]
    pick = hot(iota((META, ROW_DEV), 0) == rank)
    taken = mm(parts.astype(bf16), pick)
    value = taken[0:1] + taken[1:2] + taken[2:3]
    out_ref[...] = jnp.where(rank >= 0, value, owned)


def call(kernel, shapes, args, specs, scratch=(), flops=0, bytes_accessed=0):
    return pl.pallas_call(
        kernel,
        out_shape=shapes,
        in_specs=[pl.BlockSpec(memory_space=s) for s in specs],
        out_specs=jax.tree.map(lambda _: pl.BlockSpec(memory_space=pltpu.VMEM), shapes),
        scratch_shapes=scratch,
        compiler_params=pltpu.CompilerParams(vmem_limit_bytes=48 * 1024 * 1024),
        cost_estimate=pl.CostEstimate(flops=flops, bytes_accessed=bytes_accessed, transcendentals=0),
    )(*args)


VMEM, SMEM = pltpu.VMEM, pltpu.SMEM


def fast(embeddings, clusters, order):
    shape = jax.ShapeDtypeStruct
    y, core = lax.axis_index("y"), lax.axis_index("core")
    chip = (lax.axis_index("x") * 4 + lax.axis_index("z")) * 4 + y
    outbox, box, rank, flag = call(
        pack_kernel,
        (
            shape((CHIPS, 8, WIDE), bf16),
            shape((CAP, NARROW), bf16),
            shape((1, ROW_DEV), i32),
            shape((8, 128), f32),
        ),
        (chip[None].astype(i32), embeddings, clusters[None, :], order[None, :]),
        (SMEM, VMEM, VMEM, VMEM),
        flops=2 * 700_000_000,
        bytes_accessed=3_000_000,
    )
    busy_keys = lax.all_gather(box, CLUSTER_AXES, axis=0, tiled=True)
    inbox = lax.all_to_all(outbox, CHIP_AXES, split_axis=0, concat_axis=0, tiled=True)
    along = [box] + [lax.ppermute(box, "y", [(i, (i - d) % 4) for i in range(4)]) for d in (1, 2, 3)]
    swap = [(0, 1), (1, 0)]
    same = jnp.concatenate(along, axis=0)
    busy_queries = jnp.concatenate([same, lax.ppermute(same, "core", swap)], axis=0)
    other = lax.ppermute(inbox, "core", swap)
    fix, flag_block = call(
        fix_kernel,
        (shape((3 * FIX, NARROW), bf16), shape((FIX, NARROW), bf16)),
        (y[None].astype(i32), flag, inbox),
        (SMEM, VMEM, VMEM),
        flops=2 * 100_000_000,
        bytes_accessed=2_000_000,
    )
    got = [
        lax.ppermute(fix[(d - 1) * FIX : d * FIX], "y", [(i, (i + d) % 4) for i in range(4)]) for d in (1, 2, 3)
    ]
    tail = jnp.concatenate(got + [flag_block], axis=0)
    other_tail = lax.ppermute(tail, "core", swap)
    spread = call(
        owned_kernel,
        shape((CHIPS, ROW_DEV), f32),
        (inbox, other, tail, other_tail),
        (VMEM, VMEM, VMEM, VMEM),
        scratch=(pltpu.VMEM((2 * OWN, FEAT), bf16), pltpu.VMEM((2 * OWN, META), bf16)),
        flops=2 * 1_600_000_000,
        bytes_accessed=4_000_000,
    )
    returned = lax.all_to_all(spread, CHIP_AXES, split_axis=0, concat_axis=0, tiled=True)
    partial = call(
        busy_kernel,
        shape((8, META), f32),
        (y[None].astype(i32), core[None].astype(i32), busy_keys, busy_queries),
        (SMEM, SMEM, VMEM, VMEM),
        flops=2 * 900_000_000,
        bytes_accessed=4_500_000,
    )
    busy = lax.all_to_all(partial, HELPER_AXES, split_axis=0, concat_axis=0, tiled=True)
    out, worst = call(
        last_kernel,
        (shape((1, ROW_DEV), f32), shape((8, 128), f32)),
        (returned, busy, rank),
        (VMEM, VMEM, VMEM),
    )
    return out[0], worst[0, 0] > 2.0


def inverse_norms(row_values):
    wide_rows = row_values.astype(f32)
    return lax.rsqrt(jnp.sum(wide_rows * wide_rows, axis=1) + 1e-06)


def general(embeddings, clusters, order):
    owners, helpers = 16, 8
    slot_count = ROW_DEV * 5 // (2 * owners * helpers)
    total_rows = owners * helpers * slot_count
    owner_of = clusters // CL_OWN
    one_hot = (owner_of[:, None] == jnp.arange(owners, dtype=i32)[None, :]).astype(i32)
    before = jnp.cumsum(one_hot, axis=0) - one_hot
    place_in = jnp.sum(before * one_hot, axis=1)
    target = (owner_of * helpers + place_in % helpers) * slot_count + place_in // helpers
    outbox = jnp.zeros((total_rows, FEAT), embeddings.dtype).at[target].set(embeddings)
    outbox_cl = jnp.full((total_rows,), -1, i32).at[target].set(clusters)
    outbox_ord = jnp.zeros((total_rows,), i32).at[target].set(order)

    def exchange(value):
        return lax.all_to_all(value, ALL_AXES, split_axis=0, concat_axis=0, tiled=True)

    def gather(value):
        return lax.all_gather(value, HELPER_AXES, axis=0, tiled=True)

    inbox, inbox_cl, inbox_ord = exchange(outbox), exchange(outbox_cl), exchange(outbox_ord)
    query_inv = inverse_norms(inbox)

    def advance(best, block):
        key_emb, key_cl, key_ord = block
        gram = lax.dot_general(inbox, key_emb, (((1,), (1,)), ((), ())), preferred_element_type=f32)
        cosine = gram * query_inv[:, None] * inverse_norms(key_emb)[None, :]
        live = (key_cl[None, :] == inbox_cl[:, None]) & (key_ord[None, :] < inbox_ord[:, None])
        return jnp.maximum(best, jnp.max(jnp.where(live, cosine, -1.0), axis=1)), None

    blocks = (
        gather(inbox).reshape(helpers, total_rows, FEAT),
        gather(inbox_cl).reshape(helpers, total_rows),
        gather(inbox_ord).reshape(helpers, total_rows),
    )
    best, _ = lax.scan(advance, jnp.full((total_rows,), -1.0, f32), blocks)
    return exchange(best)[target]


def local(embeddings, clusters, order):
    out, overflow = fast(embeddings, clusters, order)
    return lax.cond(overflow, lambda: general(embeddings, clusters, order), lambda: out)


def solution(mesh):
    grid = Mesh(mesh.devices.reshape(4, 4, 4, 2), ALL_AXES)
    placed = (P(ALL_AXES, None), P(ALL_AXES), P(ALL_AXES))
    return jax.shard_map(local, mesh=grid, in_specs=placed, out_specs=P(ALL_AXES), check_vma=False)
```

```python
import jax
import jax.numpy as jnp
from jax import lax
from jax.experimental import pallas as pl
from jax.experimental.pallas import tpu as pltpu
from jax.sharding import Mesh, PartitionSpec as P

CL_OWN = 32
ROW_DEV = 512
FEAT = 1024
OWNERS = 16
CAP = 80
CHIPS = 64
BINS = 4
PLACES = 12
FIX = 32
META = 128
WIDE = FEAT + FEAT // 2 + META
NARROW = FEAT + META
SLOTS = CHIPS * 8
EXTRA = CHIPS * 4
FLAG_ROWS = 16
TAIL = 3 * FIX + FLAG_ROWS
OWN = SLOTS + EXTRA + TAIL
LOW = -1e30
BAD = 4.0
FIELDS = 16

CHIP_AXES = ("x", "z", "y")
ALL_AXES = ("x", "z", "y", "core")
CLUSTER_AXES = ("x", "z")
HELPER_AXES = ("y", "core")

f32 = jnp.float32
bf16 = jnp.bfloat16
i32 = jnp.int32


def iota(shape, axis):
    return lax.broadcasted_iota(i32, shape, axis)


def hot(condition):
    return jnp.where(condition, 1.0, 0.0).astype(bf16)


def mm(a, b):
    return lax.dot_general(a, b, (((1,), (0,)), ((), ())), preferred_element_type=f32)


def mm_t(a, b):
    return lax.dot_general(a, b, (((1,), (1,)), ((), ())), preferred_element_type=f32)


def pieces(value):
    high = value.astype(bf16)
    rest = value - high.astype(f32)
    middle = rest.astype(bf16)
    low = (rest - middle.astype(f32)).astype(bf16)
    return high, middle, low


def bin_of(local_cluster):
    folded = local_cluster & 7
    return jnp.minimum(folded, 7 - folded)


def pack_kernel(chip_ref, emb_hbm, cl_hbm, ord_hbm, out_ref, box_ref, rank_ref, flag_ref, emb_ref, cl_ref, ord_ref, sems):
    pairs = ((cl_hbm, cl_ref), (ord_hbm, ord_ref), (emb_hbm, emb_ref))
    copies = [pltpu.make_async_copy(src, dst, sems.at[k]) for k, (src, dst) in enumerate(pairs)]
    for copy in copies:
        copy.start()
    for copy in copies:
        copy.wait()
    emb = emb_ref[...]
    cl = cl_ref[...]
    order = ord_ref[...]
    rows = emb.shape[0]
    wide = emb.astype(f32)
    square = wide * wide
    square_high = square.astype(bf16)
    square_low = (square - square_high.astype(f32)).astype(bf16)
    ones = jnp.ones((8, emb.shape[1]), bf16)
    total = (mm_t(ones, square_high) + mm_t(ones, square_low))[0:1, :] + 1e-06
    inv = lax.rsqrt(total)
    inv = inv * (1.5 - 0.5 * total * inv * inv)
    owner = cl >> 5
    local_cluster = cl & (CL_OWN - 1)
    bins = bin_of(local_cluster)
    earlier = hot(iota((rows, rows), 0) < iota((rows, rows), 1))
    is_owner = iota((OWNERS, rows), 0) == owner
    owner_hot = jnp.where(is_owner, 1.0, 0.0)
    owner_count = jnp.sum(owner_hot, axis=1, keepdims=True)
    full = jnp.where(owner_count == CAP, 1.0, 0.0)
    busy = jnp.sum(owner_hot * full, axis=0, keepdims=True) > 0.5
    is_group = iota((OWNERS * BINS, rows), 0) == owner * BINS + bins
    group_hot = jnp.where(is_group, 1.0, 0.0)
    group_count = jnp.sum(group_hot, axis=1, keepdims=True)
    ranks = mm(jnp.concatenate([group_hot, owner_hot], axis=0).astype(bf16), earlier)
    place = jnp.sum(group_hot * ranks[: OWNERS * BINS], axis=0, keepdims=True).astype(i32)
    owner_place = jnp.sum(owner_hot * ranks[OWNERS * BINS :], axis=0, keepdims=True).astype(i32)
    over = place >= PLACES
    over_ranks = mm((owner_hot * jnp.where(over, 1.0, 0.0)).astype(bf16), earlier)
    spill = jnp.sum(owner_hot * over_ranks, axis=0, keepdims=True).astype(i32)
    taken = jnp.minimum(group_count, float(PLACES))
    new_bin = bins
    new_place = place
    passed = jnp.zeros_like(place)
    for step in range(BINS):
        b = (chip_ref[0] + step) & 3
        here = iota((OWNERS * BINS, rows), 0) == owner * BINS + b
        used = jnp.sum(jnp.where(here, taken, 0.0), axis=0, keepdims=True).astype(i32)
        fits = over & (spill >= passed) & (spill < passed + (PLACES - used))
        new_bin = jnp.where(fits, b, new_bin)
        new_place = jnp.where(fits, used + spill - passed, new_place)
        passed = passed + (PLACES - used)
    base = (owner * BINS + new_bin) * 8
    main_target = jnp.where(busy | (new_place >= 8), -1, base + new_place)
    extra_target = jnp.where(busy | (new_place < 8), -8, base + new_place - 8)
    rank = jnp.where(busy, owner_place, -1)
    rank_ref[...] = rank
    most = jnp.max(jnp.where(full > 0.5, 0.0, owner_count), axis=0, keepdims=True)
    flag = (jnp.sum(full, axis=0, keepdims=True) != 1.0) | (most > BINS * PLACES)
    flag_ref[...] = jnp.broadcast_to(jnp.where(flag, 1.0, 0.0), flag_ref.shape)
    high, middle, low = pieces(inv)
    at = iota((1, rows), 1)
    fields = [
        local_cluster.astype(f32),
        (order >> 8).astype(f32),
        (order & 255).astype(f32),
        high.astype(f32),
        middle.astype(f32),
        low.astype(f32),
        jnp.ones((1, rows), f32),
        jnp.full((1, rows), chip_ref[0], i32).astype(f32),
        (at >> 8).astype(f32),
        (at & 255).astype(f32),
    ]
    field_at = iota((META, rows), 0)
    meta = jnp.zeros((META, rows), f32)
    meta_extra = jnp.zeros((META, rows), f32)
    for k, value in enumerate(fields):
        meta = jnp.where(field_at == k, value, meta)
        meta_extra = jnp.where(field_at == FIELDS + k, value, meta_extra)
    meta = meta.astype(bf16)
    meta_extra = meta_extra.astype(bf16)
    pick = hot(iota((CAP, rows), 0) == rank)
    box_ref[:, :FEAT] = mm(pick, emb).astype(bf16)
    box_ref[:, FEAT:] = mm_t(pick, meta).astype(bf16)
    slot = iota((SLOTS, rows), 0)
    pick = hot(slot == main_target)
    pick_first = hot(slot == extra_target)
    pick_second = hot(slot - 4 == extra_target)
    half = FEAT // 2
    out_ref[:, :, :FEAT] = mm(pick, emb).astype(bf16).reshape(CHIPS, 8, FEAT)
    halves = mm(pick_first, emb[:, :half]) + mm(pick_second, emb[:, half:])
    out_ref[:, :, FEAT : FEAT + half] = halves.astype(bf16).reshape(CHIPS, 8, half)
    beside = mm_t(pick, meta) + mm_t(pick_first, meta_extra)
    out_ref[:, :, FEAT + half :] = beside.astype(bf16).reshape(CHIPS, 8, META)


def fix_kernel(y_ref, flag_in_ref, in_ref, fix_ref, flag_ref):
    half = FEAT // 2
    meta = in_ref[:, :, FEAT + half :].reshape(SLOTS, META)
    turn = hot(iota((2 * FIELDS, META), 0) == iota((2 * FIELDS, META), 1))
    rows = mm_t(turn, meta)
    earlier = hot(iota((SLOTS, SLOTS), 0) < iota((SLOTS, SLOTS), 1))
    y = y_ref[0]

    def away(first):
        steps = (bin_of(rows[first : first + 1].astype(i32)) - y) & 3
        return jnp.where(rows[first + 6 : first + 7] > 0.5, steps, 0)

    main = away(0)
    extra = away(FIELDS)
    step_at = iota((8, SLOTS), 0)
    main_hot = jnp.where(step_at == main, 1.0, 0.0)
    extra_hot = jnp.where(step_at == extra, 1.0, 0.0)
    ranks = mm(jnp.concatenate([main_hot, extra_hot], axis=0).astype(bf16), earlier)
    main_count = jnp.sum(main_hot, axis=1, keepdims=True)
    count = main_count + jnp.sum(extra_hot, axis=1, keepdims=True)
    main_place = jnp.sum(main_hot * ranks[:8], axis=0, keepdims=True).astype(i32)
    extra_place = jnp.sum(extra_hot * (ranks[8:] + main_count), axis=0, keepdims=True).astype(i32)
    main_target = jnp.where((main > 0) & (main_place < FIX), (main - 1) * FIX + main_place, -1)
    extra_target = jnp.where((extra > 0) & (extra_place < FIX), (extra - 1) * FIX + extra_place, -1)
    slot = iota((3 * FIX, SLOTS), 0)
    pick = hot(slot == main_target)
    pick_first = hot(slot == extra_target)
    later = hot(iota((SLOTS, SLOTS), 1) == iota((SLOTS, SLOTS), 0) + 4)
    pick_second = mm(pick_first, later).astype(bf16)
    whole = in_ref[:, :, :FEAT].reshape(SLOTS, FEAT)
    halves = in_ref[:, :, FEAT : FEAT + half].reshape(SLOTS, half)
    taken = mm(pick, whole)
    fix_ref[:, :half] = (taken[:, :half] + mm(pick_first, halves)).astype(bf16)
    fix_ref[:, half:FEAT] = (taken[:, half:] + mm(pick_second, halves)).astype(bf16)
    back = hot((iota((META, META), 0) == iota((META, META), 1) + FIELDS) & (iota((META, META), 1) < FIELDS))
    keep = hot((iota((META, META), 0) == iota((META, META), 1)) & (iota((META, META), 1) < FIELDS))
    beside = mm(mm(pick, meta).astype(bf16), keep) + mm(mm(pick_first, meta).astype(bf16), back)
    fix_ref[:, FEAT:] = beside.astype(bf16)
    step_row = iota((8, 1), 0)
    too_many = jnp.max(jnp.where((step_row > 0) & (count > FIX), 1.0, 0.0), axis=0, keepdims=True)
    flag = jnp.maximum(flag_in_ref[0:1, 0:1], too_many)
    spot = (iota(flag_ref.shape, 0) == 0) & (iota(flag_ref.shape, 1) == FEAT + 10)
    flag_ref[...] = jnp.where(spot, flag, 0.0).astype(bf16)


def key_columns(meta):
    wide = meta.astype(f32)
    position = wide[:, 1:2] * 256.0 + wide[:, 2:3]
    position = jnp.where(wide[:, 6:7] > 0.5, position, 1e9)
    return wide[:, 0:1], position, wide[:, 3:4] + wide[:, 4:5] + wide[:, 5:6]


def query_rows(meta):
    turn = hot(iota((FIELDS, META), 0) == iota((FIELDS, META), 1))
    return mm_t(turn, meta)


def best_over_keys(keys, metas, queries, query_fields, blocks):
    query_cl = query_fields[0:1]
    query_ord = query_fields[1:2] * 256.0 + query_fields[2:3]
    query_inv = query_fields[3:4] + query_fields[4:5] + query_fields[5:6]
    best = jnp.full(query_cl.shape, LOW, f32)
    size = keys.shape[0] // blocks
    for k in range(blocks):
        at = slice(k * size, (k + 1) * size)
        cl, position, inv = key_columns(metas[at, :])
        scaled = mm_t(keys[at, :], queries) * inv
        live = (cl == query_cl) & (position < query_ord)
        best = jnp.maximum(best, jnp.max(jnp.where(live, scaled, LOW), axis=0, keepdims=True))
    return jnp.maximum(best * query_inv, -1.0)


def owned_kernel(own_ref, other_ref, own_tail_ref, other_tail_ref, out_ref, keys, metas):
    half = FEAT // 2
    source = iota((EXTRA, SLOTS), 1)
    wanted = iota((EXTRA, SLOTS), 0)
    first = hot(source == (wanted >> 2) * 8 + (wanted & 3))
    second = hot(source == (wanted >> 2) * 8 + (wanted & 3) + 4)
    back = hot((iota((META, META), 0) == iota((META, META), 1) + FIELDS) & (iota((META, META), 1) < FIELDS))
    for ref, tail, base in ((own_ref, own_tail_ref, 0), (other_ref, other_tail_ref, OWN)):
        at = slice(base, base + SLOTS)
        keys[at, :] = ref[:, :, :FEAT].reshape(SLOTS, FEAT)
        meta = ref[:, :, FEAT + half :].reshape(SLOTS, META)
        metas[at, :] = meta
        at = slice(base + SLOTS, base + SLOTS + EXTRA)
        halves = ref[:, :, FEAT : FEAT + half].reshape(SLOTS, half)
        keys[at, :half] = mm(first, halves).astype(bf16)
        keys[at, half:] = mm(second, halves).astype(bf16)
        metas[at, :] = mm(mm(first, meta).astype(bf16), back).astype(bf16)
        at = slice(base + SLOTS + EXTRA, base + OWN)
        keys[at, :] = tail[:, :FEAT]
        metas[at, :] = tail[:, FEAT:]
    fields = query_rows(metas[:OWN, :])
    best = best_over_keys(keys, metas, keys[:OWN, :], fields, 4)
    from_chip = jnp.where((iota((CHIPS, OWN), 0).astype(f32) == fields[7:8]) & (fields[6:7] > 0.5), 1.0, 0.0)
    high, middle, low = pieces(best)
    left = jnp.concatenate(
        [from_chip, from_chip * high.astype(f32), from_chip * middle.astype(f32), from_chip * low.astype(f32)], axis=0
    ).astype(bf16)
    wide = metas[:OWN, :].astype(f32)
    place = wide[:, 8:9] * 256.0 + wide[:, 9:10]
    right = hot(iota((OWN, ROW_DEV), 1).astype(f32) == place)
    spread = mm(left, right)
    value = spread[CHIPS : 2 * CHIPS] + spread[2 * CHIPS : 3 * CHIPS] + spread[3 * CHIPS :]
    out = jnp.where(spread[:CHIPS] > 0.5, value, -1.0)
    at = slice(3 * FIX, 3 * FIX + 1), slice(FEAT + 10, FEAT + 11)
    flag = jnp.maximum(own_tail_ref[at].astype(f32), other_tail_ref[at].astype(f32))
    out = jnp.where(flag > 0.5, BAD, out)
    for k in range(ROW_DEV // META):
        out_ref[:, k, :] = out[:, k * META : (k + 1) * META]


def busy_kernel(keys_ref, queries_ref, out_ref):
    fields = query_rows(queries_ref[:, FEAT:])
    best = best_over_keys(keys_ref.at[:, :FEAT], keys_ref.at[:, FEAT:], queries_ref[:, :FEAT], fields, 4)
    out_ref[...] = jnp.full(out_ref.shape, -1.0, f32)
    for k in range(8):
        out_ref[k : k + 1, :CAP] = best[:, k * CAP : (k + 1) * CAP]


def last_kernel(spread_ref, busy_ref, rank_ref, out_ref, flag_ref):
    best = jnp.max(spread_ref[...], axis=0)
    worst = jnp.max(jnp.max(best, axis=0, keepdims=True), axis=1, keepdims=True)
    flag_ref[...] = jnp.broadcast_to(worst, flag_ref.shape)
    owned = jnp.concatenate([best[k : k + 1] for k in range(ROW_DEV // META)], axis=1)
    busy = jnp.max(busy_ref[...], axis=0, keepdims=True)
    high, middle, low = pieces(busy)
    parts = jnp.concatenate([high.astype(f32), middle.astype(f32), low.astype(f32), jnp.zeros((5, META), f32)], axis=0)
    rank = rank_ref[...]
    pick = hot(iota((META, ROW_DEV), 0) == rank)
    taken = mm(parts.astype(bf16), pick)
    value = taken[0:1] + taken[1:2] + taken[2:3]
    out_ref[...] = jnp.where(rank >= 0, value, owned)


def call(kernel, shapes, args, specs, scratch=(), flops=0, bytes_accessed=0, vmem=28):
    return pl.pallas_call(
        kernel,
        out_shape=shapes,
        in_specs=[pl.BlockSpec(memory_space=s) for s in specs],
        out_specs=jax.tree.map(lambda _: pl.BlockSpec(memory_space=pltpu.VMEM), shapes),
        scratch_shapes=scratch,
        compiler_params=pltpu.CompilerParams(vmem_limit_bytes=vmem * 1024 * 1024),
        cost_estimate=pl.CostEstimate(flops=flops, bytes_accessed=bytes_accessed, transcendentals=0),
    )(*args)


VMEM, SMEM = pltpu.VMEM, pltpu.SMEM


def fast(embeddings, clusters, order):
    shape = jax.ShapeDtypeStruct
    y = lax.axis_index("y")
    chip = (lax.axis_index("x") * 4 + lax.axis_index("z")) * 4 + y
    outbox, box, rank, flag = call(
        pack_kernel,
        (
            shape((CHIPS, 8, WIDE), bf16),
            shape((CAP, NARROW), bf16),
            shape((1, ROW_DEV), i32),
            shape((8, 128), f32),
        ),
        (chip[None].astype(i32), embeddings, clusters[None, :], order[None, :]),
        (SMEM, pl.ANY, pl.ANY, pl.ANY),
        scratch=(
            pltpu.VMEM((ROW_DEV, FEAT), bf16),
            pltpu.VMEM((1, ROW_DEV), i32),
            pltpu.VMEM((1, ROW_DEV), i32),
            pltpu.SemaphoreType.DMA((3,)),
        ),
        flops=2 * 700_000_000,
        bytes_accessed=3_000_000,
    )
    busy_keys = lax.all_gather(box, CLUSTER_AXES, axis=0, tiled=True)
    inbox = lax.all_to_all(outbox, CHIP_AXES, split_axis=0, concat_axis=0, tiled=True)
    swap = [(0, 1), (1, 0)]
    along = [box] + [lax.ppermute(box, "y", [(i, (i - d) % 4) for i in range(4)]) for d in (1, 2, 3)]
    other = lax.ppermute(inbox, "core", swap)
    fix, flag_block = call(
        fix_kernel,
        (shape((3 * FIX, NARROW), bf16), shape((FLAG_ROWS, NARROW), bf16)),
        (y[None].astype(i32), flag, inbox),
        (SMEM, VMEM, VMEM),
        flops=2 * 100_000_000,
        bytes_accessed=2_000_000,
    )
    fix, *along = lax.optimization_barrier((fix, *along))
    got = [
        lax.ppermute(fix[(d - 1) * FIX : d * FIX], "y", [(i, (i + d) % 4) for i in range(4)]) for d in (1, 2, 3)
    ]
    tail = jnp.concatenate(got + [flag_block], axis=0)
    other_tail = lax.ppermute(tail, "core", swap)
    spread = call(
        owned_kernel,
        shape((CHIPS, ROW_DEV // META, META), f32),
        (inbox, other, tail, other_tail),
        (VMEM, VMEM, VMEM, VMEM),
        scratch=(pltpu.VMEM((2 * OWN, FEAT), bf16), pltpu.VMEM((2 * OWN, META), bf16)),
        flops=2 * 1_600_000_000,
        bytes_accessed=4_000_000,
    )
    spread, *along = lax.optimization_barrier((spread, *along))
    same = jnp.concatenate(along, axis=0)
    busy_queries = jnp.concatenate([same, lax.ppermute(same, "core", swap)], axis=0)
    returned = lax.all_to_all(spread, CHIP_AXES, split_axis=0, concat_axis=0, tiled=True)
    partial = call(
        busy_kernel,
        shape((8, META), f32),
        (busy_keys, busy_queries),
        (VMEM, VMEM),
        flops=2 * 900_000_000,
        bytes_accessed=4_500_000,
    )
    partial, returned = lax.optimization_barrier((partial, returned))
    both = jnp.maximum(partial[:4], lax.ppermute(partial[4:], "core", swap))
    back = [lax.ppermute(both[d : d + 1], "y", [(i, (i + d) % 4) for i in range(4)]) for d in (1, 2, 3)]
    busy = jnp.concatenate([both[:1], *back], axis=0)
    out, worst = call(
        last_kernel,
        (shape((1, ROW_DEV), f32), shape((8, 128), f32)),
        (returned, busy, rank),
        (VMEM, VMEM, VMEM),
    )
    return out[0], worst[0, 0] > 2.0


def inverse_norms(row_values):
    wide_rows = row_values.astype(f32)
    return lax.rsqrt(jnp.sum(wide_rows * wide_rows, axis=1) + 1e-06)


def general(embeddings, clusters, order):
    owners, helpers = 16, 8
    slot_count = ROW_DEV * 5 // (2 * owners * helpers)
    total_rows = owners * helpers * slot_count
    owner_of = clusters // CL_OWN
    one_hot = (owner_of[:, None] == jnp.arange(owners, dtype=i32)[None, :]).astype(i32)
    before = jnp.cumsum(one_hot, axis=0) - one_hot
    place_in = jnp.sum(before * one_hot, axis=1)
    target = (owner_of * helpers + place_in % helpers) * slot_count + place_in // helpers
    outbox = jnp.zeros((total_rows, FEAT), embeddings.dtype).at[target].set(embeddings)
    outbox_cl = jnp.full((total_rows,), -1, i32).at[target].set(clusters)
    outbox_ord = jnp.zeros((total_rows,), i32).at[target].set(order)

    def exchange(value):
        return lax.all_to_all(value, ALL_AXES, split_axis=0, concat_axis=0, tiled=True)

    def gather(value):
        return lax.all_gather(value, HELPER_AXES, axis=0, tiled=True)

    inbox, inbox_cl, inbox_ord = exchange(outbox), exchange(outbox_cl), exchange(outbox_ord)
    query_inv = inverse_norms(inbox)

    def advance(best, block):
        key_emb, key_cl, key_ord = block
        gram = lax.dot_general(inbox, key_emb, (((1,), (1,)), ((), ())), preferred_element_type=f32)
        cosine = gram * query_inv[:, None] * inverse_norms(key_emb)[None, :]
        live = (key_cl[None, :] == inbox_cl[:, None]) & (key_ord[None, :] < inbox_ord[:, None])
        return jnp.maximum(best, jnp.max(jnp.where(live, cosine, -1.0), axis=1)), None

    blocks = (
        gather(inbox).reshape(helpers, total_rows, FEAT),
        gather(inbox_cl).reshape(helpers, total_rows),
        gather(inbox_ord).reshape(helpers, total_rows),
    )
    best, _ = lax.scan(advance, jnp.full((total_rows,), -1.0, f32), blocks)
    return exchange(best)[target]


def local(embeddings, clusters, order):
    out, overflow = fast(embeddings, clusters, order)
    return lax.cond(overflow, lambda: general(embeddings, clusters, order), lambda: out)


def solution(mesh):
    grid = Mesh(mesh.devices.reshape(4, 4, 4, 2), ALL_AXES)
    placed = (P(ALL_AXES, None), P(ALL_AXES), P(ALL_AXES))
    return jax.shard_map(local, mesh=grid, in_specs=placed, out_specs=P(ALL_AXES), check_vma=False)
```

```python
import jax
import jax.numpy as jnp
from jax import lax
from jax.experimental import pallas as pl
from jax.experimental.pallas import tpu as pltpu
from jax.sharding import Mesh, PartitionSpec as P

CL_OWN = 32
ROW_DEV = 512
FEAT = 1024
OWNERS = 16
CAP = 80
CHIPS = 64
BINS = 4
PLACES = 12
FIX = 32
META = 128
WIDE = FEAT + FEAT // 2 + META
NARROW = FEAT + META
SLOTS = CHIPS * 8
EXTRA = CHIPS * 4
FLAG_ROWS = 16
TAIL = 3 * FIX + FLAG_ROWS
MAIN = SLOTS + EXTRA
LOW = -1e30
BAD = 4.0
FIELDS = 16

CHIP_AXES = ("x", "z", "y")
ALL_AXES = ("x", "z", "y", "core")
CLUSTER_AXES = ("x", "z")
HELPER_AXES = ("y", "core")

f32 = jnp.float32
bf16 = jnp.bfloat16
i32 = jnp.int32


def iota(shape, axis):
    return lax.broadcasted_iota(i32, shape, axis)


def hot(condition):
    return jnp.where(condition, 1.0, 0.0).astype(bf16)


def mm(a, b):
    return lax.dot_general(a, b, (((1,), (0,)), ((), ())), preferred_element_type=f32)


def mm_t(a, b):
    return lax.dot_general(a, b, (((1,), (1,)), ((), ())), preferred_element_type=f32)


def pieces(value):
    high = value.astype(bf16)
    rest = value - high.astype(f32)
    middle = rest.astype(bf16)
    low = (rest - middle.astype(f32)).astype(bf16)
    return high, middle, low


def bin_of(local_cluster):
    folded = local_cluster & 7
    return jnp.minimum(folded, 7 - folded)


def pack_kernel(chip_ref, emb_hbm, cl_hbm, ord_hbm, out_ref, box_ref, rank_ref, flag_ref, emb_ref, cl_ref, ord_ref, sems):
    pairs = ((cl_hbm, cl_ref), (ord_hbm, ord_ref), (emb_hbm, emb_ref))
    copies = [pltpu.make_async_copy(src, dst, sems.at[k]) for k, (src, dst) in enumerate(pairs)]
    for copy in copies:
        copy.start()
    copies[0].wait()
    copies[1].wait()
    cl = cl_ref[...]
    order = ord_ref[...]
    rows = emb_ref.shape[0]
    owner = cl >> 5
    local_cluster = cl & (CL_OWN - 1)
    bins = bin_of(local_cluster)
    earlier = hot(iota((rows, rows), 0) < iota((rows, rows), 1))
    is_owner = iota((OWNERS, rows), 0) == owner
    owner_hot = jnp.where(is_owner, 1.0, 0.0)
    owner_count = jnp.sum(owner_hot, axis=1, keepdims=True)
    full = jnp.where(owner_count == CAP, 1.0, 0.0)
    busy = jnp.sum(owner_hot * full, axis=0, keepdims=True) > 0.5
    is_group = iota((OWNERS * BINS, rows), 0) == owner * BINS + bins
    group_hot = jnp.where(is_group, 1.0, 0.0)
    group_count = jnp.sum(group_hot, axis=1, keepdims=True)
    ranks = mm(jnp.concatenate([group_hot, owner_hot], axis=0).astype(bf16), earlier)
    place = jnp.sum(group_hot * ranks[: OWNERS * BINS], axis=0, keepdims=True).astype(i32)
    owner_place = jnp.sum(owner_hot * ranks[OWNERS * BINS :], axis=0, keepdims=True).astype(i32)
    over = place >= PLACES
    over_ranks = mm((owner_hot * jnp.where(over, 1.0, 0.0)).astype(bf16), earlier)
    spill = jnp.sum(owner_hot * over_ranks, axis=0, keepdims=True).astype(i32)
    taken = jnp.minimum(group_count, float(PLACES))
    new_bin = bins
    new_place = place
    passed = jnp.zeros_like(place)
    for step in range(BINS):
        b = (chip_ref[0] + step) & 3
        here = iota((OWNERS * BINS, rows), 0) == owner * BINS + b
        used = jnp.sum(jnp.where(here, taken, 0.0), axis=0, keepdims=True).astype(i32)
        fits = over & (spill >= passed) & (spill < passed + (PLACES - used))
        new_bin = jnp.where(fits, b, new_bin)
        new_place = jnp.where(fits, used + spill - passed, new_place)
        passed = passed + (PLACES - used)
    base = (owner * BINS + new_bin) * 8
    main_target = jnp.where(busy | (new_place >= 8), -1, base + new_place)
    extra_target = jnp.where(busy | (new_place < 8), -8, base + new_place - 8)
    rank = jnp.where(busy, owner_place, -1)
    rank_ref[...] = rank
    most = jnp.max(jnp.where(full > 0.5, 0.0, owner_count), axis=0, keepdims=True)
    flag = (jnp.sum(full, axis=0, keepdims=True) != 1.0) | (most > BINS * PLACES)
    flag_ref[...] = jnp.broadcast_to(jnp.where(flag, 1.0, 0.0), flag_ref.shape)
    copies[2].wait()
    emb = emb_ref[...]
    wide = emb.astype(f32)
    square = wide * wide
    square_high = square.astype(bf16)
    square_low = (square - square_high.astype(f32)).astype(bf16)
    ones = jnp.ones((8, emb.shape[1]), bf16)
    total = (mm_t(ones, square_high) + mm_t(ones, square_low))[0:1, :] + 1e-06
    inv = lax.rsqrt(total)
    inv = inv * (1.5 - 0.5 * total * inv * inv)
    high, middle, low = pieces(inv)
    at = iota((1, rows), 1)
    fields = [
        local_cluster.astype(f32),
        (order >> 8).astype(f32),
        (order & 255).astype(f32),
        high.astype(f32),
        middle.astype(f32),
        low.astype(f32),
        jnp.ones((1, rows), f32),
        jnp.full((1, rows), chip_ref[0], i32).astype(f32),
        (at >> 8).astype(f32),
        (at & 255).astype(f32),
    ]
    field_at = iota((META, rows), 0)
    meta = jnp.zeros((META, rows), f32)
    meta_extra = jnp.zeros((META, rows), f32)
    for k, value in enumerate(fields):
        meta = jnp.where(field_at == k, value, meta)
        meta_extra = jnp.where(field_at == FIELDS + k, value, meta_extra)
    meta = meta.astype(bf16)
    meta_extra = meta_extra.astype(bf16)
    pick = hot(iota((CAP, rows), 0) == rank)
    box_ref[:, :FEAT] = mm(pick, emb).astype(bf16)
    box_ref[:, FEAT:] = mm_t(pick, meta).astype(bf16)
    slot = iota((SLOTS, rows), 0)
    pick = hot(slot == main_target)
    pick_first = hot(slot == extra_target)
    pick_second = hot(slot - 4 == extra_target)
    half = FEAT // 2
    out_ref[:, :, :FEAT] = mm(pick, emb).astype(bf16).reshape(CHIPS, 8, FEAT)
    halves = mm(pick_first, emb[:, :half]) + mm(pick_second, emb[:, half:])
    out_ref[:, :, FEAT : FEAT + half] = halves.astype(bf16).reshape(CHIPS, 8, half)
    beside = mm_t(pick, meta) + mm_t(pick_first, meta_extra)
    out_ref[:, :, FEAT + half :] = beside.astype(bf16).reshape(CHIPS, 8, META)


def shifted(step):
    lanes = iota((META, META), 1)
    return hot((iota((META, META), 0) == lanes + step) & (lanes < FIELDS))


def fix_kernel(y_ref, flag_in_ref, in_ref, fix_ref, flag_ref):
    half = FEAT // 2
    meta = in_ref[:, :, FEAT + half :].reshape(SLOTS, META)
    turn = hot(iota((2 * FIELDS, META), 0) == iota((2 * FIELDS, META), 1))
    rows = mm_t(turn, meta)
    earlier = hot(iota((SLOTS, SLOTS), 0) < iota((SLOTS, SLOTS), 1))
    y = y_ref[0]

    def away(first):
        steps = (bin_of(rows[first : first + 1].astype(i32)) - y) & 3
        return jnp.where(rows[first + 6 : first + 7] > 0.5, steps, 0)

    main = away(0)
    extra = away(FIELDS)
    step_at = iota((8, SLOTS), 0)
    main_hot = jnp.where(step_at == main, 1.0, 0.0)
    extra_hot = jnp.where(step_at == extra, 1.0, 0.0)
    ranks = mm(jnp.concatenate([main_hot, extra_hot], axis=0).astype(bf16), earlier)
    main_count = jnp.sum(main_hot, axis=1, keepdims=True)
    count = main_count + jnp.sum(extra_hot, axis=1, keepdims=True)
    main_place = jnp.sum(main_hot * ranks[:8], axis=0, keepdims=True).astype(i32)
    extra_place = jnp.sum(extra_hot * (ranks[8:] + main_count), axis=0, keepdims=True).astype(i32)
    main_target = jnp.where((main > 0) & (main_place < FIX), (main - 1) * FIX + main_place, -1)
    extra_target = jnp.where((extra > 0) & (extra_place < FIX), (extra - 1) * FIX + extra_place, -1)
    slot = iota((3 * FIX, SLOTS), 0)
    pick = hot(slot == main_target)
    pick_first = hot(slot == extra_target)
    later = hot(iota((SLOTS, SLOTS), 1) == iota((SLOTS, SLOTS), 0) + 4)
    pick_second = mm(pick_first, later).astype(bf16)
    whole = in_ref[:, :, :FEAT].reshape(SLOTS, FEAT)
    halves = in_ref[:, :, FEAT : FEAT + half].reshape(SLOTS, half)
    taken = mm(pick, whole)
    fix_ref[:, :half] = (taken[:, :half] + mm(pick_first, halves)).astype(bf16)
    fix_ref[:, half:FEAT] = (taken[:, half:] + mm(pick_second, halves)).astype(bf16)
    beside = mm(mm(pick, meta).astype(bf16), shifted(0)) + mm(mm(pick_first, meta).astype(bf16), shifted(FIELDS))
    fix_ref[:, FEAT:] = beside.astype(bf16)
    step_row = iota((8, 1), 0)
    too_many = jnp.max(jnp.where((step_row > 0) & (count > FIX), 1.0, 0.0), axis=0, keepdims=True)
    flag = jnp.maximum(flag_in_ref[0:1, 0:1], too_many)
    spot = (iota(flag_ref.shape, 0) == 0) & (iota(flag_ref.shape, 1) == FEAT + 10)
    flag_ref[...] = jnp.where(spot, flag, 0.0).astype(bf16)


def key_columns(meta):
    wide = meta.astype(f32)
    position = wide[:, 1:2] * 256.0 + wide[:, 2:3]
    position = jnp.where(wide[:, 6:7] > 0.5, position, 1e9)
    return wide[:, 0:1], position, wide[:, 3:4] + wide[:, 4:5] + wide[:, 5:6]


def query_rows(meta):
    turn = hot(iota((FIELDS, META), 0) == iota((FIELDS, META), 1))
    return mm_t(turn, meta)


def best_over_keys(keys, metas, queries, query_fields, blocks):
    query_cl = query_fields[0:1]
    query_ord = query_fields[1:2] * 256.0 + query_fields[2:3]
    query_inv = query_fields[3:4] + query_fields[4:5] + query_fields[5:6]
    best = jnp.full(query_cl.shape, LOW, f32)
    size = keys.shape[0] // blocks
    for k in range(blocks):
        at = slice(k * size, (k + 1) * size)
        cl, position, inv = key_columns(metas[at, :])
        scaled = mm_t(keys[at, :], queries) * inv
        live = (cl == query_cl) & (position < query_ord)
        best = jnp.maximum(best, jnp.max(jnp.where(live, scaled, LOW), axis=0, keepdims=True))
    return jnp.maximum(best * query_inv, -1.0)


def selections():
    source = iota((EXTRA, SLOTS), 1)
    wanted = iota((EXTRA, SLOTS), 0)
    at = (wanted >> 2) * 8 + (wanted & 3)
    return hot(source == at), hot(source == at + 4)


def spread_out(best, fields, metas):
    rows = best.shape[1]
    from_chip = jnp.where((iota((CHIPS, rows), 0).astype(f32) == fields[7:8]) & (fields[6:7] > 0.5), 1.0, 0.0)
    high, middle, low = pieces(best)
    left = jnp.concatenate(
        [from_chip, from_chip * high.astype(f32), from_chip * middle.astype(f32), from_chip * low.astype(f32)], axis=0
    ).astype(bf16)
    wide = metas.astype(f32)
    place = wide[:, 8:9] * 256.0 + wide[:, 9:10]
    right = hot(iota((rows, ROW_DEV), 1).astype(f32) == place)
    spread = mm(left, right)
    value = spread[CHIPS : 2 * CHIPS] + spread[2 * CHIPS : 3 * CHIPS] + spread[3 * CHIPS :]
    return jnp.where(spread[:CHIPS] > 0.5, value, -1.0)


def main_kernel(own_ref, other_ref, keys_ref, metas_ref, best_ref):
    half = FEAT // 2
    first, second = selections()
    for k, ref in enumerate((own_ref, other_ref)):
        at = slice(k * MAIN, k * MAIN + SLOTS)
        keys_ref[at, :] = ref[:, :, :FEAT].reshape(SLOTS, FEAT)
        meta = ref[:, :, FEAT + half :].reshape(SLOTS, META)
        metas_ref[at, :] = meta
        at = slice(k * MAIN + SLOTS, (k + 1) * MAIN)
        halves = ref[:, :, FEAT : FEAT + half].reshape(SLOTS, half)
        keys_ref[at, :half] = mm(first, halves).astype(bf16)
        keys_ref[at, half:] = mm(second, halves).astype(bf16)
        metas_ref[at, :] = mm(mm(first, meta).astype(bf16), shifted(FIELDS)).astype(bf16)
    fields = query_rows(metas_ref[:MAIN, :])
    best = best_over_keys(keys_ref, metas_ref, keys_ref[:MAIN, :], fields, 4)
    best_ref[...] = jnp.broadcast_to(best, best_ref.shape)


def tail_kernel(keys_ref, metas_ref, best_ref, own_tail_ref, other_tail_ref, out_ref):
    metas = metas_ref[:MAIN, :]
    fields = query_rows(metas)
    best = best_ref[0:1, :]
    for tail in (own_tail_ref, other_tail_ref):
        best = jnp.maximum(best, best_over_keys(tail.at[:, :FEAT], tail.at[:, FEAT:], keys_ref[:MAIN, :], fields, 1))
    out = spread_out(best, fields, metas)
    metas = own_tail_ref[:, FEAT:]
    fields = query_rows(metas)
    queries = own_tail_ref[:, :FEAT]
    best = best_over_keys(keys_ref, metas_ref, queries, fields, 2)
    for tail in (own_tail_ref, other_tail_ref):
        best = jnp.maximum(best, best_over_keys(tail.at[:, :FEAT], tail.at[:, FEAT:], queries, fields, 1))
    out = jnp.maximum(out, spread_out(best, fields, metas))
    at = slice(3 * FIX, 3 * FIX + 1), slice(FEAT + 10, FEAT + 11)
    flag = jnp.maximum(own_tail_ref[at].astype(f32), other_tail_ref[at].astype(f32))
    out = jnp.where(flag > 0.5, BAD, out)
    for k in range(ROW_DEV // META):
        out_ref[:, k, :] = out[:, k * META : (k + 1) * META]


def busy_kernel(keys_ref, queries_ref, out_ref):
    fields = query_rows(queries_ref[:, FEAT:])
    best = best_over_keys(keys_ref.at[:, :FEAT], keys_ref.at[:, FEAT:], queries_ref[:, :FEAT], fields, 4)
    out_ref[...] = jnp.full(out_ref.shape, -1.0, f32)
    for k in range(8):
        out_ref[k : k + 1, :CAP] = best[:, k * CAP : (k + 1) * CAP]


def last_kernel(spread_ref, busy_ref, rank_ref, out_ref, flag_ref):
    best = jnp.max(spread_ref[...], axis=0)
    worst = jnp.max(jnp.max(best, axis=0, keepdims=True), axis=1, keepdims=True)
    flag_ref[...] = jnp.broadcast_to(worst, flag_ref.shape)
    owned = jnp.concatenate([best[k : k + 1] for k in range(ROW_DEV // META)], axis=1)
    busy = jnp.max(busy_ref[...], axis=0, keepdims=True)
    high, middle, low = pieces(busy)
    parts = jnp.concatenate([high.astype(f32), middle.astype(f32), low.astype(f32), jnp.zeros((5, META), f32)], axis=0)
    rank = rank_ref[...]
    pick = hot(iota((META, ROW_DEV), 0) == rank)
    taken = mm(parts.astype(bf16), pick)
    value = taken[0:1] + taken[1:2] + taken[2:3]
    out_ref[...] = jnp.where(rank >= 0, value, owned)


def call(kernel, shapes, args, specs, scratch=(), flops=0, bytes_accessed=0, vmem=28):
    return pl.pallas_call(
        kernel,
        out_shape=shapes,
        in_specs=[pl.BlockSpec(memory_space=s) for s in specs],
        out_specs=jax.tree.map(lambda _: pl.BlockSpec(memory_space=pltpu.VMEM), shapes),
        scratch_shapes=scratch,
        compiler_params=pltpu.CompilerParams(vmem_limit_bytes=vmem * 1024 * 1024),
        cost_estimate=pl.CostEstimate(flops=flops, bytes_accessed=bytes_accessed, transcendentals=0),
    )(*args)


VMEM, SMEM = pltpu.VMEM, pltpu.SMEM


def fast(embeddings, clusters, order):
    shape = jax.ShapeDtypeStruct
    y = lax.axis_index("y")
    chip = (lax.axis_index("x") * 4 + lax.axis_index("z")) * 4 + y
    outbox, box, rank, flag = call(
        pack_kernel,
        (
            shape((CHIPS, 8, WIDE), bf16),
            shape((CAP, NARROW), bf16),
            shape((1, ROW_DEV), i32),
            shape((8, 128), f32),
        ),
        (chip[None].astype(i32), embeddings, clusters[None, :], order[None, :]),
        (SMEM, pl.ANY, pl.ANY, pl.ANY),
        scratch=(
            pltpu.VMEM((ROW_DEV, FEAT), bf16),
            pltpu.VMEM((1, ROW_DEV), i32),
            pltpu.VMEM((1, ROW_DEV), i32),
            pltpu.SemaphoreType.DMA((3,)),
        ),
        vmem=58,
        flops=2 * 700_000_000,
        bytes_accessed=3_000_000,
    )
    busy_keys = lax.all_gather(box, CLUSTER_AXES, axis=0, tiled=True)
    inbox = lax.all_to_all(outbox, CHIP_AXES, split_axis=0, concat_axis=0, tiled=True)
    swap = [(0, 1), (1, 0)]
    along = [box] + [lax.ppermute(box, "y", [(i, (i - d) % 4) for i in range(4)]) for d in (1, 2, 3)]
    inbox, *along = lax.optimization_barrier((inbox, *along))
    other = lax.ppermute(inbox, "core", swap)
    fix, flag_block = call(
        fix_kernel,
        (shape((3 * FIX, NARROW), bf16), shape((FLAG_ROWS, NARROW), bf16)),
        (y[None].astype(i32), flag, inbox),
        (SMEM, VMEM, VMEM),
        flops=2 * 100_000_000,
        bytes_accessed=2_000_000,
    )
    keys, metas, best = call(
        main_kernel,
        (shape((2 * MAIN, FEAT), bf16), shape((2 * MAIN, META), bf16), shape((8, MAIN), f32)),
        (inbox, other),
        (VMEM, VMEM),
        flops=2 * 1_400_000_000,
        bytes_accessed=7_000_000,
    )
    got = [
        lax.ppermute(fix[(d - 1) * FIX : d * FIX], "y", [(i, (i + d) % 4) for i in range(4)]) for d in (1, 2, 3)
    ]
    best, *got = lax.optimization_barrier((best, *got))
    tail = jnp.concatenate(got + [flag_block], axis=0)
    other_tail = lax.ppermute(tail, "core", swap)
    spread = call(
        tail_kernel,
        shape((CHIPS, ROW_DEV // META, META), f32),
        (keys, metas, best, tail, other_tail),
        (VMEM, VMEM, VMEM, VMEM, VMEM),
        flops=2 * 500_000_000,
        bytes_accessed=4_000_000,
    )
    spread, *along = lax.optimization_barrier((spread, *along))
    same = jnp.concatenate(along, axis=0)
    busy_queries = jnp.concatenate([same, lax.ppermute(same, "core", swap)], axis=0)
    returned = lax.all_to_all(spread, CHIP_AXES, split_axis=0, concat_axis=0, tiled=True)
    partial = call(
        busy_kernel,
        shape((8, META), f32),
        (busy_keys, busy_queries),
        (VMEM, VMEM),
        flops=2 * 900_000_000,
        bytes_accessed=4_500_000,
    )
    partial, returned = lax.optimization_barrier((partial, returned))
    both = jnp.maximum(partial[:4], lax.ppermute(partial[4:], "core", swap))
    back = [lax.ppermute(both[d : d + 1], "y", [(i, (i + d) % 4) for i in range(4)]) for d in (1, 2, 3)]
    busy = jnp.concatenate([both[:1], *back], axis=0)
    out, worst = call(
        last_kernel,
        (shape((1, ROW_DEV), f32), shape((8, 128), f32)),
        (returned, busy, rank),
        (VMEM, VMEM, VMEM),
    )
    return out[0], worst[0, 0] > 2.0


def inverse_norms(row_values):
    wide_rows = row_values.astype(f32)
    return lax.rsqrt(jnp.sum(wide_rows * wide_rows, axis=1) + 1e-06)


def general(embeddings, clusters, order):
    owners, helpers = 16, 8
    slot_count = ROW_DEV * 5 // (2 * owners * helpers)
    total_rows = owners * helpers * slot_count
    owner_of = clusters // CL_OWN
    one_hot = (owner_of[:, None] == jnp.arange(owners, dtype=i32)[None, :]).astype(i32)
    before = jnp.cumsum(one_hot, axis=0) - one_hot
    place_in = jnp.sum(before * one_hot, axis=1)
    target = (owner_of * helpers + place_in % helpers) * slot_count + place_in // helpers
    outbox = jnp.zeros((total_rows, FEAT), embeddings.dtype).at[target].set(embeddings)
    outbox_cl = jnp.full((total_rows,), -1, i32).at[target].set(clusters)
    outbox_ord = jnp.zeros((total_rows,), i32).at[target].set(order)

    def exchange(value):
        return lax.all_to_all(value, ALL_AXES, split_axis=0, concat_axis=0, tiled=True)

    def gather(value):
        return lax.all_gather(value, HELPER_AXES, axis=0, tiled=True)

    inbox, inbox_cl, inbox_ord = exchange(outbox), exchange(outbox_cl), exchange(outbox_ord)
    query_inv = inverse_norms(inbox)

    def advance(best, block):
        key_emb, key_cl, key_ord = block
        gram = lax.dot_general(inbox, key_emb, (((1,), (1,)), ((), ())), preferred_element_type=f32)
        cosine = gram * query_inv[:, None] * inverse_norms(key_emb)[None, :]
        live = (key_cl[None, :] == inbox_cl[:, None]) & (key_ord[None, :] < inbox_ord[:, None])
        return jnp.maximum(best, jnp.max(jnp.where(live, cosine, -1.0), axis=1)), None

    blocks = (
        gather(inbox).reshape(helpers, total_rows, FEAT),
        gather(inbox_cl).reshape(helpers, total_rows),
        gather(inbox_ord).reshape(helpers, total_rows),
    )
    best, _ = lax.scan(advance, jnp.full((total_rows,), -1.0, f32), blocks)
    return exchange(best)[target]


def local(embeddings, clusters, order):
    out, overflow = fast(embeddings, clusters, order)
    return lax.cond(overflow, lambda: general(embeddings, clusters, order), lambda: out)


def solution(mesh):
    grid = Mesh(mesh.devices.reshape(4, 4, 4, 2), ALL_AXES)
    placed = (P(ALL_AXES, None), P(ALL_AXES), P(ALL_AXES))
    return jax.shard_map(local, mesh=grid, in_specs=placed, out_specs=P(ALL_AXES), check_vma=False)
```

```python
import jax
import jax.numpy as jnp
import numpy as np
from jax import lax
from jax.experimental import pallas as pl
from jax.experimental.pallas import tpu as pltpu
from jax.sharding import Mesh, PartitionSpec as P

CL_OWN = 32
ROW_DEV = 512
FEAT = 1024
OWNERS = 16
CAP = 80
CHIPS = 64
BINS = 4
PLACES = 12
FIX = 32
META = 128
HALF = FEAT // 2
META_AT = FEAT + HALF
BUSY_AT = META_AT + META
WIDE = BUSY_AT + FEAT + HALF
NARROW = FEAT + META
SLOTS = CHIPS * 8
EXTRA = CHIPS * 4
FLAG_ROWS = 16
TAIL = 3 * FIX + FLAG_ROWS
MAIN = SLOTS + EXTRA
LOW = -1e30
BAD = 4.0
FIELDS = 16

BLOCKS = (
    (1, 11, 12, 21, 32, 33, 43, 51, 58, 69, 70),
    (0, 11, 12, 13, 14, 15, 16, 17, 18, 19, 20),
    (10, 11, 12, 30, 31, 40, 41, 48, 54, 60, 61, 71),
    (5, 6, 11, 12, 25, 26, 42, 45, 56, 59, 75, 76),
    (3, 4, 11, 12, 23, 24, 38, 39, 50, 52, 62, 77),
    (9, 11, 12, 28, 29, 36, 37, 44, 57, 63, 64, 72),
    (7, 8, 11, 12, 27, 34, 49, 53, 67, 68, 73, 74),
    (2, 11, 12, 22, 35, 46, 47, 55, 65, 66, 78, 79),
    (0, 1, 2, 3, 4, 5, 6, 7, 8, 9, 10, 41),
    (1, 20, 30, 31, 41, 42, 50, 57, 67, 68, 78, 79),
    (1, 16, 25, 26, 36, 37, 46, 47, 54, 62, 73, 74),
    (1, 14, 15, 23, 24, 35, 45, 53, 60, 61, 72, 76),
    (1, 19, 28, 29, 40, 41, 49, 56, 65, 66, 77),
    (1, 17, 18, 27, 38, 39, 48, 55, 63, 64, 75, 76),
    (1, 13, 22, 34, 44, 52, 59, 71),
    (0, 69, 70, 71, 72, 73, 74, 75, 76, 77, 78, 79),
    (10, 20, 28, 29, 38, 39, 46, 47, 53, 59, 69, 70),
    (5, 6, 16, 30, 31, 35, 49, 52, 63, 64, 69, 70),
    (3, 4, 14, 15, 27, 42, 44, 54, 65, 66, 69, 70),
    (9, 19, 25, 26, 34, 41, 50, 55, 60, 61, 69, 70),
    (7, 8, 17, 18, 22, 40, 41, 45, 57, 62, 69, 70),
    (2, 13, 23, 24, 36, 37, 48, 56, 67, 68, 69, 70),
    (0, 43, 44, 45, 46, 47, 48, 49, 50, 76),
    (9, 20, 27, 35, 43, 56, 62, 71),
    (10, 16, 23, 24, 34, 40, 43, 57, 65, 66, 75, 76),
    (7, 8, 14, 15, 30, 31, 36, 37, 43, 55, 59, 77),
    (5, 6, 19, 22, 38, 39, 43, 54, 67, 68, 72),
    (2, 17, 18, 28, 29, 42, 43, 52, 60, 61, 73, 74),
    (3, 4, 13, 25, 26, 40, 43, 53, 63, 64, 78, 79),
    (0, 32, 33, 34, 35, 36, 37, 38, 39, 40, 41, 42),
    (7, 8, 20, 25, 26, 32, 33, 48, 52, 65, 66, 72),
    (3, 4, 16, 28, 29, 32, 33, 45, 55, 67, 68, 71),
    (10, 14, 15, 22, 32, 33, 50, 56, 63, 64, 73, 74),
    (2, 19, 30, 31, 32, 33, 41, 44, 53, 62, 75, 76),
    (9, 17, 18, 23, 24, 32, 33, 49, 54, 59, 78, 79),
    (5, 6, 13, 27, 32, 33, 46, 47, 57, 60, 61, 77),
    (0, 58, 59, 60, 61, 62, 63, 64, 65, 66, 67, 68),
    (5, 6, 20, 23, 24, 40, 41, 44, 55, 58, 73, 74),
    (9, 16, 22, 42, 48, 53, 58, 77),
    (2, 14, 15, 25, 26, 38, 39, 49, 57, 58, 71),
    (10, 19, 27, 36, 37, 45, 52, 58, 78, 79),
    (3, 4, 17, 18, 30, 31, 34, 46, 47, 56, 58, 72),
    (7, 8, 13, 28, 29, 35, 50, 54, 58, 75, 76),
    (0, 9, 51, 52, 53, 54, 55, 56, 57, 76),
    (3, 4, 20, 22, 36, 37, 49, 51, 60, 61, 75, 76),
    (2, 16, 27, 40, 41, 43, 50, 51, 59, 72),
    (5, 6, 14, 15, 28, 29, 34, 48, 51, 62, 78, 79),
    (7, 8, 19, 23, 24, 42, 46, 47, 51, 63, 64, 71),
    (10, 17, 18, 25, 26, 35, 44, 51, 67, 68, 76, 77),
    (9, 13, 30, 31, 38, 39, 45, 51, 65, 66, 73, 74),
    (0, 21, 22, 23, 24, 25, 26, 27, 28, 29, 30, 31),
    (2, 13, 20, 21, 34, 41, 45, 54, 63, 64, 76, 77),
    (7, 8, 16, 21, 38, 39, 44, 56, 60, 61, 78, 79),
    (9, 14, 15, 21, 40, 41, 46, 47, 52, 67, 68, 75),
    (3, 4, 19, 21, 35, 48, 57, 59, 73, 74),
    (5, 6, 17, 18, 21, 36, 37, 50, 53, 65, 66, 71),
    (10, 13, 21, 42, 49, 55, 62, 72),
)

CHIP_AXES = ("x", "z", "y")
ALL_AXES = ("x", "z", "y", "core")
CLUSTER_AXES = ("x", "z")
HELPER_AXES = ("y", "core")

f32 = jnp.float32
bf16 = jnp.bfloat16
i32 = jnp.int32


def iota(shape, axis):
    return lax.broadcasted_iota(i32, shape, axis)


def hot(condition):
    return jnp.where(condition, 1.0, 0.0).astype(bf16)


def mm(a, b):
    return lax.dot_general(a, b, (((1,), (0,)), ((), ())), preferred_element_type=f32)


def mm_t(a, b):
    return lax.dot_general(a, b, (((1,), (1,)), ((), ())), preferred_element_type=f32)


def pieces(value):
    high = value.astype(bf16)
    rest = value - high.astype(f32)
    middle = rest.astype(bf16)
    low = (rest - middle.astype(f32)).astype(bf16)
    return high, middle, low


def bin_of(local_cluster):
    folded = local_cluster & 7
    return jnp.minimum(folded, 7 - folded)


def spots(table_ref, column):
    return hot(iota((SLOTS, CAP), 1).astype(f32) == table_ref[:, column : column + 1].astype(f32))


def pack_kernel(chip_ref, emb_hbm, cl_hbm, ord_hbm, table_hbm, out_ref, flag_ref, emb_ref, cl_ref, ord_ref, table_ref, sems):
    pairs = ((cl_hbm, cl_ref), (ord_hbm, ord_ref), (emb_hbm, emb_ref), (table_hbm, table_ref))
    copies = [pltpu.make_async_copy(src, dst, sems.at[k]) for k, (src, dst) in enumerate(pairs)]
    for copy in copies:
        copy.start()
    copies[0].wait()
    copies[1].wait()
    cl = cl_ref[...]
    order = ord_ref[...]
    rows = emb_ref.shape[0]
    owner = cl >> 5
    local_cluster = cl & (CL_OWN - 1)
    bins = bin_of(local_cluster)
    earlier = hot(iota((rows, rows), 0) < iota((rows, rows), 1))
    is_owner = iota((OWNERS, rows), 0) == owner
    owner_hot = jnp.where(is_owner, 1.0, 0.0)
    owner_count = jnp.sum(owner_hot, axis=1, keepdims=True)
    full = jnp.where(owner_count == CAP, 1.0, 0.0)
    busy = jnp.sum(owner_hot * full, axis=0, keepdims=True) > 0.5
    is_group = iota((OWNERS * BINS, rows), 0) == owner * BINS + bins
    group_hot = jnp.where(is_group, 1.0, 0.0)
    group_count = jnp.sum(group_hot, axis=1, keepdims=True)
    ranks = mm(jnp.concatenate([group_hot, owner_hot], axis=0).astype(bf16), earlier)
    place = jnp.sum(group_hot * ranks[: OWNERS * BINS], axis=0, keepdims=True).astype(i32)
    owner_place = jnp.sum(owner_hot * ranks[OWNERS * BINS :], axis=0, keepdims=True).astype(i32)
    over = place >= PLACES
    over_ranks = mm((owner_hot * jnp.where(over, 1.0, 0.0)).astype(bf16), earlier)
    spill = jnp.sum(owner_hot * over_ranks, axis=0, keepdims=True).astype(i32)
    taken = jnp.minimum(group_count, float(PLACES))
    new_bin = bins
    new_place = place
    passed = jnp.zeros_like(place)
    for step in range(BINS):
        b = (chip_ref[0] + step) & 3
        here = iota((OWNERS * BINS, rows), 0) == owner * BINS + b
        used = jnp.sum(jnp.where(here, taken, 0.0), axis=0, keepdims=True).astype(i32)
        fits = over & (spill >= passed) & (spill < passed + (PLACES - used))
        new_bin = jnp.where(fits, b, new_bin)
        new_place = jnp.where(fits, used + spill - passed, new_place)
        passed = passed + (PLACES - used)
    base = (owner * BINS + new_bin) * 8
    main_target = jnp.where(busy | (new_place >= 8), -1, base + new_place)
    extra_target = jnp.where(busy | (new_place < 8), -8, base + new_place - 8)
    rank = jnp.where(busy, owner_place, -1)
    most = jnp.max(jnp.where(full > 0.5, 0.0, owner_count), axis=0, keepdims=True)
    flag = (jnp.sum(full, axis=0, keepdims=True) != 1.0) | (most > BINS * PLACES)
    flag_ref[...] = jnp.broadcast_to(jnp.where(flag, 1.0, 0.0), flag_ref.shape)
    copies[2].wait()
    copies[3].wait()
    emb = emb_ref[...]
    wide = emb.astype(f32)
    square = wide * wide
    square_high = square.astype(bf16)
    square_low = (square - square_high.astype(f32)).astype(bf16)
    ones = jnp.ones((8, emb.shape[1]), bf16)
    total = (mm_t(ones, square_high) + mm_t(ones, square_low))[0:1, :] + 1e-06
    inv = lax.rsqrt(total)
    inv = inv * (1.5 - 0.5 * total * inv * inv)
    high, middle, low = pieces(inv)
    at = iota((1, rows), 1)
    fields = [
        local_cluster.astype(f32),
        (order >> 8).astype(f32),
        (order & 255).astype(f32),
        high.astype(f32),
        middle.astype(f32),
        low.astype(f32),
        jnp.ones((1, rows), f32),
        jnp.full((1, rows), chip_ref[0], i32).astype(f32),
        (at >> 8).astype(f32),
        (at & 255).astype(f32),
    ]
    field_at = iota((META, rows), 0)
    meta = jnp.zeros((META, rows), f32)
    meta_extra = jnp.zeros((META, rows), f32)
    meta_busy = jnp.zeros((META, rows), f32)
    meta_busy_extra = jnp.zeros((META, rows), f32)
    for k, value in enumerate(fields):
        meta = jnp.where(field_at == k, value, meta)
        meta_extra = jnp.where(field_at == FIELDS + k, value, meta_extra)
        meta_busy = jnp.where(field_at == 2 * FIELDS + k, value, meta_busy)
        meta_busy_extra = jnp.where(field_at == 3 * FIELDS + k, value, meta_busy_extra)
    meta = meta.astype(bf16)
    meta_extra = meta_extra.astype(bf16)
    pick = hot(iota((CAP, rows), 0) == rank)
    box = mm(pick, emb).astype(bf16)
    box_meta = mm_t(pick, meta_busy.astype(bf16)).astype(bf16)
    box_meta_extra = mm_t(pick, meta_busy_extra.astype(bf16)).astype(bf16)
    slot = iota((SLOTS, rows), 0)
    pick = hot(slot == main_target)
    pick_first = hot(slot == extra_target)
    pick_second = hot(slot - 4 == extra_target)
    out_ref[:, :, :FEAT] = mm(pick, emb).astype(bf16).reshape(CHIPS, 8, FEAT)
    halves = mm(pick_first, emb[:, :HALF]) + mm(pick_second, emb[:, HALF:])
    out_ref[:, :, FEAT:META_AT] = halves.astype(bf16).reshape(CHIPS, 8, HALF)
    whole, first, second = (spots(table_ref, k) for k in range(3))
    beside = mm_t(pick, meta) + mm_t(pick_first, meta_extra) + mm(whole, box_meta) + mm(first, box_meta_extra)
    out_ref[:, :, META_AT:BUSY_AT] = beside.astype(bf16).reshape(CHIPS, 8, META)
    out_ref[:, :, BUSY_AT : BUSY_AT + FEAT] = mm(whole, box).astype(bf16).reshape(CHIPS, 8, FEAT)
    halves = mm(first, box[:, :HALF]) + mm(second, box[:, HALF:])
    out_ref[:, :, BUSY_AT + FEAT :] = halves.astype(bf16).reshape(CHIPS, 8, HALF)


def shifted(step):
    lanes = iota((META, META), 1)
    return hot((iota((META, META), 0) == lanes + step) & (lanes < FIELDS))


def fix_kernel(y_ref, flag_in_ref, in_ref, fix_ref, flag_ref):
    meta = in_ref[:, :, META_AT:BUSY_AT].reshape(SLOTS, META)
    turn = hot(iota((2 * FIELDS, META), 0) == iota((2 * FIELDS, META), 1))
    rows = mm_t(turn, meta)
    earlier = hot(iota((SLOTS, SLOTS), 0) < iota((SLOTS, SLOTS), 1))
    y = y_ref[0]

    def away(first):
        steps = (bin_of(rows[first : first + 1].astype(i32)) - y) & 3
        return jnp.where(rows[first + 6 : first + 7] > 0.5, steps, 0)

    main = away(0)
    extra = away(FIELDS)
    step_at = iota((8, SLOTS), 0)
    main_hot = jnp.where(step_at == main, 1.0, 0.0)
    extra_hot = jnp.where(step_at == extra, 1.0, 0.0)
    ranks = mm(jnp.concatenate([main_hot, extra_hot], axis=0).astype(bf16), earlier)
    main_count = jnp.sum(main_hot, axis=1, keepdims=True)
    count = main_count + jnp.sum(extra_hot, axis=1, keepdims=True)
    main_place = jnp.sum(main_hot * ranks[:8], axis=0, keepdims=True).astype(i32)
    extra_place = jnp.sum(extra_hot * (ranks[8:] + main_count), axis=0, keepdims=True).astype(i32)
    main_target = jnp.where((main > 0) & (main_place < FIX), (main - 1) * FIX + main_place, -1)
    extra_target = jnp.where((extra > 0) & (extra_place < FIX), (extra - 1) * FIX + extra_place, -1)
    slot = iota((3 * FIX, SLOTS), 0)
    pick = hot(slot == main_target)
    pick_first = hot(slot == extra_target)
    later = hot(iota((SLOTS, SLOTS), 1) == iota((SLOTS, SLOTS), 0) + 4)
    pick_second = mm(pick_first, later).astype(bf16)
    whole = in_ref[:, :, :FEAT].reshape(SLOTS, FEAT)
    halves = in_ref[:, :, FEAT:META_AT].reshape(SLOTS, HALF)
    taken = mm(pick, whole)
    fix_ref[:, :HALF] = (taken[:, :HALF] + mm(pick_first, halves)).astype(bf16)
    fix_ref[:, HALF:FEAT] = (taken[:, HALF:] + mm(pick_second, halves)).astype(bf16)
    beside = mm(mm(pick, meta).astype(bf16), shifted(0)) + mm(mm(pick_first, meta).astype(bf16), shifted(FIELDS))
    fix_ref[:, FEAT:] = beside.astype(bf16)
    step_row = iota((8, 1), 0)
    too_many = jnp.max(jnp.where((step_row > 0) & (count > FIX), 1.0, 0.0), axis=0, keepdims=True)
    flag = jnp.maximum(flag_in_ref[0:1, 0:1], too_many)
    spot = (iota(flag_ref.shape, 0) == 0) & (iota(flag_ref.shape, 1) == FEAT + 10)
    flag_ref[...] = jnp.where(spot, flag, 0.0).astype(bf16)


def key_columns(meta):
    wide = meta.astype(f32)
    position = wide[:, 1:2] * 256.0 + wide[:, 2:3]
    position = jnp.where(wide[:, 6:7] > 0.5, position, 1e9)
    return wide[:, 0:1], position, wide[:, 3:4] + wide[:, 4:5] + wide[:, 5:6]


def query_rows(meta):
    turn = hot(iota((FIELDS, META), 0) == iota((FIELDS, META), 1))
    return mm_t(turn, meta)


def best_over_keys(keys, metas, queries, query_fields, blocks):
    query_cl = query_fields[0:1]
    query_ord = query_fields[1:2] * 256.0 + query_fields[2:3]
    query_inv = query_fields[3:4] + query_fields[4:5] + query_fields[5:6]
    best = jnp.full(query_cl.shape, LOW, f32)
    size = keys.shape[0] // blocks
    for k in range(blocks):
        at = slice(k * size, (k + 1) * size)
        cl, position, inv = key_columns(metas[at, :])
        scaled = mm_t(keys[at, :], queries) * inv
        live = (cl == query_cl) & (position < query_ord)
        best = jnp.maximum(best, jnp.max(jnp.where(live, scaled, LOW), axis=0, keepdims=True))
    return jnp.maximum(best * query_inv, -1.0)


def selections():
    source = iota((EXTRA, SLOTS), 1)
    wanted = iota((EXTRA, SLOTS), 0)
    at = (wanted >> 2) * 8 + (wanted & 3)
    return hot(source == at), hot(source == at + 4)


def spread_out(best, fields, metas):
    rows = best.shape[1]
    from_chip = jnp.where((iota((CHIPS, rows), 0).astype(f32) == fields[7:8]) & (fields[6:7] > 0.5), 1.0, 0.0)
    high, middle, low = pieces(best)
    left = jnp.concatenate(
        [from_chip, from_chip * high.astype(f32), from_chip * middle.astype(f32), from_chip * low.astype(f32)], axis=0
    ).astype(bf16)
    wide = metas.astype(f32)
    place = wide[:, 8:9] * 256.0 + wide[:, 9:10]
    right = hot(iota((rows, ROW_DEV), 1).astype(f32) == place)
    spread = mm(left, right)
    value = spread[CHIPS : 2 * CHIPS] + spread[2 * CHIPS : 3 * CHIPS] + spread[3 * CHIPS :]
    return jnp.where(spread[:CHIPS] > 0.5, value, -1.0)


def unfold(ref, at, keys, first, second):
    keys[:SLOTS, :] = ref[:, :, at : at + FEAT].reshape(SLOTS, FEAT)
    halves = ref[:, :, at + FEAT : at + FEAT + HALF].reshape(SLOTS, HALF)
    keys[SLOTS:, :HALF] = mm(first, halves).astype(bf16)
    keys[SLOTS:, HALF:] = mm(second, halves).astype(bf16)


def unfold_meta(ref, owned, busy, first):
    meta = ref[:, :, META_AT:BUSY_AT].reshape(SLOTS, META)
    meta_first = mm(first, meta).astype(bf16)
    owned[:SLOTS, :] = meta
    owned[SLOTS:, :] = mm(meta_first, shifted(FIELDS)).astype(bf16)
    busy[:SLOTS, :] = mm(meta, shifted(2 * FIELDS)).astype(bf16)
    busy[SLOTS:, :] = mm(meta_first, shifted(3 * FIELDS)).astype(bf16)


def own_kernel(in_ref, keys_ref, metas_ref, best_ref):
    first, second = selections()
    unfold_meta(in_ref, metas_ref.at[0], metas_ref.at[1], first)
    for k, at in enumerate((0, BUSY_AT)):
        unfold(in_ref, at, keys_ref.at[k], first, second)
        fields = query_rows(metas_ref[k])
        best = best_over_keys(keys_ref.at[k], metas_ref.at[k], keys_ref[k], fields, 2)
        best_ref[k] = jnp.broadcast_to(best, best_ref.shape[1:])


def rest_kernel(in_ref, keys_ref, metas_ref, best_ref, own_tail_ref, other_tail_ref, out_ref, others, other_metas):
    first, second = selections()
    unfold_meta(in_ref, other_metas.at[0], other_metas.at[1], first)
    tails = own_tail_ref, other_tail_ref
    out = None
    for k, at in enumerate((0, BUSY_AT)):
        unfold(in_ref, at, others.at[k], first, second)
        metas, queries = metas_ref[k], keys_ref[k]
        fields = query_rows(metas)
        best = best_over_keys(others.at[k], other_metas.at[k], queries, fields, 2)
        best = jnp.maximum(best, best_ref[k, 0:1, :])
        if k == 0:
            for tail in tails:
                best = jnp.maximum(best, best_over_keys(tail.at[:, :FEAT], tail.at[:, FEAT:], queries, fields, 1))
        part = spread_out(best, fields, metas)
        out = part if out is None else jnp.maximum(out, part)
    metas, queries = own_tail_ref[:, FEAT:], own_tail_ref[:, :FEAT]
    fields = query_rows(metas)
    best = best_over_keys(keys_ref.at[0], metas_ref.at[0], queries, fields, 1)
    best = jnp.maximum(best, best_over_keys(others.at[0], other_metas.at[0], queries, fields, 1))
    for tail in tails:
        best = jnp.maximum(best, best_over_keys(tail.at[:, :FEAT], tail.at[:, FEAT:], queries, fields, 1))
    out = jnp.maximum(out, spread_out(best, fields, metas))
    at = slice(3 * FIX, 3 * FIX + 1), slice(FEAT + 10, FEAT + 11)
    flag = jnp.maximum(own_tail_ref[at].astype(f32), other_tail_ref[at].astype(f32))
    out = jnp.where(flag > 0.5, BAD, out)
    for k in range(ROW_DEV // META):
        out_ref[:, k, :] = out[:, k * META : (k + 1) * META]


def last_kernel(spread_ref, out_ref, flag_ref):
    best = jnp.max(spread_ref[...], axis=0)
    out_ref[...] = best
    worst = jnp.max(jnp.max(best, axis=0, keepdims=True), axis=1, keepdims=True)
    flag_ref[...] = jnp.broadcast_to(worst, flag_ref.shape)


def call(kernel, shapes, args, specs, scratch=(), flops=0, bytes_accessed=0, vmem=28):
    return pl.pallas_call(
        kernel,
        out_shape=shapes,
        in_specs=[pl.BlockSpec(memory_space=s) for s in specs],
        out_specs=jax.tree.map(lambda _: pl.BlockSpec(memory_space=pltpu.VMEM), shapes),
        scratch_shapes=scratch,
        compiler_params=pltpu.CompilerParams(vmem_limit_bytes=vmem * 1024 * 1024),
        cost_estimate=pl.CostEstimate(flops=flops, bytes_accessed=bytes_accessed, transcendentals=0),
    )(*args)


VMEM, SMEM = pltpu.VMEM, pltpu.SMEM


def places():
    table = np.full((SLOTS, META), -1, np.float32)
    for chip, block in enumerate(BLOCKS):
        for k, row in enumerate(block):
            if k < 8:
                table[chip * 8 + k, 0] = row
            else:
                table[chip * 8 + k - 8, 1] = row
                table[chip * 8 + k - 4, 2] = row
    return jnp.asarray(table, bf16)


def fast(embeddings, clusters, order):
    shape = jax.ShapeDtypeStruct
    y = lax.axis_index("y")
    chip = (lax.axis_index("x") * 4 + lax.axis_index("z")) * 4 + y
    swap = [(0, 1), (1, 0)]

    def to_chips(value):
        return lax.all_to_all(value, CHIP_AXES, split_axis=0, concat_axis=0, tiled=True)

    outbox, flag = call(
        pack_kernel,
        (shape((CHIPS, 8, WIDE), bf16), shape((8, 128), f32)),
        (chip[None].astype(i32), embeddings, clusters[None, :], order[None, :], places()),
        (SMEM, pl.ANY, pl.ANY, pl.ANY, pl.ANY),
        scratch=(
            pltpu.VMEM((ROW_DEV, FEAT), bf16),
            pltpu.VMEM((1, ROW_DEV), i32),
            pltpu.VMEM((1, ROW_DEV), i32),
            pltpu.VMEM((SLOTS, META), bf16),
            pltpu.SemaphoreType.DMA((4,)),
        ),
        vmem=58,
    )
    inbox = to_chips(outbox)
    other = lax.ppermute(inbox, "core", swap)
    fix, flag_block = call(
        fix_kernel,
        (shape((3 * FIX, NARROW), bf16), shape((FLAG_ROWS, NARROW), bf16)),
        (y[None].astype(i32), flag, inbox),
        (SMEM, VMEM, VMEM),
        flops=2 * 100_000_000,
        bytes_accessed=2_000_000,
    )
    got = [
        lax.ppermute(fix[(d - 1) * FIX : d * FIX], "y", [(i, (i + d) % 4) for i in range(4)]) for d in (1, 2, 3)
    ]
    keys, metas, best = call(
        own_kernel,
        (shape((2, MAIN, FEAT), bf16), shape((2, MAIN, META), bf16), shape((2, 8, MAIN), f32)),
        (inbox,),
        (VMEM,),
        flops=2 * 1_500_000_000,
        bytes_accessed=7_000_000,
    )
    best, *got = lax.optimization_barrier((best, *got))
    tail = jnp.concatenate(got + [flag_block], axis=0)
    other_tail = lax.ppermute(tail, "core", swap)
    spread = call(
        rest_kernel,
        shape((CHIPS, ROW_DEV // META, META), f32),
        (other, keys, metas, best, tail, other_tail),
        (VMEM,) * 6,
        scratch=(pltpu.VMEM((2, MAIN, FEAT), bf16), pltpu.VMEM((2, MAIN, META), bf16)),
        flops=2 * 2_000_000_000,
        bytes_accessed=7_000_000,
    )
    out, worst = call(
        last_kernel,
        (shape((ROW_DEV // META, META), f32), shape((8, 128), f32)),
        (to_chips(spread),),
        (VMEM,),
    )
    return out.reshape(ROW_DEV), worst[0, 0] > 2.0


def inverse_norms(row_values):
    wide_rows = row_values.astype(f32)
    return lax.rsqrt(jnp.sum(wide_rows * wide_rows, axis=1) + 1e-06)


def general(embeddings, clusters, order):
    owners, helpers = 16, 8
    slot_count = ROW_DEV * 5 // (2 * owners * helpers)
    total_rows = owners * helpers * slot_count
    owner_of = clusters // CL_OWN
    one_hot = (owner_of[:, None] == jnp.arange(owners, dtype=i32)[None, :]).astype(i32)
    before = jnp.cumsum(one_hot, axis=0) - one_hot
    place_in = jnp.sum(before * one_hot, axis=1)
    target = (owner_of * helpers + place_in % helpers) * slot_count + place_in // helpers
    outbox = jnp.zeros((total_rows, FEAT), embeddings.dtype).at[target].set(embeddings)
    outbox_cl = jnp.full((total_rows,), -1, i32).at[target].set(clusters)
    outbox_ord = jnp.zeros((total_rows,), i32).at[target].set(order)

    def exchange(value):
        return lax.all_to_all(value, ALL_AXES, split_axis=0, concat_axis=0, tiled=True)

    def gather(value):
        return lax.all_gather(value, HELPER_AXES, axis=0, tiled=True)

    inbox, inbox_cl, inbox_ord = exchange(outbox), exchange(outbox_cl), exchange(outbox_ord)
    query_inv = inverse_norms(inbox)

    def advance(best, block):
        key_emb, key_cl, key_ord = block
        gram = lax.dot_general(inbox, key_emb, (((1,), (1,)), ((), ())), preferred_element_type=f32)
        cosine = gram * query_inv[:, None] * inverse_norms(key_emb)[None, :]
        live = (key_cl[None, :] == inbox_cl[:, None]) & (key_ord[None, :] < inbox_ord[:, None])
        return jnp.maximum(best, jnp.max(jnp.where(live, cosine, -1.0), axis=1)), None

    blocks = (
        gather(inbox).reshape(helpers, total_rows, FEAT),
        gather(inbox_cl).reshape(helpers, total_rows),
        gather(inbox_ord).reshape(helpers, total_rows),
    )
    best, _ = lax.scan(advance, jnp.full((total_rows,), -1.0, f32), blocks)
    return exchange(best)[target]


def local(embeddings, clusters, order):
    out, overflow = fast(embeddings, clusters, order)
    return lax.cond(overflow, lambda: general(embeddings, clusters, order), lambda: out)


def solution(mesh):
    grid = Mesh(mesh.devices.reshape(4, 4, 4, 2), ALL_AXES)
    placed = (P(ALL_AXES, None), P(ALL_AXES), P(ALL_AXES))
    return jax.shard_map(local, mesh=grid, in_specs=placed, out_specs=P(ALL_AXES), check_vma=False)
```

```python
import jax
import jax.numpy as jnp
from jax import lax
from jax.experimental import pallas as pl
from jax.experimental.pallas import tpu as pltpu
from jax.sharding import Mesh, PartitionSpec as P

CL_OWN = 32
ROW_DEV = 512
FEAT = 1024
OWNERS = 16
CAP = 80
CHIPS = 64
BINS = 4
PLACES = 12
FIX = 32
META = 128
WIDE = FEAT + FEAT // 2 + META
NARROW = FEAT + META
SLOTS = CHIPS * 8
EXTRA = CHIPS * 4
FLAG_ROWS = 16
TAIL = 3 * FIX + FLAG_ROWS
MAIN = SLOTS + EXTRA
LOW = -1e30
BAD = 4.0
FIELDS = 16

CHIP_AXES = ("x", "z", "y")
ALL_AXES = ("x", "z", "y", "core")
CLUSTER_AXES = ("x", "z")
HELPER_AXES = ("y", "core")

f32 = jnp.float32
bf16 = jnp.bfloat16
i32 = jnp.int32


def iota(shape, axis):
    return lax.broadcasted_iota(i32, shape, axis)


def hot(condition):
    return jnp.where(condition, 1.0, 0.0).astype(bf16)


def mm(a, b):
    return lax.dot_general(a, b, (((1,), (0,)), ((), ())), preferred_element_type=f32)


def mm_t(a, b):
    return lax.dot_general(a, b, (((1,), (1,)), ((), ())), preferred_element_type=f32)


def pieces(value):
    high = value.astype(bf16)
    rest = value - high.astype(f32)
    middle = rest.astype(bf16)
    low = (rest - middle.astype(f32)).astype(bf16)
    return high, middle, low


def bin_of(local_cluster):
    folded = local_cluster & 7
    return jnp.minimum(folded, 7 - folded)


def pack_kernel(chip_ref, emb_hbm, cl_hbm, ord_hbm, out_ref, box_ref, rank_ref, flag_ref, emb_ref, cl_ref, ord_ref, sems):
    pairs = ((cl_hbm, cl_ref), (ord_hbm, ord_ref), (emb_hbm, emb_ref))
    copies = [pltpu.make_async_copy(src, dst, sems.at[k]) for k, (src, dst) in enumerate(pairs)]
    for copy in copies:
        copy.start()
    copies[0].wait()
    copies[1].wait()
    cl = cl_ref[...]
    order = ord_ref[...]
    rows = emb_ref.shape[0]
    owner = cl >> 5
    local_cluster = cl & (CL_OWN - 1)
    bins = bin_of(local_cluster)
    earlier = hot(iota((rows, rows), 0) < iota((rows, rows), 1))
    is_owner = iota((OWNERS, rows), 0) == owner
    owner_hot = jnp.where(is_owner, 1.0, 0.0)
    owner_count = jnp.sum(owner_hot, axis=1, keepdims=True)
    full = jnp.where(owner_count == CAP, 1.0, 0.0)
    busy = jnp.sum(owner_hot * full, axis=0, keepdims=True) > 0.5
    is_group = iota((OWNERS * BINS, rows), 0) == owner * BINS + bins
    group_hot = jnp.where(is_group, 1.0, 0.0)
    group_count = jnp.sum(group_hot, axis=1, keepdims=True)
    ranks = mm(jnp.concatenate([group_hot, owner_hot], axis=0).astype(bf16), earlier)
    place = jnp.sum(group_hot * ranks[: OWNERS * BINS], axis=0, keepdims=True).astype(i32)
    owner_place = jnp.sum(owner_hot * ranks[OWNERS * BINS :], axis=0, keepdims=True).astype(i32)
    over = place >= PLACES
    over_ranks = mm((owner_hot * jnp.where(over, 1.0, 0.0)).astype(bf16), earlier)
    spill = jnp.sum(owner_hot * over_ranks, axis=0, keepdims=True).astype(i32)
    taken = jnp.minimum(group_count, float(PLACES))
    new_bin = bins
    new_place = place
    passed = jnp.zeros_like(place)
    for step in range(BINS):
        b = (chip_ref[0] + step) & 3
        here = iota((OWNERS * BINS, rows), 0) == owner * BINS + b
        used = jnp.sum(jnp.where(here, taken, 0.0), axis=0, keepdims=True).astype(i32)
        fits = over & (spill >= passed) & (spill < passed + (PLACES - used))
        new_bin = jnp.where(fits, b, new_bin)
        new_place = jnp.where(fits, used + spill - passed, new_place)
        passed = passed + (PLACES - used)
    base = (owner * BINS + new_bin) * 8
    main_target = jnp.where(busy | (new_place >= 8), -1, base + new_place)
    extra_target = jnp.where(busy | (new_place < 8), -8, base + new_place - 8)
    rank = jnp.where(busy, owner_place, -1)
    rank_ref[...] = rank
    most = jnp.max(jnp.where(full > 0.5, 0.0, owner_count), axis=0, keepdims=True)
    flag = (jnp.sum(full, axis=0, keepdims=True) != 1.0) | (most > BINS * PLACES)
    flag_ref[...] = jnp.broadcast_to(jnp.where(flag, 1.0, 0.0), flag_ref.shape)
    copies[2].wait()
    emb = emb_ref[...]
    wide = emb.astype(f32)
    square = wide * wide
    square_high = square.astype(bf16)
    square_low = (square - square_high.astype(f32)).astype(bf16)
    ones = jnp.ones((8, emb.shape[1]), bf16)
    total = (mm_t(ones, square_high) + mm_t(ones, square_low))[0:1, :] + 1e-06
    inv = lax.rsqrt(total)
    inv = inv * (1.5 - 0.5 * total * inv * inv)
    high, middle, low = pieces(inv)
    at = iota((1, rows), 1)
    fields = [
        local_cluster.astype(f32),
        (order >> 8).astype(f32),
        (order & 255).astype(f32),
        high.astype(f32),
        middle.astype(f32),
        low.astype(f32),
        jnp.ones((1, rows), f32),
        jnp.full((1, rows), chip_ref[0], i32).astype(f32),
        (at >> 8).astype(f32),
        (at & 255).astype(f32),
    ]
    field_at = iota((META, rows), 0)
    meta = jnp.zeros((META, rows), f32)
    meta_extra = jnp.zeros((META, rows), f32)
    for k, value in enumerate(fields):
        meta = jnp.where(field_at == k, value, meta)
        meta_extra = jnp.where(field_at == FIELDS + k, value, meta_extra)
    meta = meta.astype(bf16)
    meta_extra = meta_extra.astype(bf16)
    pick = hot(iota((CAP, rows), 0) == rank)
    box_ref[:, :FEAT] = mm(pick, emb).astype(bf16)
    box_ref[:, FEAT:] = mm_t(pick, meta).astype(bf16)
    slot = iota((SLOTS, rows), 0)
    pick = hot(slot == main_target)
    pick_first = hot(slot == extra_target)
    pick_second = hot(slot - 4 == extra_target)
    half = FEAT // 2
    out_ref[:, :, :FEAT] = mm(pick, emb).astype(bf16).reshape(CHIPS, 8, FEAT)
    halves = mm(pick_first, emb[:, :half]) + mm(pick_second, emb[:, half:])
    out_ref[:, :, FEAT : FEAT + half] = halves.astype(bf16).reshape(CHIPS, 8, half)
    beside = mm_t(pick, meta) + mm_t(pick_first, meta_extra)
    out_ref[:, :, FEAT + half :] = beside.astype(bf16).reshape(CHIPS, 8, META)


def shifted(step):
    lanes = iota((META, META), 1)
    return hot((iota((META, META), 0) == lanes + step) & (lanes < FIELDS))


def fix_kernel(y_ref, flag_in_ref, in_ref, fix_ref, flag_ref):
    half = FEAT // 2
    meta = in_ref[:, :, FEAT + half :].reshape(SLOTS, META)
    turn = hot(iota((2 * FIELDS, META), 0) == iota((2 * FIELDS, META), 1))
    rows = mm_t(turn, meta)
    earlier = hot(iota((SLOTS, SLOTS), 0) < iota((SLOTS, SLOTS), 1))
    y = y_ref[0]

    def away(first):
        steps = (bin_of(rows[first : first + 1].astype(i32)) - y) & 3
        return jnp.where(rows[first + 6 : first + 7] > 0.5, steps, 0)

    main = away(0)
    extra = away(FIELDS)
    step_at = iota((8, SLOTS), 0)
    main_hot = jnp.where(step_at == main, 1.0, 0.0)
    extra_hot = jnp.where(step_at == extra, 1.0, 0.0)
    ranks = mm(jnp.concatenate([main_hot, extra_hot], axis=0).astype(bf16), earlier)
    main_count = jnp.sum(main_hot, axis=1, keepdims=True)
    count = main_count + jnp.sum(extra_hot, axis=1, keepdims=True)
    main_place = jnp.sum(main_hot * ranks[:8], axis=0, keepdims=True).astype(i32)
    extra_place = jnp.sum(extra_hot * (ranks[8:] + main_count), axis=0, keepdims=True).astype(i32)
    main_target = jnp.where((main > 0) & (main_place < FIX), (main - 1) * FIX + main_place, -1)
    extra_target = jnp.where((extra > 0) & (extra_place < FIX), (extra - 1) * FIX + extra_place, -1)
    slot = iota((3 * FIX, SLOTS), 0)
    pick = hot(slot == main_target)
    pick_first = hot(slot == extra_target)
    later = hot(iota((SLOTS, SLOTS), 1) == iota((SLOTS, SLOTS), 0) + 4)
    pick_second = mm(pick_first, later).astype(bf16)
    whole = in_ref[:, :, :FEAT].reshape(SLOTS, FEAT)
    halves = in_ref[:, :, FEAT : FEAT + half].reshape(SLOTS, half)
    taken = mm(pick, whole)
    fix_ref[:, :half] = (taken[:, :half] + mm(pick_first, halves)).astype(bf16)
    fix_ref[:, half:FEAT] = (taken[:, half:] + mm(pick_second, halves)).astype(bf16)
    beside = mm(mm(pick, meta).astype(bf16), shifted(0)) + mm(mm(pick_first, meta).astype(bf16), shifted(FIELDS))
    fix_ref[:, FEAT:] = beside.astype(bf16)
    step_row = iota((8, 1), 0)
    too_many = jnp.max(jnp.where((step_row > 0) & (count > FIX), 1.0, 0.0), axis=0, keepdims=True)
    flag = jnp.maximum(flag_in_ref[0:1, 0:1], too_many)
    spot = (iota(flag_ref.shape, 0) == 0) & (iota(flag_ref.shape, 1) == FEAT + 10)
    flag_ref[...] = jnp.where(spot, flag, 0.0).astype(bf16)


def key_columns(meta):
    wide = meta.astype(f32)
    position = wide[:, 1:2] * 256.0 + wide[:, 2:3]
    position = jnp.where(wide[:, 6:7] > 0.5, position, 1e9)
    return wide[:, 0:1], position, wide[:, 3:4] + wide[:, 4:5] + wide[:, 5:6]


def query_rows(meta):
    turn = hot(iota((FIELDS, META), 0) == iota((FIELDS, META), 1))
    return mm_t(turn, meta)


def best_over_keys(keys, metas, queries, query_fields, blocks):
    query_cl = query_fields[0:1]
    query_ord = query_fields[1:2] * 256.0 + query_fields[2:3]
    query_inv = query_fields[3:4] + query_fields[4:5] + query_fields[5:6]
    best = jnp.full(query_cl.shape, LOW, f32)
    size = keys.shape[0] // blocks
    for k in range(blocks):
        at = slice(k * size, (k + 1) * size)
        cl, position, inv = key_columns(metas[at, :])
        scaled = mm_t(keys[at, :], queries) * inv
        live = (cl == query_cl) & (position < query_ord)
        best = jnp.maximum(best, jnp.max(jnp.where(live, scaled, LOW), axis=0, keepdims=True))
    return jnp.maximum(best * query_inv, -1.0)


def selections():
    source = iota((EXTRA, SLOTS), 1)
    wanted = iota((EXTRA, SLOTS), 0)
    at = (wanted >> 2) * 8 + (wanted & 3)
    return hot(source == at), hot(source == at + 4)


def spread_out(best, fields, metas):
    rows = best.shape[1]
    from_chip = jnp.where((iota((CHIPS, rows), 0).astype(f32) == fields[7:8]) & (fields[6:7] > 0.5), 1.0, 0.0)
    high, middle, low = pieces(best)
    left = jnp.concatenate(
        [from_chip, from_chip * high.astype(f32), from_chip * middle.astype(f32), from_chip * low.astype(f32)], axis=0
    ).astype(bf16)
    wide = metas.astype(f32)
    place = wide[:, 8:9] * 256.0 + wide[:, 9:10]
    right = hot(iota((rows, ROW_DEV), 1).astype(f32) == place)
    spread = mm(left, right)
    value = spread[CHIPS : 2 * CHIPS] + spread[2 * CHIPS : 3 * CHIPS] + spread[3 * CHIPS :]
    return jnp.where(spread[:CHIPS] > 0.5, value, -1.0)


def main_kernel(own_ref, other_ref, keys_ref, metas_ref, best_ref):
    half = FEAT // 2
    first, second = selections()
    for k, ref in enumerate((own_ref, other_ref)):
        at = slice(k * MAIN, k * MAIN + SLOTS)
        keys_ref[at, :] = ref[:, :, :FEAT].reshape(SLOTS, FEAT)
        meta = ref[:, :, FEAT + half :].reshape(SLOTS, META)
        metas_ref[at, :] = meta
        at = slice(k * MAIN + SLOTS, (k + 1) * MAIN)
        halves = ref[:, :, FEAT : FEAT + half].reshape(SLOTS, half)
        keys_ref[at, :half] = mm(first, halves).astype(bf16)
        keys_ref[at, half:] = mm(second, halves).astype(bf16)
        metas_ref[at, :] = mm(mm(first, meta).astype(bf16), shifted(FIELDS)).astype(bf16)
    fields = query_rows(metas_ref[:MAIN, :])
    best = best_over_keys(keys_ref, metas_ref, keys_ref[:MAIN, :], fields, 4)
    best_ref[...] = jnp.broadcast_to(best, best_ref.shape)


def tail_kernel(keys_ref, metas_ref, best_ref, own_tail_ref, other_tail_ref, out_ref):
    metas = metas_ref[:MAIN, :]
    fields = query_rows(metas)
    best = best_ref[0:1, :]
    for tail in (own_tail_ref, other_tail_ref):
        best = jnp.maximum(best, best_over_keys(tail.at[:, :FEAT], tail.at[:, FEAT:], keys_ref[:MAIN, :], fields, 1))
    out = spread_out(best, fields, metas)
    metas = own_tail_ref[:, FEAT:]
    fields = query_rows(metas)
    queries = own_tail_ref[:, :FEAT]
    best = best_over_keys(keys_ref, metas_ref, queries, fields, 2)
    for tail in (own_tail_ref, other_tail_ref):
        best = jnp.maximum(best, best_over_keys(tail.at[:, :FEAT], tail.at[:, FEAT:], queries, fields, 1))
    out = jnp.maximum(out, spread_out(best, fields, metas))
    at = slice(3 * FIX, 3 * FIX + 1), slice(FEAT + 10, FEAT + 11)
    flag = jnp.maximum(own_tail_ref[at].astype(f32), other_tail_ref[at].astype(f32))
    out = jnp.where(flag > 0.5, BAD, out)
    for k in range(ROW_DEV // META):
        out_ref[:, k, :] = out[:, k * META : (k + 1) * META]


def busy_kernel(keys_ref, queries_ref, out_ref):
    fields = query_rows(queries_ref[:, FEAT:])
    best = best_over_keys(keys_ref.at[:, :FEAT], keys_ref.at[:, FEAT:], queries_ref[:, :FEAT], fields, 4)
    out_ref[...] = jnp.full(out_ref.shape, -1.0, f32)
    for k in range(8):
        at = 2 * (k & 3) + (k >> 2)
        out_ref[at : at + 1, :CAP] = best[:, k * CAP : (k + 1) * CAP]


def last_kernel(spread_ref, busy_ref, rank_ref, out_ref, flag_ref):
    best = jnp.max(spread_ref[...], axis=0)
    worst = jnp.max(jnp.max(best, axis=0, keepdims=True), axis=1, keepdims=True)
    flag_ref[...] = jnp.broadcast_to(worst, flag_ref.shape)
    owned = jnp.concatenate([best[k : k + 1] for k in range(ROW_DEV // META)], axis=1)
    busy = jnp.max(busy_ref[...], axis=0, keepdims=True)
    high, middle, low = pieces(busy)
    parts = jnp.concatenate([high.astype(f32), middle.astype(f32), low.astype(f32), jnp.zeros((5, META), f32)], axis=0)
    rank = rank_ref[...]
    pick = hot(iota((META, ROW_DEV), 0) == rank)
    taken = mm(parts.astype(bf16), pick)
    value = taken[0:1] + taken[1:2] + taken[2:3]
    out_ref[...] = jnp.where(rank >= 0, value, owned)


def call(kernel, shapes, args, specs, scratch=(), flops=0, bytes_accessed=0, vmem=28):
    return pl.pallas_call(
        kernel,
        out_shape=shapes,
        in_specs=[pl.BlockSpec(memory_space=s) for s in specs],
        out_specs=jax.tree.map(lambda _: pl.BlockSpec(memory_space=pltpu.VMEM), shapes),
        scratch_shapes=scratch,
        compiler_params=pltpu.CompilerParams(vmem_limit_bytes=vmem * 1024 * 1024),
        cost_estimate=pl.CostEstimate(flops=flops, bytes_accessed=bytes_accessed, transcendentals=0),
    )(*args)


VMEM, SMEM = pltpu.VMEM, pltpu.SMEM


def fast(embeddings, clusters, order):
    shape = jax.ShapeDtypeStruct
    y = lax.axis_index("y")
    chip = (lax.axis_index("x") * 4 + lax.axis_index("z")) * 4 + y
    outbox, box, rank, flag = call(
        pack_kernel,
        (
            shape((CHIPS, 8, WIDE), bf16),
            shape((CAP, NARROW), bf16),
            shape((1, ROW_DEV), i32),
            shape((8, 128), f32),
        ),
        (chip[None].astype(i32), embeddings, clusters[None, :], order[None, :]),
        (SMEM, pl.ANY, pl.ANY, pl.ANY),
        scratch=(
            pltpu.VMEM((ROW_DEV, FEAT), bf16),
            pltpu.VMEM((1, ROW_DEV), i32),
            pltpu.VMEM((1, ROW_DEV), i32),
            pltpu.SemaphoreType.DMA((3,)),
        ),
        vmem=58,
        flops=2 * 700_000_000,
        bytes_accessed=3_000_000,
    )
    busy_keys = lax.all_gather(box, CLUSTER_AXES, axis=0, tiled=True)
    inbox = lax.all_to_all(outbox, CHIP_AXES, split_axis=0, concat_axis=0, tiled=True)
    swap = [(0, 1), (1, 0)]
    along = [box] + [lax.ppermute(box, "y", [(i, (i - d) % 4) for i in range(4)]) for d in (1, 2, 3)]
    inbox, *along = lax.optimization_barrier((inbox, *along))
    other = lax.ppermute(inbox, "core", swap)
    fix, flag_block = call(
        fix_kernel,
        (shape((3 * FIX, NARROW), bf16), shape((FLAG_ROWS, NARROW), bf16)),
        (y[None].astype(i32), flag, inbox),
        (SMEM, VMEM, VMEM),
        flops=2 * 100_000_000,
        bytes_accessed=2_000_000,
    )
    keys, metas, best = call(
        main_kernel,
        (shape((2 * MAIN, FEAT), bf16), shape((2 * MAIN, META), bf16), shape((8, MAIN), f32)),
        (inbox, other),
        (VMEM, VMEM),
        flops=2 * 1_400_000_000,
        bytes_accessed=7_000_000,
    )
    got = [
        lax.ppermute(fix[(d - 1) * FIX : d * FIX], "y", [(i, (i + d) % 4) for i in range(4)]) for d in (1, 2, 3)
    ]
    best, *got = lax.optimization_barrier((best, *got))
    tail = jnp.concatenate(got + [flag_block], axis=0)
    other_tail = lax.ppermute(tail, "core", swap)
    spread = call(
        tail_kernel,
        shape((CHIPS, ROW_DEV // META, META), f32),
        (keys, metas, best, tail, other_tail),
        (VMEM, VMEM, VMEM, VMEM, VMEM),
        flops=2 * 500_000_000,
        bytes_accessed=4_000_000,
    )
    spread, *along = lax.optimization_barrier((spread, *along))
    same = jnp.concatenate(along, axis=0)
    busy_queries = jnp.concatenate([same, lax.ppermute(same, "core", swap)], axis=0)
    returned = lax.all_to_all(spread, CHIP_AXES, split_axis=0, concat_axis=0, tiled=True)
    partial = call(
        busy_kernel,
        shape((8, META), f32),
        (busy_keys, busy_queries),
        (VMEM, VMEM),
        flops=2 * 900_000_000,
        bytes_accessed=4_500_000,
    )
    parts = [partial[:2]]
    for d in (1, 2, 3):
        parts.append(lax.ppermute(partial[2 * d : 2 * d + 2], "y", [(i, (i + d) % 4) for i in range(4)]))
    to_other = jnp.concatenate([part[1:] for part in parts], axis=0)
    to_other, returned = lax.optimization_barrier((to_other, returned))
    busy = jnp.concatenate([part[:1] for part in parts] + [lax.ppermute(to_other, "core", swap)], axis=0)
    out, worst = call(
        last_kernel,
        (shape((1, ROW_DEV), f32), shape((8, 128), f32)),
        (returned, busy, rank),
        (VMEM, VMEM, VMEM),
    )
    return out[0], worst[0, 0] > 2.0


def inverse_norms(row_values):
    wide_rows = row_values.astype(f32)
    return lax.rsqrt(jnp.sum(wide_rows * wide_rows, axis=1) + 1e-06)


def general(embeddings, clusters, order):
    owners, helpers = 16, 8
    slot_count = ROW_DEV * 5 // (2 * owners * helpers)
    total_rows = owners * helpers * slot_count
    owner_of = clusters // CL_OWN
    one_hot = (owner_of[:, None] == jnp.arange(owners, dtype=i32)[None, :]).astype(i32)
    before = jnp.cumsum(one_hot, axis=0) - one_hot
    place_in = jnp.sum(before * one_hot, axis=1)
    target = (owner_of * helpers + place_in % helpers) * slot_count + place_in // helpers
    outbox = jnp.zeros((total_rows, FEAT), embeddings.dtype).at[target].set(embeddings)
    outbox_cl = jnp.full((total_rows,), -1, i32).at[target].set(clusters)
    outbox_ord = jnp.zeros((total_rows,), i32).at[target].set(order)

    def exchange(value):
        return lax.all_to_all(value, ALL_AXES, split_axis=0, concat_axis=0, tiled=True)

    def gather(value):
        return lax.all_gather(value, HELPER_AXES, axis=0, tiled=True)

    inbox, inbox_cl, inbox_ord = exchange(outbox), exchange(outbox_cl), exchange(outbox_ord)
    query_inv = inverse_norms(inbox)

    def advance(best, block):
        key_emb, key_cl, key_ord = block
        gram = lax.dot_general(inbox, key_emb, (((1,), (1,)), ((), ())), preferred_element_type=f32)
        cosine = gram * query_inv[:, None] * inverse_norms(key_emb)[None, :]
        live = (key_cl[None, :] == inbox_cl[:, None]) & (key_ord[None, :] < inbox_ord[:, None])
        return jnp.maximum(best, jnp.max(jnp.where(live, cosine, -1.0), axis=1)), None

    blocks = (
        gather(inbox).reshape(helpers, total_rows, FEAT),
        gather(inbox_cl).reshape(helpers, total_rows),
        gather(inbox_ord).reshape(helpers, total_rows),
    )
    best, _ = lax.scan(advance, jnp.full((total_rows,), -1.0, f32), blocks)
    return exchange(best)[target]


def local(embeddings, clusters, order):
    out, overflow = fast(embeddings, clusters, order)
    return lax.cond(overflow, lambda: general(embeddings, clusters, order), lambda: out)


def solution(mesh):
    grid = Mesh(mesh.devices.reshape(4, 4, 4, 2), ALL_AXES)
    placed = (P(ALL_AXES, None), P(ALL_AXES), P(ALL_AXES))
    return jax.shard_map(local, mesh=grid, in_specs=placed, out_specs=P(ALL_AXES), check_vma=False)
```

```python
import jax
import jax.numpy as jnp
from jax import lax
from jax.experimental import pallas as pl
from jax.experimental.pallas import tpu as pltpu
from jax.sharding import Mesh, PartitionSpec as P

CL_OWN = 32
ROW_DEV = 512
FEAT = 1024
OWNERS = 16
CAP = 80
CHIPS = 64
BINS = 4
PLACES = 11
FIX = 32
META = 128
WIDE = FEAT + FEAT // 2
NARROW = FEAT + META
SLOTS = CHIPS * 8
EXTRA = CHIPS * 4
FLAG_ROWS = 16
TAIL = 3 * FIX + FLAG_ROWS
MAIN = SLOTS + EXTRA
LOW = -1e30
BAD = 4.0
FIELDS = 16
FIELD_LANES = 16 * FIELDS
FIELD_ROW = 3

CHIP_AXES = ("x", "z", "y")
ALL_AXES = ("x", "z", "y", "core")
CLUSTER_AXES = ("x", "z")
HELPER_AXES = ("y", "core")

f32 = jnp.float32
bf16 = jnp.bfloat16
i32 = jnp.int32


def iota(shape, axis):
    return lax.broadcasted_iota(i32, shape, axis)


def hot(condition):
    return jnp.where(condition, 1.0, 0.0).astype(bf16)


def mm(a, b):
    return lax.dot_general(a, b, (((1,), (0,)), ((), ())), preferred_element_type=f32)


def mm_t(a, b):
    return lax.dot_general(a, b, (((1,), (1,)), ((), ())), preferred_element_type=f32)


def pieces(value):
    high = value.astype(bf16)
    rest = value - high.astype(f32)
    middle = rest.astype(bf16)
    low = (rest - middle.astype(f32)).astype(bf16)
    return high, middle, low


def bin_of(local_cluster):
    folded = local_cluster & 7
    return jnp.minimum(folded, 7 - folded)


def pack_kernel(chip_ref, emb_hbm, cl_hbm, ord_hbm, out_ref, box_ref, rank_ref, flag_ref, emb_ref, cl_ref, ord_ref, sems):
    pairs = ((cl_hbm, cl_ref), (ord_hbm, ord_ref), (emb_hbm, emb_ref))
    copies = [pltpu.make_async_copy(src, dst, sems.at[k]) for k, (src, dst) in enumerate(pairs)]
    for copy in copies:
        copy.start()
    copies[0].wait()
    copies[1].wait()
    cl = cl_ref[...]
    order = ord_ref[...]
    rows = emb_ref.shape[0]
    owner = cl >> 5
    local_cluster = cl & (CL_OWN - 1)
    bins = bin_of(local_cluster)
    earlier = hot(iota((rows, rows), 0) < iota((rows, rows), 1))
    is_owner = iota((OWNERS, rows), 0) == owner
    owner_hot = jnp.where(is_owner, 1.0, 0.0)
    owner_count = jnp.sum(owner_hot, axis=1, keepdims=True)
    full = jnp.where(owner_count == CAP, 1.0, 0.0)
    busy = jnp.sum(owner_hot * full, axis=0, keepdims=True) > 0.5
    is_group = iota((OWNERS * BINS, rows), 0) == owner * BINS + bins
    group_hot = jnp.where(is_group, 1.0, 0.0)
    group_count = jnp.sum(group_hot, axis=1, keepdims=True)
    ranks = mm(jnp.concatenate([group_hot, owner_hot], axis=0).astype(bf16), earlier)
    place = jnp.sum(group_hot * ranks[: OWNERS * BINS], axis=0, keepdims=True).astype(i32)
    owner_place = jnp.sum(owner_hot * ranks[OWNERS * BINS :], axis=0, keepdims=True).astype(i32)
    over = place >= PLACES
    over_ranks = mm((owner_hot * jnp.where(over, 1.0, 0.0)).astype(bf16), earlier)
    spill = jnp.sum(owner_hot * over_ranks, axis=0, keepdims=True).astype(i32)
    taken = jnp.minimum(group_count, float(PLACES))
    new_bin = bins
    new_place = place
    passed = jnp.zeros_like(place)
    for step in range(BINS):
        b = (chip_ref[0] + step) & 3
        here = iota((OWNERS * BINS, rows), 0) == owner * BINS + b
        used = jnp.sum(jnp.where(here, taken, 0.0), axis=0, keepdims=True).astype(i32)
        fits = over & (spill >= passed) & (spill < passed + (PLACES - used))
        new_bin = jnp.where(fits, b, new_bin)
        new_place = jnp.where(fits, used + spill - passed, new_place)
        passed = passed + (PLACES - used)
    base = (owner * BINS + new_bin) * 8
    main_target = jnp.where(busy | (new_place >= 8), -1, base + new_place)
    extra_target = jnp.where(busy | (new_place < 8), -8, base + new_place - 8)
    rank = jnp.where(busy, owner_place, -1)
    rank_ref[...] = rank
    most = jnp.max(jnp.where(full > 0.5, 0.0, owner_count), axis=0, keepdims=True)
    flag = (jnp.sum(full, axis=0, keepdims=True) != 1.0) | (most > BINS * PLACES)
    flag_ref[...] = jnp.broadcast_to(jnp.where(flag, 1.0, 0.0), flag_ref.shape)
    copies[2].wait()
    emb = emb_ref[...]
    wide = emb.astype(f32)
    square = wide * wide
    folded = square[:, :META]
    for k in range(1, FEAT // META):
        folded = folded + square[:, k * META : (k + 1) * META]
    ones = jnp.ones((8, META), bf16)
    total = sum(mm_t(ones, piece) for piece in pieces(folded))[0:1, :] + 1e-06
    inv = lax.rsqrt(total)
    inv = inv * (1.5 - 0.5 * total * inv * inv)
    high, middle, low = pieces(inv)
    at = iota((1, rows), 1)
    fields = [
        local_cluster.astype(f32),
        (order >> 8).astype(f32),
        (order & 255).astype(f32),
        high.astype(f32),
        middle.astype(f32),
        low.astype(f32),
        jnp.ones((1, rows), f32),
        jnp.full((1, rows), chip_ref[0], i32).astype(f32),
        (at >> 8).astype(f32),
        (at & 255).astype(f32),
    ]
    field_at = iota((META, rows), 0)
    meta = jnp.zeros((META, rows), f32)
    for k, value in enumerate(fields):
        meta = jnp.where(field_at == k, value, meta)
    sent = jnp.concatenate([meta[:FIELDS]] * (FIELD_LANES // FIELDS), axis=0)
    sent = jnp.where((iota((FIELD_LANES, rows), 0) >> 4) == new_place, sent, 0.0).astype(bf16)
    meta = meta.astype(bf16)
    pick = hot(iota((CAP, rows), 0) == rank)
    box_ref[:, :FEAT] = mm(pick, emb).astype(bf16)
    box_ref[:, FEAT:] = mm_t(pick, meta).astype(bf16)
    slot = iota((SLOTS, rows), 0)
    pick = hot(slot == main_target)
    pick_first = hot(slot == extra_target)
    pick_second = hot(slot - 4 == extra_target)
    half = FEAT // 2
    out_ref[:, :, :FEAT] = mm(pick, emb).astype(bf16).reshape(CHIPS, 8, FEAT)
    halves = mm(pick_first, emb[:, :half]) + mm(pick_second, emb[:, half:])
    to_chip = hot(iota((CHIPS, rows), 0) == jnp.where(busy, -1, owner * BINS + new_bin))
    beside = mm_t(to_chip, sent).astype(bf16)
    beside = mm(hot(iota((SLOTS, CHIPS), 0) == iota((SLOTS, CHIPS), 1) * 8 + FIELD_ROW), beside)
    halves = jnp.concatenate([halves[:, :FIELD_LANES] + beside, halves[:, FIELD_LANES:]], axis=1)
    out_ref[:, :, FEAT:] = halves.astype(bf16).reshape(CHIPS, 8, half)


def fields_of(ref):
    block = ref[:, :, FEAT : FEAT + FIELD_LANES].reshape(SLOTS, FIELD_LANES)
    spread = mm(hot(iota((SLOTS, SLOTS), 1) == (iota((SLOTS, SLOTS), 0) >> 3) * 8 + FIELD_ROW), block)
    place, group = iota((SLOTS, FIELD_LANES), 0) & 7, iota((SLOTS, FIELD_LANES), 1) >> 4
    whole = jnp.where(group == place, spread, 0.0).astype(bf16)
    half = jnp.where(group == place + 8, spread, 0.0).astype(bf16)
    source, lane = iota((FIELD_LANES, META), 0) & 15, iota((FIELD_LANES, META), 1)
    return (mm(whole, hot(source == lane)) + mm(half, hot(source == lane - FIELDS))).astype(bf16)


def shifted(step):
    lanes = iota((META, META), 1)
    return hot((iota((META, META), 0) == lanes + step) & (lanes < FIELDS))


def fix_kernel(y_ref, flag_in_ref, in_ref, fix_ref, flag_ref):
    half = FEAT // 2
    meta = fields_of(in_ref)
    turn = hot(iota((2 * FIELDS, META), 0) == iota((2 * FIELDS, META), 1))
    rows = mm_t(turn, meta)
    earlier = hot(iota((SLOTS, SLOTS), 0) < iota((SLOTS, SLOTS), 1))
    y = y_ref[0]

    def away(first):
        steps = (bin_of(rows[first : first + 1].astype(i32)) - y) & 3
        return jnp.where(rows[first + 6 : first + 7] > 0.5, steps, 0)

    main = away(0)
    extra = away(FIELDS)
    step_at = iota((8, SLOTS), 0)
    main_hot = jnp.where(step_at == main, 1.0, 0.0)
    extra_hot = jnp.where(step_at == extra, 1.0, 0.0)
    ranks = mm(jnp.concatenate([main_hot, extra_hot], axis=0).astype(bf16), earlier)
    main_count = jnp.sum(main_hot, axis=1, keepdims=True)
    count = main_count + jnp.sum(extra_hot, axis=1, keepdims=True)
    main_place = jnp.sum(main_hot * ranks[:8], axis=0, keepdims=True).astype(i32)
    extra_place = jnp.sum(extra_hot * (ranks[8:] + main_count), axis=0, keepdims=True).astype(i32)
    main_target = jnp.where((main > 0) & (main_place < FIX), (main - 1) * FIX + main_place, -1)
    extra_target = jnp.where((extra > 0) & (extra_place < FIX), (extra - 1) * FIX + extra_place, -1)
    slot = iota((3 * FIX, SLOTS), 0)
    pick = hot(slot == main_target)
    pick_first = hot(slot == extra_target)
    later = hot(iota((SLOTS, SLOTS), 1) == iota((SLOTS, SLOTS), 0) + 4)
    pick_second = mm(pick_first, later).astype(bf16)
    whole = in_ref[:, :, :FEAT].reshape(SLOTS, FEAT)
    halves = in_ref[:, :, FEAT : FEAT + half].reshape(SLOTS, half)
    taken = mm(pick, whole)
    fix_ref[:, :half] = (taken[:, :half] + mm(pick_first, halves)).astype(bf16)
    fix_ref[:, half:FEAT] = (taken[:, half:] + mm(pick_second, halves)).astype(bf16)
    beside = mm(mm(pick, meta).astype(bf16), shifted(0)) + mm(mm(pick_first, meta).astype(bf16), shifted(FIELDS))
    fix_ref[:, FEAT:] = beside.astype(bf16)
    step_row = iota((8, 1), 0)
    too_many = jnp.max(jnp.where((step_row > 0) & (count > FIX), 1.0, 0.0), axis=0, keepdims=True)
    flag = jnp.maximum(flag_in_ref[0:1, 0:1], too_many)
    spot = (iota(flag_ref.shape, 0) == 0) & (iota(flag_ref.shape, 1) == FEAT + 10)
    flag_ref[...] = jnp.where(spot, flag, 0.0).astype(bf16)


def key_columns(meta):
    wide = meta.astype(f32)
    position = wide[:, 1:2] * 256.0 + wide[:, 2:3]
    position = jnp.where(wide[:, 6:7] > 0.5, position, 1e9)
    return wide[:, 0:1], position, wide[:, 3:4] + wide[:, 4:5] + wide[:, 5:6]


def query_rows(meta):
    turn = hot(iota((FIELDS, META), 0) == iota((FIELDS, META), 1))
    return mm_t(turn, meta)


def best_over_keys(keys, metas, queries, query_fields, blocks):
    query_cl = query_fields[0:1]
    query_ord = query_fields[1:2] * 256.0 + query_fields[2:3]
    query_inv = query_fields[3:4] + query_fields[4:5] + query_fields[5:6]
    best = jnp.full(query_cl.shape, LOW, f32)
    size = keys.shape[0] // blocks
    for k in range(blocks):
        at = slice(k * size, (k + 1) * size)
        cl, position, inv = key_columns(metas[at, :])
        scaled = mm_t(keys[at, :], queries) * inv
        live = (cl == query_cl) & (position < query_ord)
        best = jnp.maximum(best, jnp.max(jnp.where(live, scaled, LOW), axis=0, keepdims=True))
    return jnp.maximum(best * query_inv, -1.0)


def selections():
    source = iota((EXTRA, SLOTS), 1)
    wanted = iota((EXTRA, SLOTS), 0)
    at = (wanted >> 2) * 8 + (wanted & 3)
    return hot(source == at), hot(source == at + 4)


def spread_out(best, fields, metas):
    rows = best.shape[1]
    from_chip = jnp.where((iota((CHIPS, rows), 0).astype(f32) == fields[7:8]) & (fields[6:7] > 0.5), 1.0, 0.0)
    high, middle, low = pieces(best)
    left = jnp.concatenate(
        [from_chip, from_chip * high.astype(f32), from_chip * middle.astype(f32), from_chip * low.astype(f32)], axis=0
    ).astype(bf16)
    wide = metas.astype(f32)
    place = wide[:, 8:9] * 256.0 + wide[:, 9:10]
    right = hot(iota((rows, ROW_DEV), 1).astype(f32) == place)
    spread = mm(left, right)
    value = spread[CHIPS : 2 * CHIPS] + spread[2 * CHIPS : 3 * CHIPS] + spread[3 * CHIPS :]
    return jnp.where(spread[:CHIPS] > 0.5, value, -1.0)


def main_kernel(own_ref, other_ref, keys_ref, metas_ref, best_ref):
    half = FEAT // 2
    first, second = selections()
    for k, ref in enumerate((own_ref, other_ref)):
        at = slice(k * MAIN, k * MAIN + SLOTS)
        keys_ref[at, :] = ref[:, :, :FEAT].reshape(SLOTS, FEAT)
        meta = fields_of(ref)
        metas_ref[at, :] = meta
        at = slice(k * MAIN + SLOTS, (k + 1) * MAIN)
        halves = ref[:, :, FEAT : FEAT + half].reshape(SLOTS, half)
        keys_ref[at, :half] = mm(first, halves).astype(bf16)
        keys_ref[at, half:] = mm(second, halves).astype(bf16)
        metas_ref[at, :] = mm(mm(first, meta).astype(bf16), shifted(FIELDS)).astype(bf16)
    fields = query_rows(metas_ref[:MAIN, :])
    best = best_over_keys(keys_ref, metas_ref, keys_ref[:MAIN, :], fields, 4)
    best_ref[...] = jnp.broadcast_to(best, best_ref.shape)


def tail_kernel(keys_ref, metas_ref, best_ref, own_tail_ref, other_tail_ref, out_ref):
    metas = metas_ref[:MAIN, :]
    fields = query_rows(metas)
    best = best_ref[0:1, :]
    for tail in (own_tail_ref, other_tail_ref):
        best = jnp.maximum(best, best_over_keys(tail.at[:, :FEAT], tail.at[:, FEAT:], keys_ref[:MAIN, :], fields, 1))
    out = spread_out(best, fields, metas)
    metas = own_tail_ref[:, FEAT:]
    fields = query_rows(metas)
    queries = own_tail_ref[:, :FEAT]
    best = best_over_keys(keys_ref, metas_ref, queries, fields, 2)
    for tail in (own_tail_ref, other_tail_ref):
        best = jnp.maximum(best, best_over_keys(tail.at[:, :FEAT], tail.at[:, FEAT:], queries, fields, 1))
    out = jnp.maximum(out, spread_out(best, fields, metas))
    at = slice(3 * FIX, 3 * FIX + 1), slice(FEAT + 10, FEAT + 11)
    flag = jnp.maximum(own_tail_ref[at].astype(f32), other_tail_ref[at].astype(f32))
    out = jnp.where(flag > 0.5, BAD, out)
    for k in range(ROW_DEV // META):
        out_ref[:, k, :] = out[:, k * META : (k + 1) * META]


def busy_kernel(keys_ref, queries_ref, out_ref):
    fields = query_rows(queries_ref[:, FEAT:])
    best = best_over_keys(keys_ref.at[:, :FEAT], keys_ref.at[:, FEAT:], queries_ref[:, :FEAT], fields, 4)
    out_ref[...] = jnp.full(out_ref.shape, -1.0, f32)
    for k in range(8):
        at = 2 * (k & 3) + (k >> 2)
        out_ref[at : at + 1, :CAP] = best[:, k * CAP : (k + 1) * CAP]


def last_kernel(spread_ref, busy_ref, rank_ref, out_ref, flag_ref):
    best = jnp.max(spread_ref[...], axis=0)
    worst = jnp.max(jnp.max(best, axis=0, keepdims=True), axis=1, keepdims=True)
    flag_ref[0] = jnp.where(jnp.max(worst) > 2.0, 1, 0)
    owned = jnp.concatenate([best[k : k + 1] for k in range(ROW_DEV // META)], axis=1)
    busy = jnp.max(busy_ref[...], axis=0, keepdims=True)
    high, middle, low = pieces(busy)
    parts = jnp.concatenate([high.astype(f32), middle.astype(f32), low.astype(f32), jnp.zeros((5, META), f32)], axis=0)
    rank = rank_ref[...]
    pick = hot(iota((META, ROW_DEV), 0) == rank)
    taken = mm(parts.astype(bf16), pick)
    value = taken[0:1] + taken[1:2] + taken[2:3]
    out_ref[...] = jnp.where(rank >= 0, value, owned)


def call(kernel, shapes, args, specs, scratch=(), flops=0, bytes_accessed=0, vmem=28, outs=None):
    return pl.pallas_call(
        kernel,
        out_shape=shapes,
        in_specs=[pl.BlockSpec(memory_space=s) for s in specs],
        out_specs=outs or jax.tree.map(lambda _: pl.BlockSpec(memory_space=VMEM), shapes),
        scratch_shapes=scratch,
        compiler_params=pltpu.CompilerParams(vmem_limit_bytes=vmem * 1024 * 1024),
        cost_estimate=pl.CostEstimate(flops=flops, bytes_accessed=bytes_accessed, transcendentals=0),
    )(*args)


VMEM, SMEM = pltpu.VMEM, pltpu.SMEM


def fast(embeddings, clusters, order):
    shape = jax.ShapeDtypeStruct
    y = lax.axis_index("y")
    chip = (lax.axis_index("x") * 4 + lax.axis_index("z")) * 4 + y
    outbox, box, rank, flag = call(
        pack_kernel,
        (
            shape((CHIPS, 8, WIDE), bf16),
            shape((CAP, NARROW), bf16),
            shape((1, ROW_DEV), i32),
            shape((8, 128), f32),
        ),
        (chip[None].astype(i32), embeddings, clusters[None, :], order[None, :]),
        (SMEM, pl.ANY, pl.ANY, pl.ANY),
        scratch=(
            pltpu.VMEM((ROW_DEV, FEAT), bf16),
            pltpu.VMEM((1, ROW_DEV), i32),
            pltpu.VMEM((1, ROW_DEV), i32),
            pltpu.SemaphoreType.DMA((3,)),
        ),
        vmem=58,
        flops=2 * 700_000_000,
        bytes_accessed=3_000_000,
    )
    busy_keys = lax.all_gather(box, CLUSTER_AXES, axis=0, tiled=True)
    inbox = lax.all_to_all(outbox, CHIP_AXES, split_axis=0, concat_axis=0, tiled=True)
    swap = [(0, 1), (1, 0)]
    along = [box] + [lax.ppermute(box, "y", [(i, (i - d) % 4) for i in range(4)]) for d in (1, 2, 3)]
    inbox, *along = lax.optimization_barrier((inbox, *along))
    other = lax.ppermute(inbox, "core", swap)
    fix, flag_block = call(
        fix_kernel,
        (shape((3 * FIX, NARROW), bf16), shape((FLAG_ROWS, NARROW), bf16)),
        (y[None].astype(i32), flag, inbox),
        (SMEM, VMEM, VMEM),
        flops=2 * 100_000_000,
        bytes_accessed=2_000_000,
    )
    keys, metas, best = call(
        main_kernel,
        (shape((2 * MAIN, FEAT), bf16), shape((2 * MAIN, META), bf16), shape((8, MAIN), f32)),
        (inbox, other),
        (VMEM, VMEM),
        flops=2 * 1_400_000_000,
        bytes_accessed=7_000_000,
    )
    got = [
        lax.ppermute(fix[(d - 1) * FIX : d * FIX], "y", [(i, (i + d) % 4) for i in range(4)]) for d in (1, 2, 3)
    ]
    best, *got = lax.optimization_barrier((best, *got))
    tail = jnp.concatenate(got + [flag_block], axis=0)
    other_tail = lax.ppermute(tail, "core", swap)
    spread = call(
        tail_kernel,
        shape((CHIPS, ROW_DEV // META, META), f32),
        (keys, metas, best, tail, other_tail),
        (VMEM, VMEM, VMEM, VMEM, VMEM),
        flops=2 * 500_000_000,
        bytes_accessed=4_000_000,
    )
    spread, *along = lax.optimization_barrier((spread, *along))
    same = jnp.concatenate(along, axis=0)
    busy_queries = jnp.concatenate([same, lax.ppermute(same, "core", swap)], axis=0)
    returned = lax.all_to_all(spread, CHIP_AXES, split_axis=0, concat_axis=0, tiled=True)
    partial = call(
        busy_kernel,
        shape((8, META), f32),
        (busy_keys, busy_queries),
        (VMEM, VMEM),
        flops=2 * 900_000_000,
        bytes_accessed=4_500_000,
    )
    parts = [partial[:2]]
    for d in (1, 2, 3):
        parts.append(lax.ppermute(partial[2 * d : 2 * d + 2], "y", [(i, (i + d) % 4) for i in range(4)]))
    to_other = jnp.concatenate([part[1:] for part in parts], axis=0)
    to_other, returned = lax.optimization_barrier((to_other, returned))
    busy = jnp.concatenate([part[:1] for part in parts] + [lax.ppermute(to_other, "core", swap)], axis=0)
    out, worst = call(
        last_kernel,
        (shape((1, ROW_DEV), f32), shape((1,), i32)),
        (returned, busy, rank),
        (VMEM, VMEM, VMEM),
        outs=(pl.BlockSpec(memory_space=VMEM), pl.BlockSpec(memory_space=SMEM)),
    )
    return out[0], worst[0] > 0


def inverse_norms(row_values):
    wide_rows = row_values.astype(f32)
    return lax.rsqrt(jnp.sum(wide_rows * wide_rows, axis=1) + 1e-06)


def general(embeddings, clusters, order):
    owners, helpers = 16, 8
    slot_count = ROW_DEV * 5 // (2 * owners * helpers)
    total_rows = owners * helpers * slot_count
    owner_of = clusters // CL_OWN
    one_hot = (owner_of[:, None] == jnp.arange(owners, dtype=i32)[None, :]).astype(i32)
    before = jnp.cumsum(one_hot, axis=0) - one_hot
    place_in = jnp.sum(before * one_hot, axis=1)
    target = (owner_of * helpers + place_in % helpers) * slot_count + place_in // helpers
    outbox = jnp.zeros((total_rows, FEAT), embeddings.dtype).at[target].set(embeddings)
    outbox_cl = jnp.full((total_rows,), -1, i32).at[target].set(clusters)
    outbox_ord = jnp.zeros((total_rows,), i32).at[target].set(order)

    def exchange(value):
        return lax.all_to_all(value, ALL_AXES, split_axis=0, concat_axis=0, tiled=True)

    def gather(value):
        return lax.all_gather(value, HELPER_AXES, axis=0, tiled=True)

    inbox, inbox_cl, inbox_ord = exchange(outbox), exchange(outbox_cl), exchange(outbox_ord)
    query_inv = inverse_norms(inbox)

    def advance(best, block):
        key_emb, key_cl, key_ord = block
        gram = lax.dot_general(inbox, key_emb, (((1,), (1,)), ((), ())), preferred_element_type=f32)
        cosine = gram * query_inv[:, None] * inverse_norms(key_emb)[None, :]
        live = (key_cl[None, :] == inbox_cl[:, None]) & (key_ord[None, :] < inbox_ord[:, None])
        return jnp.maximum(best, jnp.max(jnp.where(live, cosine, -1.0), axis=1)), None

    blocks = (
        gather(inbox).reshape(helpers, total_rows, FEAT),
        gather(inbox_cl).reshape(helpers, total_rows),
        gather(inbox_ord).reshape(helpers, total_rows),
    )
    best, _ = lax.scan(advance, jnp.full((total_rows,), -1.0, f32), blocks)
    return exchange(best)[target]


def local(embeddings, clusters, order):
    out, overflow = fast(embeddings, clusters, order)
    return lax.cond(overflow, lambda: general(embeddings, clusters, order), lambda: out)


def solution(mesh):
    grid = Mesh(mesh.devices.reshape(4, 4, 4, 2), ALL_AXES)
    placed = (P(ALL_AXES, None), P(ALL_AXES), P(ALL_AXES))
    return jax.shard_map(local, mesh=grid, in_specs=placed, out_specs=P(ALL_AXES), check_vma=False)
```

```python
import jax
import jax.numpy as jnp
from jax import lax
from jax.experimental import pallas as pl
from jax.experimental.pallas import tpu as pltpu
from jax.sharding import Mesh, PartitionSpec as P

CL_OWN = 32
ROW_DEV = 512
FEAT = 1024
OWNERS = 16
CAP = 80
CHIPS = 64
BINS = 4
PLACES = 11
FIX = 32
META = 128
WIDE = FEAT + FEAT // 2
NARROW = FEAT + META
SLOTS = CHIPS * 8
EXTRA = CHIPS * 4
FLAG_ROWS = 16
TAIL = 3 * FIX + FLAG_ROWS
MAIN = SLOTS + EXTRA
LOW = -1e30
BAD = 4.0
FIELDS = 16
FIELD_LANES = 16 * FIELDS
FIELD_ROW = 3

CHIP_AXES = ("x", "z", "y")
ALL_AXES = ("x", "z", "y", "core")
CLUSTER_AXES = ("x", "z")
HELPER_AXES = ("y", "core")

f32 = jnp.float32
bf16 = jnp.bfloat16
i32 = jnp.int32


def iota(shape, axis):
    return lax.broadcasted_iota(i32, shape, axis)


def hot(condition):
    return jnp.where(condition, 1.0, 0.0).astype(bf16)


def mm(a, b):
    return lax.dot_general(a, b, (((1,), (0,)), ((), ())), preferred_element_type=f32)


def mm_t(a, b):
    return lax.dot_general(a, b, (((1,), (1,)), ((), ())), preferred_element_type=f32)


def pieces(value):
    high = value.astype(bf16)
    rest = value - high.astype(f32)
    middle = rest.astype(bf16)
    low = (rest - middle.astype(f32)).astype(bf16)
    return high, middle, low


def bin_of(local_cluster):
    folded = local_cluster & 7
    return jnp.minimum(folded, 7 - folded)


def pack_kernel(chip_ref, emb_hbm, cl_hbm, ord_hbm, out_ref, box_ref, rank_ref, flag_ref, emb_ref, cl_ref, ord_ref, sems):
    pairs = ((cl_hbm, cl_ref), (ord_hbm, ord_ref), (emb_hbm, emb_ref))
    copies = [pltpu.make_async_copy(src, dst, sems.at[k]) for k, (src, dst) in enumerate(pairs)]
    for copy in copies:
        copy.start()
    copies[0].wait()
    copies[1].wait()
    cl = cl_ref[...]
    order = ord_ref[...]
    rows = emb_ref.shape[0]
    owner = cl >> 5
    local_cluster = cl & (CL_OWN - 1)
    bins = bin_of(local_cluster)
    earlier = hot(iota((rows, rows), 0) < iota((rows, rows), 1))
    is_owner = iota((OWNERS, rows), 0) == owner
    owner_hot = jnp.where(is_owner, 1.0, 0.0)
    owner_count = jnp.sum(owner_hot, axis=1, keepdims=True)
    full = jnp.where(owner_count == CAP, 1.0, 0.0)
    busy = jnp.sum(owner_hot * full, axis=0, keepdims=True) > 0.5
    is_group = iota((OWNERS * BINS, rows), 0) == owner * BINS + bins
    group_hot = jnp.where(is_group, 1.0, 0.0)
    group_count = jnp.sum(group_hot, axis=1, keepdims=True)
    ranks = mm(jnp.concatenate([group_hot, owner_hot], axis=0).astype(bf16), earlier)
    place = jnp.sum(group_hot * ranks[: OWNERS * BINS], axis=0, keepdims=True).astype(i32)
    owner_place = jnp.sum(owner_hot * ranks[OWNERS * BINS :], axis=0, keepdims=True).astype(i32)
    over = place >= PLACES
    over_ranks = mm((owner_hot * jnp.where(over, 1.0, 0.0)).astype(bf16), earlier)
    spill = jnp.sum(owner_hot * over_ranks, axis=0, keepdims=True).astype(i32)
    taken = jnp.minimum(group_count, float(PLACES))
    new_bin = bins
    new_place = place
    passed = jnp.zeros_like(place)
    for step in range(BINS):
        b = (chip_ref[0] + step) & 3
        here = iota((OWNERS * BINS, rows), 0) == owner * BINS + b
        used = jnp.sum(jnp.where(here, taken, 0.0), axis=0, keepdims=True).astype(i32)
        fits = over & (spill >= passed) & (spill < passed + (PLACES - used))
        new_bin = jnp.where(fits, b, new_bin)
        new_place = jnp.where(fits, used + spill - passed, new_place)
        passed = passed + (PLACES - used)
    base = (owner * BINS + new_bin) * 8
    main_target = jnp.where(busy | (new_place >= 8), -1, base + new_place)
    extra_target = jnp.where(busy | (new_place < 8), -8, base + new_place - 8)
    rank = jnp.where(busy, owner_place, -1)
    rank_ref[...] = rank
    most = jnp.max(jnp.where(full > 0.5, 0.0, owner_count), axis=0, keepdims=True)
    flag = (jnp.sum(full, axis=0, keepdims=True) != 1.0) | (most > BINS * PLACES)
    flag_ref[...] = jnp.broadcast_to(jnp.where(flag, 1.0, 0.0), flag_ref.shape)
    copies[2].wait()
    emb = emb_ref[...]
    wide = emb.astype(f32)
    square = wide * wide
    folded = square[:, :META]
    for k in range(1, FEAT // META):
        folded = folded + square[:, k * META : (k + 1) * META]
    ones = jnp.ones((8, META), bf16)
    total = sum(mm_t(ones, piece) for piece in pieces(folded))[0:1, :] + 1e-06
    inv = lax.rsqrt(total)
    inv = inv * (1.5 - 0.5 * total * inv * inv)
    high, middle, low = pieces(inv)
    at = iota((1, rows), 1)
    fields = [
        local_cluster.astype(f32),
        (order >> 8).astype(f32),
        (order & 255).astype(f32),
        high.astype(f32),
        middle.astype(f32),
        low.astype(f32),
        jnp.ones((1, rows), f32),
        jnp.full((1, rows), chip_ref[0], i32).astype(f32),
        (at >> 8).astype(f32),
        (at & 255).astype(f32),
    ]
    field_at = iota((META, rows), 0)
    meta = jnp.zeros((META, rows), f32)
    for k, value in enumerate(fields):
        meta = jnp.where(field_at == k, value, meta)
    sent = jnp.concatenate([meta[:FIELDS]] * (FIELD_LANES // FIELDS), axis=0)
    sent = jnp.where((iota((FIELD_LANES, rows), 0) >> 4) == new_place, sent, 0.0).astype(bf16)
    meta = meta.astype(bf16)
    pick = hot(iota((CAP, rows), 0) == rank)
    box_ref[:, :FEAT] = mm(pick, emb).astype(bf16)
    box_ref[:, FEAT:] = mm_t(pick, meta).astype(bf16)
    slot = iota((SLOTS, rows), 0)
    pick = hot(slot == main_target)
    pick_first = hot(slot == extra_target)
    pick_second = hot(slot - 4 == extra_target)
    half = FEAT // 2
    out_ref[:, :, :FEAT] = mm(pick, emb).astype(bf16).reshape(CHIPS, 8, FEAT)
    halves = mm(pick_first, emb[:, :half]) + mm(pick_second, emb[:, half:])
    to_chip = hot(iota((CHIPS, rows), 0) == jnp.where(busy, -1, owner * BINS + new_bin))
    beside = mm_t(to_chip, sent).astype(bf16)
    beside = mm(hot(iota((SLOTS, CHIPS), 0) == iota((SLOTS, CHIPS), 1) * 8 + FIELD_ROW), beside)
    halves = jnp.concatenate([halves[:, :FIELD_LANES] + beside, halves[:, FIELD_LANES:]], axis=1)
    out_ref[:, :, FEAT:] = halves.astype(bf16).reshape(CHIPS, 8, half)


def fields_of(ref):
    block = ref[:, :, FEAT : FEAT + FIELD_LANES].reshape(SLOTS, FIELD_LANES)
    block = mm(hot(iota((CHIPS, SLOTS), 1) == iota((CHIPS, SLOTS), 0) * 8 + FIELD_ROW), block).astype(bf16)
    spread = mm(hot(iota((SLOTS, CHIPS), 1) == iota((SLOTS, CHIPS), 0) >> 3), block)
    place, group = iota((SLOTS, FIELD_LANES), 0) & 7, iota((SLOTS, FIELD_LANES), 1) >> 4
    kept = jnp.where((group & 7) == place, spread, 0.0).astype(bf16)
    source, lane = iota((FIELD_LANES, META), 0), iota((FIELD_LANES, META), 1)
    return mm(kept, hot((source & 15) + FIELDS * (source >> 7) == lane)).astype(bf16)


def shifted(step):
    lanes = iota((META, META), 1)
    return hot((iota((META, META), 0) == lanes + step) & (lanes < FIELDS))


def fix_kernel(y_ref, flag_in_ref, in_ref, fix_ref, flag_ref, meta_ref):
    half = FEAT // 2
    meta = fields_of(in_ref)
    meta_ref[...] = meta
    turn = hot(iota((2 * FIELDS, META), 0) == iota((2 * FIELDS, META), 1))
    rows = mm_t(turn, meta)
    earlier = hot(iota((SLOTS, SLOTS), 0) < iota((SLOTS, SLOTS), 1))
    y = y_ref[0]

    def away(first):
        steps = (bin_of(rows[first : first + 1].astype(i32)) - y) & 3
        return jnp.where(rows[first + 6 : first + 7] > 0.5, steps, 0)

    main = away(0)
    extra = away(FIELDS)
    step_at = iota((8, SLOTS), 0)
    main_hot = jnp.where(step_at == main, 1.0, 0.0)
    extra_hot = jnp.where(step_at == extra, 1.0, 0.0)
    ranks = mm(jnp.concatenate([main_hot, extra_hot], axis=0).astype(bf16), earlier)
    main_count = jnp.sum(main_hot, axis=1, keepdims=True)
    count = main_count + jnp.sum(extra_hot, axis=1, keepdims=True)
    main_place = jnp.sum(main_hot * ranks[:8], axis=0, keepdims=True).astype(i32)
    extra_place = jnp.sum(extra_hot * (ranks[8:] + main_count), axis=0, keepdims=True).astype(i32)
    main_target = jnp.where((main > 0) & (main_place < FIX), (main - 1) * FIX + main_place, -1)
    extra_target = jnp.where((extra > 0) & (extra_place < FIX), (extra - 1) * FIX + extra_place, -1)
    slot = iota((3 * FIX, SLOTS), 0)
    pick = hot(slot == main_target)
    pick_first = hot(slot == extra_target)
    later = hot(iota((SLOTS, SLOTS), 1) == iota((SLOTS, SLOTS), 0) + 4)
    pick_second = mm(pick_first, later).astype(bf16)
    whole = in_ref[:, :, :FEAT].reshape(SLOTS, FEAT)
    halves = in_ref[:, :, FEAT : FEAT + half].reshape(SLOTS, half)
    taken = mm(pick, whole)
    fix_ref[:, :half] = (taken[:, :half] + mm(pick_first, halves)).astype(bf16)
    fix_ref[:, half:FEAT] = (taken[:, half:] + mm(pick_second, halves)).astype(bf16)
    beside = mm(mm(pick, meta).astype(bf16), shifted(0)) + mm(mm(pick_first, meta).astype(bf16), shifted(FIELDS))
    fix_ref[:, FEAT:] = beside.astype(bf16)
    step_row = iota((8, 1), 0)
    too_many = jnp.max(jnp.where((step_row > 0) & (count > FIX), 1.0, 0.0), axis=0, keepdims=True)
    flag = jnp.maximum(flag_in_ref[0:1, 0:1], too_many)
    spot = (iota(flag_ref.shape, 0) == 0) & (iota(flag_ref.shape, 1) == FEAT + 10)
    flag_ref[...] = jnp.where(spot, flag, 0.0).astype(bf16)


def key_columns(meta):
    wide = meta.astype(f32)
    position = wide[:, 1:2] * 256.0 + wide[:, 2:3]
    position = jnp.where(wide[:, 6:7] > 0.5, position, 1e9)
    return wide[:, 0:1], position, wide[:, 3:4] + wide[:, 4:5] + wide[:, 5:6]


def query_rows(meta):
    turn = hot(iota((FIELDS, META), 0) == iota((FIELDS, META), 1))
    return mm_t(turn, meta)


def best_over_keys(keys, metas, queries, query_fields, blocks):
    query_cl = query_fields[0:1]
    query_ord = query_fields[1:2] * 256.0 + query_fields[2:3]
    query_inv = query_fields[3:4] + query_fields[4:5] + query_fields[5:6]
    best = jnp.full(query_cl.shape, LOW, f32)
    size = keys.shape[0] // blocks
    for k in range(blocks):
        at = slice(k * size, (k + 1) * size)
        cl, position, inv = key_columns(metas[at, :])
        scaled = mm_t(keys[at, :], queries) * inv
        live = (cl == query_cl) & (position < query_ord)
        best = jnp.maximum(best, jnp.max(jnp.where(live, scaled, LOW), axis=0, keepdims=True))
    return jnp.maximum(best * query_inv, -1.0)


def selections():
    source = iota((EXTRA, SLOTS), 1)
    wanted = iota((EXTRA, SLOTS), 0)
    at = (wanted >> 2) * 8 + (wanted & 3)
    return hot(source == at), hot(source == at + 4)


def spread_out(best, fields, metas):
    rows = best.shape[1]
    from_chip = jnp.where((iota((CHIPS, rows), 0).astype(f32) == fields[7:8]) & (fields[6:7] > 0.5), 1.0, 0.0)
    high, middle, low = pieces(best)
    left = jnp.concatenate(
        [from_chip, from_chip * high.astype(f32), from_chip * middle.astype(f32), from_chip * low.astype(f32)], axis=0
    ).astype(bf16)
    wide = metas.astype(f32)
    place = wide[:, 8:9] * 256.0 + wide[:, 9:10]
    right = hot(iota((rows, ROW_DEV), 1).astype(f32) == place)
    spread = mm(left, right)
    value = spread[CHIPS : 2 * CHIPS] + spread[2 * CHIPS : 3 * CHIPS] + spread[3 * CHIPS :]
    return jnp.where(spread[:CHIPS] > 0.5, value, -1.0)


def main_kernel(own_ref, own_meta_ref, other_ref, keys_ref, metas_ref, best_ref):
    half = FEAT // 2
    first, second = selections()
    for k, ref in enumerate((own_ref, other_ref)):
        at = slice(k * MAIN, k * MAIN + SLOTS)
        keys_ref[at, :] = ref[:, :, :FEAT].reshape(SLOTS, FEAT)
        meta = own_meta_ref[...] if k == 0 else fields_of(ref)
        metas_ref[at, :] = meta
        at = slice(k * MAIN + SLOTS, (k + 1) * MAIN)
        halves = ref[:, :, FEAT : FEAT + half].reshape(SLOTS, half)
        keys_ref[at, :half] = mm(first, halves).astype(bf16)
        keys_ref[at, half:] = mm(second, halves).astype(bf16)
        metas_ref[at, :] = mm(mm(first, meta).astype(bf16), shifted(FIELDS)).astype(bf16)
    fields = query_rows(metas_ref[:MAIN, :])
    best = best_over_keys(keys_ref, metas_ref, keys_ref[:MAIN, :], fields, 4)
    best_ref[...] = jnp.broadcast_to(best, best_ref.shape)


def tail_kernel(keys_ref, metas_ref, best_ref, own_tail_ref, other_tail_ref, out_ref):
    metas = metas_ref[:MAIN, :]
    fields = query_rows(metas)
    best = best_ref[0:1, :]
    for tail in (own_tail_ref, other_tail_ref):
        best = jnp.maximum(best, best_over_keys(tail.at[:, :FEAT], tail.at[:, FEAT:], keys_ref[:MAIN, :], fields, 1))
    out = spread_out(best, fields, metas)
    metas = own_tail_ref[:, FEAT:]
    fields = query_rows(metas)
    queries = own_tail_ref[:, :FEAT]
    best = best_over_keys(keys_ref, metas_ref, queries, fields, 2)
    for tail in (own_tail_ref, other_tail_ref):
        best = jnp.maximum(best, best_over_keys(tail.at[:, :FEAT], tail.at[:, FEAT:], queries, fields, 1))
    out = jnp.maximum(out, spread_out(best, fields, metas))
    at = slice(3 * FIX, 3 * FIX + 1), slice(FEAT + 10, FEAT + 11)
    flag = jnp.maximum(own_tail_ref[at].astype(f32), other_tail_ref[at].astype(f32))
    out = jnp.where(flag > 0.5, BAD, out)
    for k in range(ROW_DEV // META):
        out_ref[:, k, :] = out[:, k * META : (k + 1) * META]


def busy_kernel(keys_ref, queries_ref, out_ref):
    fields = query_rows(queries_ref[:, FEAT:])
    best = best_over_keys(keys_ref.at[:, :FEAT], keys_ref.at[:, FEAT:], queries_ref[:, :FEAT], fields, 4)
    out_ref[...] = jnp.full(out_ref.shape, -1.0, f32)
    for k in range(8):
        at = 2 * (k & 3) + (k >> 2)
        out_ref[at : at + 1, :CAP] = best[:, k * CAP : (k + 1) * CAP]


def last_kernel(spread_ref, busy_ref, rank_ref, out_ref, flag_ref):
    best = jnp.max(spread_ref[...], axis=0)
    worst = jnp.max(jnp.max(best, axis=0, keepdims=True), axis=1, keepdims=True)
    flag_ref[0] = jnp.where(jnp.max(worst) > 2.0, 1, 0)
    owned = jnp.concatenate([best[k : k + 1] for k in range(ROW_DEV // META)], axis=1)
    busy = jnp.max(busy_ref[...], axis=0, keepdims=True)
    high, middle, low = pieces(busy)
    parts = jnp.concatenate([high.astype(f32), middle.astype(f32), low.astype(f32), jnp.zeros((5, META), f32)], axis=0)
    rank = rank_ref[...]
    pick = hot(iota((META, ROW_DEV), 0) == rank)
    taken = mm(parts.astype(bf16), pick)
    value = taken[0:1] + taken[1:2] + taken[2:3]
    out_ref[...] = jnp.where(rank >= 0, value, owned)


def call(kernel, shapes, args, specs, scratch=(), flops=0, bytes_accessed=0, vmem=28, outs=None):
    return pl.pallas_call(
        kernel,
        out_shape=shapes,
        in_specs=[pl.BlockSpec(memory_space=s) for s in specs],
        out_specs=outs or jax.tree.map(lambda _: pl.BlockSpec(memory_space=VMEM), shapes),
        scratch_shapes=scratch,
        compiler_params=pltpu.CompilerParams(vmem_limit_bytes=vmem * 1024 * 1024),
        cost_estimate=pl.CostEstimate(flops=flops, bytes_accessed=bytes_accessed, transcendentals=0),
    )(*args)


VMEM, SMEM = pltpu.VMEM, pltpu.SMEM


def fast(embeddings, clusters, order):
    shape = jax.ShapeDtypeStruct
    y = lax.axis_index("y")
    chip = (lax.axis_index("x") * 4 + lax.axis_index("z")) * 4 + y
    outbox, box, rank, flag = call(
        pack_kernel,
        (
            shape((CHIPS, 8, WIDE), bf16),
            shape((CAP, NARROW), bf16),
            shape((1, ROW_DEV), i32),
            shape((8, 128), f32),
        ),
        (chip[None].astype(i32), embeddings, clusters[None, :], order[None, :]),
        (SMEM, pl.ANY, pl.ANY, pl.ANY),
        scratch=(
            pltpu.VMEM((ROW_DEV, FEAT), bf16),
            pltpu.VMEM((1, ROW_DEV), i32),
            pltpu.VMEM((1, ROW_DEV), i32),
            pltpu.SemaphoreType.DMA((3,)),
        ),
        vmem=58,
        flops=2 * 700_000_000,
        bytes_accessed=3_000_000,
    )
    busy_keys = lax.all_gather(box, CLUSTER_AXES, axis=0, tiled=True)
    inbox = lax.all_to_all(outbox, CHIP_AXES, split_axis=0, concat_axis=0, tiled=True)
    swap = [(0, 1), (1, 0)]
    along = [box] + [lax.ppermute(box, "y", [(i, (i - d) % 4) for i in range(4)]) for d in (1, 2, 3)]
    inbox, *along = lax.optimization_barrier((inbox, *along))
    other = lax.ppermute(inbox, "core", swap)
    fix, flag_block, own_meta = call(
        fix_kernel,
        (shape((3 * FIX, NARROW), bf16), shape((FLAG_ROWS, NARROW), bf16), shape((SLOTS, META), bf16)),
        (y[None].astype(i32), flag, inbox),
        (SMEM, VMEM, VMEM),
        flops=2 * 100_000_000,
        bytes_accessed=2_000_000,
    )
    keys, metas, best = call(
        main_kernel,
        (shape((2 * MAIN, FEAT), bf16), shape((2 * MAIN, META), bf16), shape((8, MAIN), f32)),
        (inbox, own_meta, other),
        (VMEM, VMEM, VMEM),
        flops=2 * 1_400_000_000,
        bytes_accessed=7_000_000,
    )
    got = [
        lax.ppermute(fix[(d - 1) * FIX : d * FIX], "y", [(i, (i + d) % 4) for i in range(4)]) for d in (1, 2, 3)
    ]
    best, *got = lax.optimization_barrier((best, *got))
    tail = jnp.concatenate(got + [flag_block], axis=0)
    other_tail = lax.ppermute(tail, "core", swap)
    spread = call(
        tail_kernel,
        shape((CHIPS, ROW_DEV // META, META), f32),
        (keys, metas, best, tail, other_tail),
        (VMEM, VMEM, VMEM, VMEM, VMEM),
        flops=2 * 500_000_000,
        bytes_accessed=4_000_000,
    )
    spread, *along = lax.optimization_barrier((spread, *along))
    same = jnp.concatenate(along, axis=0)
    busy_queries = jnp.concatenate([same, lax.ppermute(same, "core", swap)], axis=0)
    returned = lax.all_to_all(spread, CHIP_AXES, split_axis=0, concat_axis=0, tiled=True)
    partial = call(
        busy_kernel,
        shape((8, META), f32),
        (busy_keys, busy_queries),
        (VMEM, VMEM),
        flops=2 * 900_000_000,
        bytes_accessed=4_500_000,
    )
    parts = [partial[:2]]
    for d in (1, 2, 3):
        parts.append(lax.ppermute(partial[2 * d : 2 * d + 2], "y", [(i, (i + d) % 4) for i in range(4)]))
    to_other = jnp.concatenate([part[1:] for part in parts], axis=0)
    to_other, returned = lax.optimization_barrier((to_other, returned))
    busy = jnp.concatenate([part[:1] for part in parts] + [lax.ppermute(to_other, "core", swap)], axis=0)
    out, worst = call(
        last_kernel,
        (shape((1, ROW_DEV), f32), shape((1,), i32)),
        (returned, busy, rank),
        (VMEM, VMEM, VMEM),
        outs=(pl.BlockSpec(memory_space=VMEM), pl.BlockSpec(memory_space=SMEM)),
    )
    return out[0], worst[0]


def inverse_norms(row_values):
    wide_rows = row_values.astype(f32)
    return lax.rsqrt(jnp.sum(wide_rows * wide_rows, axis=1) + 1e-06)


def general(embeddings, clusters, order):
    owners, helpers = 16, 8
    slot_count = ROW_DEV * 5 // (2 * owners * helpers)
    total_rows = owners * helpers * slot_count
    owner_of = clusters // CL_OWN
    one_hot = (owner_of[:, None] == jnp.arange(owners, dtype=i32)[None, :]).astype(i32)
    before = jnp.cumsum(one_hot, axis=0) - one_hot
    place_in = jnp.sum(before * one_hot, axis=1)
    target = (owner_of * helpers + place_in % helpers) * slot_count + place_in // helpers
    outbox = jnp.zeros((total_rows, FEAT), embeddings.dtype).at[target].set(embeddings)
    outbox_cl = jnp.full((total_rows,), -1, i32).at[target].set(clusters)
    outbox_ord = jnp.zeros((total_rows,), i32).at[target].set(order)

    def exchange(value):
        return lax.all_to_all(value, ALL_AXES, split_axis=0, concat_axis=0, tiled=True)

    def gather(value):
        return lax.all_gather(value, HELPER_AXES, axis=0, tiled=True)

    inbox, inbox_cl, inbox_ord = exchange(outbox), exchange(outbox_cl), exchange(outbox_ord)
    query_inv = inverse_norms(inbox)

    def advance(best, block):
        key_emb, key_cl, key_ord = block
        gram = lax.dot_general(inbox, key_emb, (((1,), (1,)), ((), ())), preferred_element_type=f32)
        cosine = gram * query_inv[:, None] * inverse_norms(key_emb)[None, :]
        live = (key_cl[None, :] == inbox_cl[:, None]) & (key_ord[None, :] < inbox_ord[:, None])
        return jnp.maximum(best, jnp.max(jnp.where(live, cosine, -1.0), axis=1)), None

    blocks = (
        gather(inbox).reshape(helpers, total_rows, FEAT),
        gather(inbox_cl).reshape(helpers, total_rows),
        gather(inbox_ord).reshape(helpers, total_rows),
    )
    best, _ = lax.scan(advance, jnp.full((total_rows,), -1.0, f32), blocks)
    return exchange(best)[target]


def local(embeddings, clusters, order):
    out, overflow = fast(embeddings, clusters, order)
    return lax.switch(overflow, [lambda: out, lambda: general(embeddings, clusters, order)])


def solution(mesh):
    grid = Mesh(mesh.devices.reshape(4, 4, 4, 2), ALL_AXES)
    placed = (P(ALL_AXES, None), P(ALL_AXES), P(ALL_AXES))
    return jax.shard_map(local, mesh=grid, in_specs=placed, out_specs=P(ALL_AXES), check_vma=False)
```

```python
import jax
import jax.numpy as jnp
from jax import lax
from jax.experimental import pallas as pl
from jax.experimental.pallas import tpu as pltpu
from jax.sharding import Mesh, PartitionSpec as P

CL_OWN = 32
ROW_DEV = 512
FEAT = 1024
OWNERS = 16
CAP = 80
CHIPS = 64
BINS = 4
PLACES = 11
FIX = 32
META = 128
WIDE = FEAT + FEAT // 2
NARROW = FEAT + META
SLOTS = CHIPS * 8
EXTRA = CHIPS * 4
FLAG_ROWS = 16
TAIL = 3 * FIX + FLAG_ROWS
MAIN = SLOTS + EXTRA
LOW = -1e30
BAD = 4.0
FIELDS = 16
FIELD_LANES = 16 * FIELDS
FIELD_ROW = 3

CHIP_AXES = ("x", "z", "y")
ALL_AXES = ("x", "z", "y", "core")
CLUSTER_AXES = ("x", "z")
HELPER_AXES = ("y", "core")

f32 = jnp.float32
bf16 = jnp.bfloat16
i32 = jnp.int32


def iota(shape, axis):
    return lax.broadcasted_iota(i32, shape, axis)


def hot(condition):
    return jnp.where(condition, 1.0, 0.0).astype(bf16)


def mm(a, b):
    return lax.dot_general(a, b, (((1,), (0,)), ((), ())), preferred_element_type=f32)


def mm_t(a, b):
    return lax.dot_general(a, b, (((1,), (1,)), ((), ())), preferred_element_type=f32)


def pieces(value):
    high = value.astype(bf16)
    rest = value - high.astype(f32)
    middle = rest.astype(bf16)
    low = (rest - middle.astype(f32)).astype(bf16)
    return high, middle, low


def bin_of(local_cluster):
    folded = local_cluster & 7
    return jnp.minimum(folded, 7 - folded)


def pack_kernel(chip_ref, emb_hbm, cl_hbm, ord_hbm, out_ref, box_ref, rank_ref, flag_ref, emb_ref, cl_ref, ord_ref, sems):
    pairs = ((cl_hbm, cl_ref), (ord_hbm, ord_ref), (emb_hbm, emb_ref))
    copies = [pltpu.make_async_copy(src, dst, sems.at[k]) for k, (src, dst) in enumerate(pairs)]
    for copy in copies:
        copy.start()
    copies[0].wait()
    copies[1].wait()
    cl = cl_ref[...]
    order = ord_ref[...]
    rows = emb_ref.shape[0]
    owner = cl >> 5
    local_cluster = cl & (CL_OWN - 1)
    bins = bin_of(local_cluster)
    earlier = hot(iota((rows, rows), 0) < iota((rows, rows), 1))
    is_owner = iota((OWNERS, rows), 0) == owner
    owner_hot = jnp.where(is_owner, 1.0, 0.0)
    owner_count = jnp.sum(owner_hot, axis=1, keepdims=True)
    full = jnp.where(owner_count == CAP, 1.0, 0.0)
    busy = jnp.sum(owner_hot * full, axis=0, keepdims=True) > 0.5
    is_group = iota((OWNERS * BINS, rows), 0) == owner * BINS + bins
    group_hot = jnp.where(is_group, 1.0, 0.0)
    group_count = jnp.sum(group_hot, axis=1, keepdims=True)
    ranks = mm(jnp.concatenate([group_hot, owner_hot], axis=0).astype(bf16), earlier)
    place = jnp.sum(group_hot * ranks[: OWNERS * BINS], axis=0, keepdims=True).astype(i32)
    owner_place = jnp.sum(owner_hot * ranks[OWNERS * BINS :], axis=0, keepdims=True).astype(i32)
    over = place >= PLACES
    over_ranks = mm((owner_hot * jnp.where(over, 1.0, 0.0)).astype(bf16), earlier)
    spill = jnp.sum(owner_hot * over_ranks, axis=0, keepdims=True).astype(i32)
    taken = jnp.minimum(group_count, float(PLACES))
    new_bin = bins
    new_place = place
    passed = jnp.zeros_like(place)
    for step in range(BINS):
        b = (chip_ref[0] + step) & 3
        here = iota((OWNERS * BINS, rows), 0) == owner * BINS + b
        used = jnp.sum(jnp.where(here, taken, 0.0), axis=0, keepdims=True).astype(i32)
        fits = over & (spill >= passed) & (spill < passed + (PLACES - used))
        new_bin = jnp.where(fits, b, new_bin)
        new_place = jnp.where(fits, used + spill - passed, new_place)
        passed = passed + (PLACES - used)
    base = (owner * BINS + new_bin) * 8
    main_target = jnp.where(busy | (new_place >= 8), -1, base + new_place)
    extra_target = jnp.where(busy | (new_place < 8), -8, base + new_place - 8)
    rank = jnp.where(busy, owner_place, -1)
    rank_ref[...] = rank
    most = jnp.max(jnp.where(full > 0.5, 0.0, owner_count), axis=0, keepdims=True)
    flag = (jnp.sum(full, axis=0, keepdims=True) != 1.0) | (most > BINS * PLACES)
    flag_ref[...] = jnp.broadcast_to(jnp.where(flag, 1.0, 0.0), flag_ref.shape)
    copies[2].wait()
    emb = emb_ref[...]
    wide = emb.astype(f32)
    square = wide * wide
    folded = square[:, :META]
    for k in range(1, FEAT // META):
        folded = folded + square[:, k * META : (k + 1) * META]
    ones = jnp.ones((8, META), bf16)
    total = sum(mm_t(ones, piece) for piece in pieces(folded))[0:1, :] + 1e-06
    inv = lax.rsqrt(total)
    inv = inv * (1.5 - 0.5 * total * inv * inv)
    high, middle, low = pieces(inv)
    at = iota((1, rows), 1)
    fields = [
        local_cluster.astype(f32),
        (order >> 8).astype(f32),
        (order & 255).astype(f32),
        high.astype(f32),
        middle.astype(f32),
        low.astype(f32),
        jnp.ones((1, rows), f32),
        jnp.full((1, rows), chip_ref[0], i32).astype(f32),
        (at >> 8).astype(f32),
        (at & 255).astype(f32),
    ]
    field_at = iota((META, rows), 0)
    meta = jnp.zeros((META, rows), f32)
    for k, value in enumerate(fields):
        meta = jnp.where(field_at == k, value, meta)
    sent = jnp.concatenate([meta[:FIELDS]] * (FIELD_LANES // FIELDS), axis=0)
    sent = jnp.where((iota((FIELD_LANES, rows), 0) >> 4) == new_place, sent, 0.0).astype(bf16)
    meta = meta.astype(bf16)
    pick = hot(iota((CAP, rows), 0) == rank)
    box_ref[:, :FEAT] = mm(pick, emb).astype(bf16)
    box_ref[:, FEAT:] = mm_t(pick, meta).astype(bf16)
    slot = iota((SLOTS, rows), 0)
    pick = hot(slot == main_target)
    pick_first = hot(slot == extra_target)
    pick_second = hot(slot - 4 == extra_target)
    half = FEAT // 2
    out_ref[:, :, :FEAT] = mm(pick, emb).astype(bf16).reshape(CHIPS, 8, FEAT)
    halves = mm(pick_first, emb[:, :half]) + mm(pick_second, emb[:, half:])
    to_chip = hot(iota((CHIPS, rows), 0) == jnp.where(busy, -1, owner * BINS + new_bin))
    beside = mm_t(to_chip, sent).astype(bf16)
    beside = mm(hot(iota((SLOTS, CHIPS), 0) == iota((SLOTS, CHIPS), 1) * 8 + FIELD_ROW), beside)
    halves = jnp.concatenate([halves[:, :FIELD_LANES] + beside, halves[:, FIELD_LANES:]], axis=1)
    out_ref[:, :, FEAT:] = halves.astype(bf16).reshape(CHIPS, 8, half)


def fields_of(ref):
    block = ref[:, :, FEAT : FEAT + FIELD_LANES].reshape(SLOTS, FIELD_LANES)
    block = mm(hot(iota((CHIPS, SLOTS), 1) == iota((CHIPS, SLOTS), 0) * 8 + FIELD_ROW), block).astype(bf16)
    spread = mm(hot(iota((SLOTS, CHIPS), 1) == iota((SLOTS, CHIPS), 0) >> 3), block)
    place, group = iota((SLOTS, FIELD_LANES), 0) & 7, iota((SLOTS, FIELD_LANES), 1) >> 4
    kept = jnp.where((group & 7) == place, spread, 0.0).astype(bf16)
    source, lane = iota((FIELD_LANES, META), 0), iota((FIELD_LANES, META), 1)
    return mm(kept, hot((source & 15) + FIELDS * (source >> 7) == lane)).astype(bf16)


def shifted(step):
    lanes = iota((META, META), 1)
    return hot((iota((META, META), 0) == lanes + step) & (lanes < FIELDS))


def fix_kernel(y_ref, flag_in_ref, in_ref, fix_ref, flag_ref, meta_ref):
    half = FEAT // 2
    meta = fields_of(in_ref)
    meta_ref[...] = meta
    turn = hot(iota((2 * FIELDS, META), 0) == iota((2 * FIELDS, META), 1))
    rows = mm_t(turn, meta)
    earlier = hot(iota((SLOTS, SLOTS), 0) < iota((SLOTS, SLOTS), 1))
    y = y_ref[0]

    def away(first):
        steps = (bin_of(rows[first : first + 1].astype(i32)) - y) & 3
        return jnp.where(rows[first + 6 : first + 7] > 0.5, steps, 0)

    main = away(0)
    extra = away(FIELDS)
    step_at = iota((8, SLOTS), 0)
    main_hot = jnp.where(step_at == main, 1.0, 0.0)
    extra_hot = jnp.where(step_at == extra, 1.0, 0.0)
    ranks = mm(jnp.concatenate([main_hot, extra_hot], axis=0).astype(bf16), earlier)
    main_count = jnp.sum(main_hot, axis=1, keepdims=True)
    count = main_count + jnp.sum(extra_hot, axis=1, keepdims=True)
    main_place = jnp.sum(main_hot * ranks[:8], axis=0, keepdims=True).astype(i32)
    extra_place = jnp.sum(extra_hot * (ranks[8:] + main_count), axis=0, keepdims=True).astype(i32)
    main_target = jnp.where((main > 0) & (main_place < FIX), (main - 1) * FIX + main_place, -1)
    extra_target = jnp.where((extra > 0) & (extra_place < FIX), (extra - 1) * FIX + extra_place, -1)
    slot = iota((3 * FIX, SLOTS), 0)
    pick = hot(slot == main_target)
    pick_first = hot(slot == extra_target)
    later = hot(iota((SLOTS, SLOTS), 1) == iota((SLOTS, SLOTS), 0) + 4)
    pick_second = mm(pick_first, later).astype(bf16)
    whole = in_ref[:, :, :FEAT].reshape(SLOTS, FEAT)
    halves = in_ref[:, :, FEAT : FEAT + half].reshape(SLOTS, half)
    taken = mm(pick, whole)
    fix_ref[:, :half] = (taken[:, :half] + mm(pick_first, halves)).astype(bf16)
    fix_ref[:, half:FEAT] = (taken[:, half:] + mm(pick_second, halves)).astype(bf16)
    beside = mm(mm(pick, meta).astype(bf16), shifted(0)) + mm(mm(pick_first, meta).astype(bf16), shifted(FIELDS))
    fix_ref[:, FEAT:] = beside.astype(bf16)
    step_row = iota((8, 1), 0)
    too_many = jnp.max(jnp.where((step_row > 0) & (count > FIX), 1.0, 0.0), axis=0, keepdims=True)
    flag = jnp.maximum(flag_in_ref[0:1, 0:1], too_many)
    spot = (iota(flag_ref.shape, 0) == 0) & (iota(flag_ref.shape, 1) == FEAT + 10)
    flag_ref[...] = jnp.where(spot, flag, 0.0).astype(bf16)


def key_columns(meta):
    wide = meta.astype(f32)
    position = wide[:, 1:2] * 256.0 + wide[:, 2:3]
    position = jnp.where(wide[:, 6:7] > 0.5, position, 1e9)
    return wide[:, 0:1], position, wide[:, 3:4] + wide[:, 4:5] + wide[:, 5:6]


def query_rows(meta):
    turn = hot(iota((FIELDS, META), 0) == iota((FIELDS, META), 1))
    return mm_t(turn, meta)


def best_over_keys(keys, metas, queries, query_fields, blocks):
    query_cl = query_fields[0:1]
    query_ord = query_fields[1:2] * 256.0 + query_fields[2:3]
    query_inv = query_fields[3:4] + query_fields[4:5] + query_fields[5:6]
    best = jnp.full(query_cl.shape, LOW, f32)
    size = keys.shape[0] // blocks
    for k in range(blocks):
        at = slice(k * size, (k + 1) * size)
        cl, position, inv = key_columns(metas[at, :])
        scaled = mm_t(keys[at, :], queries) * inv
        live = (cl == query_cl) & (position < query_ord)
        best = jnp.maximum(best, jnp.max(jnp.where(live, scaled, LOW), axis=0, keepdims=True))
    return jnp.maximum(best * query_inv, -1.0)


def selections():
    source = iota((EXTRA, SLOTS), 1)
    wanted = iota((EXTRA, SLOTS), 0)
    at = (wanted >> 2) * 8 + (wanted & 3)
    return hot(source == at), hot(source == at + 4)


def spread_out(best, fields, metas):
    rows = best.shape[1]
    from_chip = jnp.where((iota((CHIPS, rows), 0).astype(f32) == fields[7:8]) & (fields[6:7] > 0.5), 1.0, 0.0)
    high, middle, low = pieces(best)
    left = jnp.concatenate(
        [from_chip, from_chip * high.astype(f32), from_chip * middle.astype(f32), from_chip * low.astype(f32)], axis=0
    ).astype(bf16)
    wide = metas.astype(f32)
    place = wide[:, 8:9] * 256.0 + wide[:, 9:10]
    right = hot(iota((rows, ROW_DEV), 1).astype(f32) == place)
    spread = mm(left, right)
    value = spread[CHIPS : 2 * CHIPS] + spread[2 * CHIPS : 3 * CHIPS] + spread[3 * CHIPS :]
    return jnp.where(spread[:CHIPS] > 0.5, value, -1.0)


def main_kernel(own_ref, own_meta_ref, other_ref, keys_ref, metas_ref, best_ref):
    half = FEAT // 2
    first, second = selections()
    for k, ref in enumerate((own_ref, other_ref)):
        at = slice(k * MAIN, k * MAIN + SLOTS)
        keys_ref[at, :] = ref[:, :, :FEAT].reshape(SLOTS, FEAT)
        meta = own_meta_ref[...] if k == 0 else fields_of(ref)
        metas_ref[at, :] = meta
        at = slice(k * MAIN + SLOTS, (k + 1) * MAIN)
        halves = ref[:, :, FEAT : FEAT + half].reshape(SLOTS, half)
        keys_ref[at, :half] = mm(first, halves).astype(bf16)
        keys_ref[at, half:] = mm(second, halves).astype(bf16)
        metas_ref[at, :] = mm(mm(first, meta).astype(bf16), shifted(FIELDS)).astype(bf16)
    fields = query_rows(metas_ref[:MAIN, :])
    best = best_over_keys(keys_ref, metas_ref, keys_ref[:MAIN, :], fields, 4)
    best_ref[...] = jnp.broadcast_to(best, best_ref.shape)


def tail_kernel(keys_ref, metas_ref, best_ref, own_tail_ref, other_tail_ref, out_ref):
    metas = metas_ref[:MAIN, :]
    fields = query_rows(metas)
    best = best_ref[0:1, :]
    for tail in (own_tail_ref, other_tail_ref):
        best = jnp.maximum(best, best_over_keys(tail.at[:, :FEAT], tail.at[:, FEAT:], keys_ref[:MAIN, :], fields, 1))
    out = spread_out(best, fields, metas)
    metas = own_tail_ref[:, FEAT:]
    fields = query_rows(metas)
    queries = own_tail_ref[:, :FEAT]
    best = best_over_keys(keys_ref, metas_ref, queries, fields, 2)
    for tail in (own_tail_ref, other_tail_ref):
        best = jnp.maximum(best, best_over_keys(tail.at[:, :FEAT], tail.at[:, FEAT:], queries, fields, 1))
    out = jnp.maximum(out, spread_out(best, fields, metas))
    at = slice(3 * FIX, 3 * FIX + 1), slice(FEAT + 10, FEAT + 11)
    flag = jnp.maximum(own_tail_ref[at].astype(f32), other_tail_ref[at].astype(f32))
    out = jnp.where(flag > 0.5, BAD, out)
    for k in range(ROW_DEV // META):
        out_ref[:, k, :] = out[:, k * META : (k + 1) * META]


def busy_kernel(keys_ref, queries_ref, out_ref):
    fields = query_rows(queries_ref[:, FEAT:])
    best = best_over_keys(keys_ref.at[:, :FEAT], keys_ref.at[:, FEAT:], queries_ref[:, :FEAT], fields, 4)
    out_ref[...] = jnp.full(out_ref.shape, -1.0, f32)
    for k in range(8):
        at = 2 * (k & 3) + (k >> 2)
        out_ref[at : at + 1, :CAP] = best[:, k * CAP : (k + 1) * CAP]


def owned_kernel(spread_ref, out_ref, flag_ref):
    best = jnp.max(spread_ref[...], axis=0)
    worst = jnp.max(jnp.max(best, axis=0, keepdims=True), axis=1, keepdims=True)
    flag_ref[0] = jnp.where(jnp.max(worst) > 2.0, 1, 0)
    out_ref[...] = jnp.concatenate([best[k : k + 1] for k in range(ROW_DEV // META)], axis=1)


def last_kernel(owned_ref, busy_ref, rank_ref, out_ref):
    busy = jnp.max(busy_ref[...], axis=0, keepdims=True)
    high, middle, low = pieces(busy)
    parts = jnp.concatenate([high.astype(f32), middle.astype(f32), low.astype(f32), jnp.zeros((5, META), f32)], axis=0)
    rank = rank_ref[...]
    pick = hot(iota((META, ROW_DEV), 0) == rank)
    taken = mm(parts.astype(bf16), pick)
    value = taken[0:1] + taken[1:2] + taken[2:3]
    out_ref[...] = jnp.where(rank >= 0, value, owned_ref[...])


def call(kernel, shapes, args, specs, scratch=(), flops=0, bytes_accessed=0, vmem=28, outs=None):
    return pl.pallas_call(
        kernel,
        out_shape=shapes,
        in_specs=[pl.BlockSpec(memory_space=s) for s in specs],
        out_specs=outs or jax.tree.map(lambda _: pl.BlockSpec(memory_space=VMEM), shapes),
        scratch_shapes=scratch,
        compiler_params=pltpu.CompilerParams(vmem_limit_bytes=vmem * 1024 * 1024),
        cost_estimate=pl.CostEstimate(flops=flops, bytes_accessed=bytes_accessed, transcendentals=0),
    )(*args)


VMEM, SMEM = pltpu.VMEM, pltpu.SMEM


def fast(embeddings, clusters, order):
    shape = jax.ShapeDtypeStruct
    y = lax.axis_index("y")
    chip = (lax.axis_index("x") * 4 + lax.axis_index("z")) * 4 + y
    outbox, box, rank, flag = call(
        pack_kernel,
        (
            shape((CHIPS, 8, WIDE), bf16),
            shape((CAP, NARROW), bf16),
            shape((1, ROW_DEV), i32),
            shape((8, 128), f32),
        ),
        (chip[None].astype(i32), embeddings, clusters[None, :], order[None, :]),
        (SMEM, pl.ANY, pl.ANY, pl.ANY),
        scratch=(
            pltpu.VMEM((ROW_DEV, FEAT), bf16),
            pltpu.VMEM((1, ROW_DEV), i32),
            pltpu.VMEM((1, ROW_DEV), i32),
            pltpu.SemaphoreType.DMA((3,)),
        ),
        vmem=58,
        flops=2 * 700_000_000,
        bytes_accessed=3_000_000,
    )
    busy_keys = lax.all_gather(box, CLUSTER_AXES, axis=0, tiled=True)
    inbox = lax.all_to_all(outbox, CHIP_AXES, split_axis=0, concat_axis=0, tiled=True)
    swap = [(0, 1), (1, 0)]
    along = [box] + [lax.ppermute(box, "y", [(i, (i - d) % 4) for i in range(4)]) for d in (1, 2, 3)]
    inbox, *along = lax.optimization_barrier((inbox, *along))
    other = lax.ppermute(inbox, "core", swap)
    fix, flag_block, own_meta = call(
        fix_kernel,
        (shape((3 * FIX, NARROW), bf16), shape((FLAG_ROWS, NARROW), bf16), shape((SLOTS, META), bf16)),
        (y[None].astype(i32), flag, inbox),
        (SMEM, VMEM, VMEM),
        flops=2 * 100_000_000,
        bytes_accessed=2_000_000,
    )
    keys, metas, best = call(
        main_kernel,
        (shape((2 * MAIN, FEAT), bf16), shape((2 * MAIN, META), bf16), shape((8, MAIN), f32)),
        (inbox, own_meta, other),
        (VMEM, VMEM, VMEM),
        flops=2 * 1_400_000_000,
        bytes_accessed=7_000_000,
    )
    got = [
        lax.ppermute(fix[(d - 1) * FIX : d * FIX], "y", [(i, (i + d) % 4) for i in range(4)]) for d in (1, 2, 3)
    ]
    best, *got = lax.optimization_barrier((best, *got))
    tail = jnp.concatenate(got + [flag_block], axis=0)
    other_tail = lax.ppermute(tail, "core", swap)
    spread = call(
        tail_kernel,
        shape((CHIPS, ROW_DEV // META, META), f32),
        (keys, metas, best, tail, other_tail),
        (VMEM, VMEM, VMEM, VMEM, VMEM),
        flops=2 * 500_000_000,
        bytes_accessed=4_000_000,
    )
    spread, *along = lax.optimization_barrier((spread, *along))
    same = jnp.concatenate(along, axis=0)
    busy_queries = jnp.concatenate([same, lax.ppermute(same, "core", swap)], axis=0)
    returned = lax.all_to_all(spread, CHIP_AXES, split_axis=0, concat_axis=0, tiled=True)
    partial = call(
        busy_kernel,
        shape((8, META), f32),
        (busy_keys, busy_queries),
        (VMEM, VMEM),
        flops=2 * 900_000_000,
        bytes_accessed=4_500_000,
    )
    parts = [partial[:2]]
    for d in (1, 2, 3):
        parts.append(lax.ppermute(partial[2 * d : 2 * d + 2], "y", [(i, (i + d) % 4) for i in range(4)]))
    to_other = jnp.concatenate([part[1:] for part in parts], axis=0)
    to_other, returned = lax.optimization_barrier((to_other, returned))
    busy = jnp.concatenate([part[:1] for part in parts] + [lax.ppermute(to_other, "core", swap)], axis=0)
    owned, worst = call(
        owned_kernel,
        (shape((1, ROW_DEV), f32), shape((1,), i32)),
        (returned,),
        (VMEM,),
        outs=(pl.BlockSpec(memory_space=VMEM), pl.BlockSpec(memory_space=SMEM)),
    )
    out = call(last_kernel, shape((1, ROW_DEV), f32), (owned, busy, rank), (VMEM, VMEM, VMEM))
    return out[0], worst[0]


def inverse_norms(row_values):
    wide_rows = row_values.astype(f32)
    return lax.rsqrt(jnp.sum(wide_rows * wide_rows, axis=1) + 1e-06)


def general(embeddings, clusters, order):
    owners, helpers = 16, 8
    slot_count = ROW_DEV * 5 // (2 * owners * helpers)
    total_rows = owners * helpers * slot_count
    owner_of = clusters // CL_OWN
    one_hot = (owner_of[:, None] == jnp.arange(owners, dtype=i32)[None, :]).astype(i32)
    before = jnp.cumsum(one_hot, axis=0) - one_hot
    place_in = jnp.sum(before * one_hot, axis=1)
    target = (owner_of * helpers + place_in % helpers) * slot_count + place_in // helpers
    outbox = jnp.zeros((total_rows, FEAT), embeddings.dtype).at[target].set(embeddings)
    outbox_cl = jnp.full((total_rows,), -1, i32).at[target].set(clusters)
    outbox_ord = jnp.zeros((total_rows,), i32).at[target].set(order)

    def exchange(value):
        return lax.all_to_all(value, ALL_AXES, split_axis=0, concat_axis=0, tiled=True)

    def gather(value):
        return lax.all_gather(value, HELPER_AXES, axis=0, tiled=True)

    inbox, inbox_cl, inbox_ord = exchange(outbox), exchange(outbox_cl), exchange(outbox_ord)
    query_inv = inverse_norms(inbox)

    def advance(best, block):
        key_emb, key_cl, key_ord = block
        gram = lax.dot_general(inbox, key_emb, (((1,), (1,)), ((), ())), preferred_element_type=f32)
        cosine = gram * query_inv[:, None] * inverse_norms(key_emb)[None, :]
        live = (key_cl[None, :] == inbox_cl[:, None]) & (key_ord[None, :] < inbox_ord[:, None])
        return jnp.maximum(best, jnp.max(jnp.where(live, cosine, -1.0), axis=1)), None

    blocks = (
        gather(inbox).reshape(helpers, total_rows, FEAT),
        gather(inbox_cl).reshape(helpers, total_rows),
        gather(inbox_ord).reshape(helpers, total_rows),
    )
    best, _ = lax.scan(advance, jnp.full((total_rows,), -1.0, f32), blocks)
    return exchange(best)[target]


def local(embeddings, clusters, order):
    out, overflow = fast(embeddings, clusters, order)
    return lax.switch(overflow, [lambda: out, lambda: general(embeddings, clusters, order)])


def solution(mesh):
    grid = Mesh(mesh.devices.reshape(4, 4, 4, 2), ALL_AXES)
    placed = (P(ALL_AXES, None), P(ALL_AXES), P(ALL_AXES))
    return jax.shard_map(local, mesh=grid, in_specs=placed, out_specs=P(ALL_AXES), check_vma=False)
```

```python
import jax
import jax.numpy as jnp
from jax import lax
from jax.experimental import pallas as pl
from jax.experimental.pallas import tpu as pltpu
from jax.sharding import Mesh, PartitionSpec as P

CL_OWN = 32
ROW_DEV = 512
FEAT = 1024
OWNERS = 16
CAP = 80
CHIPS = 64
BINS = 4
PLACES = 11
FIX = 32
META = 128
WIDE = FEAT + FEAT // 2
NARROW = FEAT + META
SLOTS = CHIPS * 8
EXTRA = CHIPS * 4
FLAG_ROWS = 16
TAIL = 3 * FIX + FLAG_ROWS
MAIN = SLOTS + EXTRA
LOW = -1e30
BAD = 4.0
FIELDS = 16
FIELD_LANES = 16 * FIELDS
FIELD_ROW = 3

CHIP_AXES = ("x", "z", "y")
ALL_AXES = ("x", "z", "y", "core")
CLUSTER_AXES = ("x", "z")
HELPER_AXES = ("y", "core")

f32 = jnp.float32
bf16 = jnp.bfloat16
i32 = jnp.int32


def iota(shape, axis):
    return lax.broadcasted_iota(i32, shape, axis)


def hot(condition):
    return jnp.where(condition, 1.0, 0.0).astype(bf16)


def mm(a, b):
    return lax.dot_general(a, b, (((1,), (0,)), ((), ())), preferred_element_type=f32)


def mm_t(a, b):
    return lax.dot_general(a, b, (((1,), (1,)), ((), ())), preferred_element_type=f32)


def pieces(value):
    high = value.astype(bf16)
    rest = value - high.astype(f32)
    middle = rest.astype(bf16)
    low = (rest - middle.astype(f32)).astype(bf16)
    return high, middle, low


def bin_of(local_cluster):
    folded = local_cluster & 7
    return jnp.minimum(folded, 7 - folded)


def pack_kernel(chip_ref, emb_hbm, cl_hbm, ord_hbm, out_ref, box_ref, rank_ref, flag_ref, emb_ref, cl_ref, ord_ref, sems):
    pairs = ((cl_hbm, cl_ref), (ord_hbm, ord_ref), (emb_hbm, emb_ref))
    copies = [pltpu.make_async_copy(src, dst, sems.at[k]) for k, (src, dst) in enumerate(pairs)]
    for copy in copies:
        copy.start()
    copies[0].wait()
    copies[1].wait()
    cl = cl_ref[...]
    order = ord_ref[...]
    rows = emb_ref.shape[0]
    owner = cl >> 5
    local_cluster = cl & (CL_OWN - 1)
    bins = bin_of(local_cluster)
    earlier = hot(iota((rows, rows), 0) < iota((rows, rows), 1))
    is_owner = iota((OWNERS, rows), 0) == owner
    owner_hot = jnp.where(is_owner, 1.0, 0.0)
    owner_count = jnp.sum(owner_hot, axis=1, keepdims=True)
    full = jnp.where(owner_count == CAP, 1.0, 0.0)
    busy = jnp.sum(owner_hot * full, axis=0, keepdims=True) > 0.5
    is_group = iota((OWNERS * BINS, rows), 0) == owner * BINS + bins
    group_hot = jnp.where(is_group, 1.0, 0.0)
    group_count = jnp.sum(group_hot, axis=1, keepdims=True)
    ranks = mm(jnp.concatenate([group_hot, owner_hot], axis=0).astype(bf16), earlier)
    place = jnp.sum(group_hot * ranks[: OWNERS * BINS], axis=0, keepdims=True).astype(i32)
    owner_place = jnp.sum(owner_hot * ranks[OWNERS * BINS :], axis=0, keepdims=True).astype(i32)
    over = place >= PLACES
    over_ranks = mm((owner_hot * jnp.where(over, 1.0, 0.0)).astype(bf16), earlier)
    spill = jnp.sum(owner_hot * over_ranks, axis=0, keepdims=True).astype(i32)
    taken = jnp.minimum(group_count, float(PLACES))
    new_bin = bins
    new_place = place
    passed = jnp.zeros_like(place)
    for step in range(BINS):
        b = (chip_ref[0] + step) & 3
        here = iota((OWNERS * BINS, rows), 0) == owner * BINS + b
        used = jnp.sum(jnp.where(here, taken, 0.0), axis=0, keepdims=True).astype(i32)
        fits = over & (spill >= passed) & (spill < passed + (PLACES - used))
        new_bin = jnp.where(fits, b, new_bin)
        new_place = jnp.where(fits, used + spill - passed, new_place)
        passed = passed + (PLACES - used)
    base = (owner * BINS + new_bin) * 8
    main_target = jnp.where(busy | (new_place >= 8), -1, base + new_place)
    extra_target = jnp.where(busy | (new_place < 8), -8, base + new_place - 8)
    rank = jnp.where(busy, owner_place, -1)
    rank_ref[...] = rank
    most = jnp.max(jnp.where(full > 0.5, 0.0, owner_count), axis=0, keepdims=True)
    flag = (jnp.sum(full, axis=0, keepdims=True) != 1.0) | (most > BINS * PLACES)
    flag_ref[...] = jnp.broadcast_to(jnp.where(flag, 1.0, 0.0), flag_ref.shape)
    copies[2].wait()
    emb = emb_ref[...]
    wide = emb.astype(f32)
    square = wide * wide
    folded = square[:, :META]
    for k in range(1, FEAT // META):
        folded = folded + square[:, k * META : (k + 1) * META]
    ones = jnp.ones((8, META), bf16)
    total = sum(mm_t(ones, piece) for piece in pieces(folded))[0:1, :] + 1e-06
    inv = lax.rsqrt(total)
    inv = inv * (1.5 - 0.5 * total * inv * inv)
    high, middle, low = pieces(inv)
    at = iota((1, rows), 1)
    fields = [
        local_cluster.astype(f32),
        (order >> 8).astype(f32),
        (order & 255).astype(f32),
        high.astype(f32),
        middle.astype(f32),
        low.astype(f32),
        jnp.ones((1, rows), f32),
        jnp.full((1, rows), chip_ref[0], i32).astype(f32),
        (at >> 8).astype(f32),
        (at & 255).astype(f32),
    ]
    field_at = iota((META, rows), 0)
    meta = jnp.zeros((META, rows), f32)
    for k, value in enumerate(fields):
        meta = jnp.where(field_at == k, value, meta)
    sent = jnp.concatenate([meta[:FIELDS]] * (FIELD_LANES // FIELDS), axis=0)
    sent = jnp.where((iota((FIELD_LANES, rows), 0) >> 4) == new_place, sent, 0.0).astype(bf16)
    meta = meta.astype(bf16)
    pick = hot(iota((CAP, rows), 0) == rank)
    box_ref[:, :FEAT] = mm(pick, emb).astype(bf16)
    box_ref[:, FEAT:] = mm_t(pick, meta).astype(bf16)
    slot = iota((SLOTS, rows), 0)
    pick = hot(slot == main_target)
    pick_first = hot(slot == extra_target)
    pick_second = hot(slot - 4 == extra_target)
    half = FEAT // 2
    out_ref[:, :, :FEAT] = mm(pick, emb).astype(bf16).reshape(CHIPS, 8, FEAT)
    halves = mm(pick_first, emb[:, :half]) + mm(pick_second, emb[:, half:])
    to_chip = hot(iota((CHIPS, rows), 0) == jnp.where(busy, -1, owner * BINS + new_bin))
    beside = mm_t(to_chip, sent).astype(bf16)
    beside = mm(hot(iota((SLOTS, CHIPS), 0) == iota((SLOTS, CHIPS), 1) * 8 + FIELD_ROW), beside)
    halves = jnp.concatenate([halves[:, :FIELD_LANES] + beside, halves[:, FIELD_LANES:]], axis=1)
    out_ref[:, :, FEAT:] = halves.astype(bf16).reshape(CHIPS, 8, half)


def fields_of(ref):
    block = ref[:, :, FEAT : FEAT + FIELD_LANES].reshape(SLOTS, FIELD_LANES)
    block = mm(hot(iota((CHIPS, SLOTS), 1) == iota((CHIPS, SLOTS), 0) * 8 + FIELD_ROW), block).astype(bf16)
    spread = mm(hot(iota((SLOTS, CHIPS), 1) == iota((SLOTS, CHIPS), 0) >> 3), block)
    place, group = iota((SLOTS, FIELD_LANES), 0) & 7, iota((SLOTS, FIELD_LANES), 1) >> 4
    kept = jnp.where((group & 7) == place, spread, 0.0).astype(bf16)
    source, lane = iota((FIELD_LANES, META), 0), iota((FIELD_LANES, META), 1)
    return mm(kept, hot((source & 15) + FIELDS * (source >> 7) == lane)).astype(bf16)


def shifted(step):
    lanes = iota((META, META), 1)
    return hot((iota((META, META), 0) == lanes + step) & (lanes < FIELDS))


def fix_kernel(y_ref, flag_in_ref, in_ref, fix_ref, flag_ref, meta_ref):
    half = FEAT // 2
    meta = fields_of(in_ref)
    meta_ref[...] = meta
    turn = hot(iota((2 * FIELDS, META), 0) == iota((2 * FIELDS, META), 1))
    rows = mm_t(turn, meta)
    earlier = hot(iota((SLOTS, SLOTS), 0) < iota((SLOTS, SLOTS), 1))
    y = y_ref[0]

    def away(first):
        steps = (bin_of(rows[first : first + 1].astype(i32)) - y) & 3
        return jnp.where(rows[first + 6 : first + 7] > 0.5, steps, 0)

    main = away(0)
    extra = away(FIELDS)
    step_at = iota((8, SLOTS), 0)
    main_hot = jnp.where(step_at == main, 1.0, 0.0)
    extra_hot = jnp.where(step_at == extra, 1.0, 0.0)
    ranks = mm(jnp.concatenate([main_hot, extra_hot], axis=0).astype(bf16), earlier)
    main_count = jnp.sum(main_hot, axis=1, keepdims=True)
    count = main_count + jnp.sum(extra_hot, axis=1, keepdims=True)
    main_place = jnp.sum(main_hot * ranks[:8], axis=0, keepdims=True).astype(i32)
    extra_place = jnp.sum(extra_hot * (ranks[8:] + main_count), axis=0, keepdims=True).astype(i32)
    main_target = jnp.where((main > 0) & (main_place < FIX), (main - 1) * FIX + main_place, -1)
    extra_target = jnp.where((extra > 0) & (extra_place < FIX), (extra - 1) * FIX + extra_place, -1)
    slot = iota((3 * FIX, SLOTS), 0)
    pick = hot(slot == main_target)
    pick_first = hot(slot == extra_target)
    later = hot(iota((SLOTS, SLOTS), 1) == iota((SLOTS, SLOTS), 0) + 4)
    pick_second = mm(pick_first, later).astype(bf16)
    whole = in_ref[:, :, :FEAT].reshape(SLOTS, FEAT)
    halves = in_ref[:, :, FEAT : FEAT + half].reshape(SLOTS, half)
    taken = mm(pick, whole)
    fix_ref[:, :half] = (taken[:, :half] + mm(pick_first, halves)).astype(bf16)
    fix_ref[:, half:FEAT] = (taken[:, half:] + mm(pick_second, halves)).astype(bf16)
    beside = mm(mm(pick, meta).astype(bf16), shifted(0)) + mm(mm(pick_first, meta).astype(bf16), shifted(FIELDS))
    fix_ref[:, FEAT:] = beside.astype(bf16)
    step_row = iota((8, 1), 0)
    too_many = jnp.max(jnp.where((step_row > 0) & (count > FIX), 1.0, 0.0), axis=0, keepdims=True)
    flag = jnp.maximum(flag_in_ref[0:1, 0:1], too_many)
    spot = (iota(flag_ref.shape, 0) == 0) & (iota(flag_ref.shape, 1) == FEAT + 10)
    flag_ref[...] = jnp.where(spot, flag, 0.0).astype(bf16)


def key_columns(meta):
    wide = meta.astype(f32)
    position = wide[:, 1:2] * 256.0 + wide[:, 2:3]
    position = jnp.where(wide[:, 6:7] > 0.5, position, 1e9)
    return wide[:, 0:1], position, wide[:, 3:4] + wide[:, 4:5] + wide[:, 5:6]


def query_rows(meta):
    turn = hot(iota((FIELDS, META), 0) == iota((FIELDS, META), 1))
    return mm_t(turn, meta)


def best_over_keys(keys, metas, queries, query_fields, blocks):
    query_cl = query_fields[0:1]
    query_ord = query_fields[1:2] * 256.0 + query_fields[2:3]
    query_inv = query_fields[3:4] + query_fields[4:5] + query_fields[5:6]
    best = jnp.full(query_cl.shape, LOW, f32)
    size = keys.shape[0] // blocks
    for k in range(blocks):
        at = slice(k * size, (k + 1) * size)
        cl, position, inv = key_columns(metas[at, :])
        scaled = mm_t(keys[at, :], queries) * inv
        live = (cl == query_cl) & (position < query_ord)
        best = jnp.maximum(best, jnp.max(jnp.where(live, scaled, LOW), axis=0, keepdims=True))
    return jnp.maximum(best * query_inv, -1.0)


def selections():
    source = iota((EXTRA, SLOTS), 1)
    wanted = iota((EXTRA, SLOTS), 0)
    at = (wanted >> 2) * 8 + (wanted & 3)
    return hot(source == at), hot(source == at + 4)


def spread_out(best, fields, metas):
    rows = best.shape[1]
    from_chip = jnp.where((iota((CHIPS, rows), 0).astype(f32) == fields[7:8]) & (fields[6:7] > 0.5), 1.0, 0.0)
    high, middle, low = pieces(best)
    left = jnp.concatenate(
        [from_chip, from_chip * high.astype(f32), from_chip * middle.astype(f32), from_chip * low.astype(f32)], axis=0
    ).astype(bf16)
    wide = metas.astype(f32)
    place = wide[:, 8:9] * 256.0 + wide[:, 9:10]
    right = hot(iota((rows, ROW_DEV), 1).astype(f32) == place)
    spread = mm(left, right)
    value = spread[CHIPS : 2 * CHIPS] + spread[2 * CHIPS : 3 * CHIPS] + spread[3 * CHIPS :]
    return jnp.where(spread[:CHIPS] > 0.5, value, -1.0)


def main_kernel(own_ref, own_meta_ref, other_ref, keys_ref, metas_ref, best_ref):
    half = FEAT // 2
    first, second = selections()
    for k, ref in enumerate((own_ref, other_ref)):
        at = slice(k * MAIN, k * MAIN + SLOTS)
        keys_ref[at, :] = ref[:, :, :FEAT].reshape(SLOTS, FEAT)
        meta = own_meta_ref[...] if k == 0 else fields_of(ref)
        metas_ref[at, :] = meta
        at = slice(k * MAIN + SLOTS, (k + 1) * MAIN)
        halves = ref[:, :, FEAT : FEAT + half].reshape(SLOTS, half)
        keys_ref[at, :half] = mm(first, halves).astype(bf16)
        keys_ref[at, half:] = mm(second, halves).astype(bf16)
        metas_ref[at, :] = mm(mm(first, meta).astype(bf16), shifted(FIELDS)).astype(bf16)
    fields = query_rows(metas_ref[:MAIN, :])
    best = best_over_keys(keys_ref, metas_ref, keys_ref[:MAIN, :], fields, 4)
    best_ref[...] = jnp.broadcast_to(best, best_ref.shape)


def tail_kernel(keys_ref, metas_ref, best_ref, own_tail_ref, other_tail_ref, out_ref):
    metas = metas_ref[:MAIN, :]
    fields = query_rows(metas)
    best = best_ref[0:1, :]
    for tail in (own_tail_ref, other_tail_ref):
        best = jnp.maximum(best, best_over_keys(tail.at[:, :FEAT], tail.at[:, FEAT:], keys_ref[:MAIN, :], fields, 1))
    out = spread_out(best, fields, metas)
    metas = own_tail_ref[:, FEAT:]
    fields = query_rows(metas)
    queries = own_tail_ref[:, :FEAT]
    best = best_over_keys(keys_ref, metas_ref, queries, fields, 2)
    for tail in (own_tail_ref, other_tail_ref):
        best = jnp.maximum(best, best_over_keys(tail.at[:, :FEAT], tail.at[:, FEAT:], queries, fields, 1))
    out = jnp.maximum(out, spread_out(best, fields, metas))
    at = slice(3 * FIX, 3 * FIX + 1), slice(FEAT + 10, FEAT + 11)
    flag = jnp.maximum(own_tail_ref[at].astype(f32), other_tail_ref[at].astype(f32))
    out = jnp.where(flag > 0.5, BAD, out)
    for k in range(ROW_DEV // META):
        out_ref[:, k, :] = out[:, k * META : (k + 1) * META]


def busy_kernel(keys_ref, queries_ref, out_ref):
    fields = query_rows(queries_ref[:, FEAT:])
    best = best_over_keys(keys_ref.at[:, :FEAT], keys_ref.at[:, FEAT:], queries_ref[:, :FEAT], fields, 4)
    out_ref[...] = jnp.full(out_ref.shape, -1.0, f32)
    for k in range(8):
        at = 2 * (k & 3) + (k >> 2)
        out_ref[at : at + 1, :CAP] = best[:, k * CAP : (k + 1) * CAP]


def owned_kernel(spread_ref, out_ref, flag_ref):
    best = jnp.max(spread_ref[...], axis=0)
    worst = jnp.max(jnp.max(best, axis=0, keepdims=True), axis=1, keepdims=True)
    flag_ref[0] = jnp.where(jnp.max(worst) > 2.0, 1, 0)
    out_ref[...] = jnp.concatenate([best[k : k + 1] for k in range(ROW_DEV // META)], axis=1)


def last_kernel(owned_ref, busy_ref, rank_ref, out_ref):
    busy = jnp.max(busy_ref[...], axis=0, keepdims=True)
    high, middle, low = pieces(busy)
    parts = jnp.concatenate([high.astype(f32), middle.astype(f32), low.astype(f32), jnp.zeros((5, META), f32)], axis=0)
    rank = rank_ref[...]
    pick = hot(iota((META, ROW_DEV), 0) == rank)
    taken = mm(parts.astype(bf16), pick)
    value = taken[0:1] + taken[1:2] + taken[2:3]
    out_ref[...] = jnp.where(rank >= 0, value, owned_ref[...])


def call(kernel, shapes, args, specs, scratch=(), flops=0, bytes_accessed=0, vmem=28, outs=None):
    return pl.pallas_call(
        kernel,
        out_shape=shapes,
        in_specs=[pl.BlockSpec(memory_space=s) for s in specs],
        out_specs=outs or jax.tree.map(lambda _: pl.BlockSpec(memory_space=VMEM), shapes),
        scratch_shapes=scratch,
        compiler_params=pltpu.CompilerParams(vmem_limit_bytes=vmem * 1024 * 1024),
        cost_estimate=pl.CostEstimate(flops=flops, bytes_accessed=bytes_accessed, transcendentals=0),
    )(*args)


VMEM, SMEM = pltpu.VMEM, pltpu.SMEM


def fast(embeddings, clusters, order):
    shape = jax.ShapeDtypeStruct
    y = lax.axis_index("y")
    chip = (lax.axis_index("x") * 4 + lax.axis_index("z")) * 4 + y
    outbox, box, rank, flag = call(
        pack_kernel,
        (
            shape((CHIPS, 8, WIDE), bf16),
            shape((CAP, NARROW), bf16),
            shape((1, ROW_DEV), i32),
            shape((8, 128), f32),
        ),
        (chip[None].astype(i32), embeddings, clusters[None, :], order[None, :]),
        (SMEM, pl.ANY, pl.ANY, pl.ANY),
        scratch=(
            pltpu.VMEM((ROW_DEV, FEAT), bf16),
            pltpu.VMEM((1, ROW_DEV), i32),
            pltpu.VMEM((1, ROW_DEV), i32),
            pltpu.SemaphoreType.DMA((3,)),
        ),
        vmem=58,
        flops=2 * 700_000_000,
        bytes_accessed=3_000_000,
    )
    busy_keys = lax.all_gather(box, CLUSTER_AXES, axis=0, tiled=True)
    inbox = lax.all_to_all(outbox, CHIP_AXES, split_axis=0, concat_axis=0, tiled=True)
    swap = [(0, 1), (1, 0)]
    along = [box] + [lax.ppermute(box, "y", [(i, (i - d) % 4) for i in range(4)]) for d in (1, 2, 3)]
    inbox, *along = lax.optimization_barrier((inbox, *along))
    other = lax.ppermute(inbox, "core", swap)
    fix, flag_block, own_meta = call(
        fix_kernel,
        (shape((3 * FIX, NARROW), bf16), shape((FLAG_ROWS, NARROW), bf16), shape((SLOTS, META), bf16)),
        (y[None].astype(i32), flag, inbox),
        (SMEM, VMEM, VMEM),
        flops=2 * 100_000_000,
        bytes_accessed=2_000_000,
    )
    keys, metas, best = call(
        main_kernel,
        (shape((2 * MAIN, FEAT), bf16), shape((2 * MAIN, META), bf16), shape((8, MAIN), f32)),
        (inbox, own_meta, other),
        (VMEM, VMEM, VMEM),
        flops=2 * 1_400_000_000,
        bytes_accessed=7_000_000,
    )
    got = [
        lax.ppermute(fix[(d - 1) * FIX : d * FIX], "y", [(i, (i + d) % 4) for i in range(4)]) for d in (1, 2, 3)
    ]
    best, *got = lax.optimization_barrier((best, *got))
    tail = jnp.concatenate(got + [flag_block], axis=0)
    other_tail = lax.ppermute(tail, "core", swap)
    spread = call(
        tail_kernel,
        shape((CHIPS, ROW_DEV // META, META), f32),
        (keys, metas, best, tail, other_tail),
        (VMEM, VMEM, VMEM, VMEM, VMEM),
        flops=2 * 500_000_000,
        bytes_accessed=4_000_000,
    )
    spread, *along = lax.optimization_barrier((spread, *along))
    same = jnp.concatenate(along, axis=0)
    busy_queries = jnp.concatenate([same, lax.ppermute(same, "core", swap)], axis=0)
    returned = lax.all_to_all(spread, CHIP_AXES, split_axis=0, concat_axis=0, tiled=True)
    partial = call(
        busy_kernel,
        shape((8, META), f32),
        (busy_keys, busy_queries),
        (VMEM, VMEM),
        flops=2 * 900_000_000,
        bytes_accessed=4_500_000,
    )
    parts = [partial[:2]]
    for d in (2, 1, 3):
        parts.append(lax.ppermute(partial[2 * d : 2 * d + 2], "y", [(i, (i + d) % 4) for i in range(4)]))
    to_other = jnp.concatenate([part[1:] for part in parts], axis=0)
    to_other, returned = lax.optimization_barrier((to_other, returned))
    busy = jnp.concatenate([part[:1] for part in parts] + [lax.ppermute(to_other, "core", swap)], axis=0)
    owned, worst = call(
        owned_kernel,
        (shape((1, ROW_DEV), f32), shape((1,), i32)),
        (returned,),
        (VMEM,),
        outs=(pl.BlockSpec(memory_space=VMEM), pl.BlockSpec(memory_space=SMEM)),
    )
    out = call(last_kernel, shape((1, ROW_DEV), f32), (owned, busy, rank), (VMEM, VMEM, VMEM))
    return out[0], worst[0]


def inverse_norms(row_values):
    wide_rows = row_values.astype(f32)
    return lax.rsqrt(jnp.sum(wide_rows * wide_rows, axis=1) + 1e-06)


def general(embeddings, clusters, order):
    owners, helpers = 16, 8
    slot_count = ROW_DEV * 5 // (2 * owners * helpers)
    total_rows = owners * helpers * slot_count
    owner_of = clusters // CL_OWN
    one_hot = (owner_of[:, None] == jnp.arange(owners, dtype=i32)[None, :]).astype(i32)
    before = jnp.cumsum(one_hot, axis=0) - one_hot
    place_in = jnp.sum(before * one_hot, axis=1)
    target = (owner_of * helpers + place_in % helpers) * slot_count + place_in // helpers
    outbox = jnp.zeros((total_rows, FEAT), embeddings.dtype).at[target].set(embeddings)
    outbox_cl = jnp.full((total_rows,), -1, i32).at[target].set(clusters)
    outbox_ord = jnp.zeros((total_rows,), i32).at[target].set(order)

    def exchange(value):
        return lax.all_to_all(value, ALL_AXES, split_axis=0, concat_axis=0, tiled=True)

    def gather(value):
        return lax.all_gather(value, HELPER_AXES, axis=0, tiled=True)

    inbox, inbox_cl, inbox_ord = exchange(outbox), exchange(outbox_cl), exchange(outbox_ord)
    query_inv = inverse_norms(inbox)

    def advance(best, block):
        key_emb, key_cl, key_ord = block
        gram = lax.dot_general(inbox, key_emb, (((1,), (1,)), ((), ())), preferred_element_type=f32)
        cosine = gram * query_inv[:, None] * inverse_norms(key_emb)[None, :]
        live = (key_cl[None, :] == inbox_cl[:, None]) & (key_ord[None, :] < inbox_ord[:, None])
        return jnp.maximum(best, jnp.max(jnp.where(live, cosine, -1.0), axis=1)), None

    blocks = (
        gather(inbox).reshape(helpers, total_rows, FEAT),
        gather(inbox_cl).reshape(helpers, total_rows),
        gather(inbox_ord).reshape(helpers, total_rows),
    )
    best, _ = lax.scan(advance, jnp.full((total_rows,), -1.0, f32), blocks)
    return exchange(best)[target]


def local(embeddings, clusters, order):
    out, overflow = fast(embeddings, clusters, order)
    return lax.switch(overflow, [lambda: out, lambda: general(embeddings, clusters, order)])


def solution(mesh):
    grid = Mesh(mesh.devices.reshape(4, 4, 4, 2), ALL_AXES)
    placed = (P(ALL_AXES, None), P(ALL_AXES), P(ALL_AXES))
    return jax.shard_map(local, mesh=grid, in_specs=placed, out_specs=P(ALL_AXES), check_vma=False)
```
